128 devices in a mesh: dev: 2 (over x_hi), row: 32 (over z, y, x_lo), col: 2 (over core).
Axes of the slice: x: 4 (x_hi: 2, x_lo: 2; x = x_hi * 2 + x_lo), y: 4, z: 4, core: 2. Of those that a mesh axis runs over, the one named last changes fastest.
Arguments:
- tokens: bfloat16 [4, 4096, 1600], P('dev', 'row', 'col'), may hold values from -6 to 6
- segments: int32 [4, 4096], P('dev'), may hold values from 0 to 3, as said below
- first_gain: float32 [1600], P('col'), may hold values from 0.25 to 1.75
- first_bias: float32 [1600], P('col'), may hold values from -4 to 4
- attention_in: bfloat16 [1600, 3, 1600], P('row', None, 'col'), may hold values from -0.15625 to 0.15625
- attention_bias: float32 [2, 1600], P(None, 'col'), may hold values from -6 to 6
- attention_out: bfloat16 [1600, 1600], P('row', 'col'), may hold values from -2.5 to 2.5
- output_bias: float32 [1600], P('col'), may hold values from -4 to 4
- second_gain: float32 [1600], P('col'), may hold values from 0.25 to 1.75
- second_bias: float32 [1600], P('col'), may hold values from -4 to 4
- expand_weight: bfloat16 [1600, 6400], P('row', 'col'), may hold values from -0.15625 to 0.15625
- expand_bias: float32 [6400], P('col'), may hold values from -6 to 6
- contract_weight: bfloat16 [6400, 1600], P('row', 'col'), may hold values from -0.078125 to 0.078125
- contract_bias: float32 [1600], P('col'), may hold values from -4 to 4
- cotangent: bfloat16 [4, 4096, 1600], P('dev', 'row', 'col'), may hold values from -6 to 6
Outputs:
- result: bfloat16 [4, 4096, 1600], P('dev', 'row', 'col')
- gradient_tokens: bfloat16 [4, 4096, 1600], P('dev', 'row', 'col')
- gradient_first_gain: float32 [1600], P('col')
- gradient_first_bias: float32 [1600], P('col')
- gradient_attention_in: float32 [1600, 3, 1600], P('row', None, 'col')
- gradient_attention_bias: float32 [2, 1600], P(None, 'col')
- gradient_attention_out: float32 [1600, 1600], P('row', 'col')
- gradient_output_bias: float32 [1600], P('col')
- gradient_second_gain: float32 [1600], P('col')
- gradient_second_bias: float32 [1600], P('col')
- gradient_expand_weight: float32 [1600, 6400], P('row', 'col')
- gradient_expand_bias: float32 [6400], P('col')
- gradient_contract_weight: float32 [6400, 1600], P('row', 'col')
- gradient_contract_bias: float32 [1600], P('col')
The draws below stay inside these ranges and needn't reach their ends.
Inputs may be any that keep to these rules, and one draw needn't show every extreme that they name: `segments`: segment numbers of a sequence start at 0 and never fall along it; a change marks the start of a new document.
All inputs are finite; a program needn't handle non-finite values.
Results may differ from the reference program's by a relative error of at most 0.025.
Values may be sent and summed in bfloat16 or wider, within the bound.
A program may use at most 512 MiB of HBM per device.

```python
import jax
import jax.numpy as jnp
from jax import lax

D = 1600
HEADS = 25
HD = 64
FF = 6400
SEQS = 2
LEN = 4096
SEQ_ALL = 4


def draw_segments(key, part):
    key = jax.random.fold_in(key, 7)
    keys_list = jax.random.split(key, 5)
    groups = SEQ_ALL // SEQS
    chosen_index = jax.random.randint(keys_list[0], (groups,), 0, SEQS)
    chosen = jnp.arange(SEQ_ALL) % SEQS == jnp.repeat(chosen_index, SEQS)
    random_bounds = jax.random.randint(keys_list[1], (SEQ_ALL, 3), 1, LEN)
    opening = jax.random.randint(keys_list[2], (SEQ_ALL, 1), 1, LEN // 16)
    closing = jax.random.randint(keys_list[3], (SEQ_ALL, 1), LEN - LEN // 16, LEN - LEN // 32)
    trailing = jax.random.randint(keys_list[4], (SEQ_ALL, 1), LEN - LEN // 32, LEN)
    spanning = jnp.concatenate((opening, closing, trailing), axis=1)
    boundaries = jnp.where(chosen[:, None], spanning, random_bounds)
    positions = jnp.arange(LEN)
    above = positions[None, None, :] >= boundaries[:, :, None]
    return jnp.sum(above.astype(jnp.int32), axis=1).astype(jnp.int32)


def steps_of(key, extent, cuts, low, top_value):
    def one(dim, blocks):
        draws = jax.random.uniform(jax.random.fold_in(jax.random.fold_in(key, 6), dim), (blocks,), jnp.float32, low / len(cuts), top_value / len(cuts))
        return jnp.repeat(jnp.exp(draws), extent[dim] // blocks).reshape((-1,) + (1,) * (len(extent) - dim - 1))

    level = one(*cuts[0])
    for cut in cuts[1:]:
        level = level * one(*cut)
    return level


def normal_values(own_key, shape, deviation, limit, shards=(), held_as=jnp.bfloat16):
    loudness = steps_of(own_key, shape, shards, -0.22, 0.18) if shards else 1.0
    entries = jax.random.normal(own_key, shape, jnp.float32) * deviation * loudness
    return jnp.minimum(jnp.maximum(entries, -limit), limit).astype(held_as)


def setup_inputs(seed: int = 0) -> dict:
    streams_of = jax.random.split(jax.random.key(seed), 16)
    return {
        "tokens": normal_values(streams_of[0], (SEQ_ALL, LEN, D), 1.0, 6.0, ((0, 2), (1, 32), (2, 2))),
        "segments": draw_segments(jax.random.fold_in(streams_of[15], 71), 0),
        "first_gain": jnp.clip(1.0 + 0.15 * jax.random.normal(streams_of[2], (D,), jnp.float32), 0.25, 1.75),
        "first_bias": normal_values(streams_of[3], (D,), 0.3, 4.0, ((0, 2),), jnp.float32),
        "attention_in": normal_values(streams_of[4], (D, 3, D), D ** -0.5, 0.15625, ((0, 32), (2, 2))),
        "attention_bias": normal_values(streams_of[5], (2, D), 0.5, 6.0, ((1, 2),), jnp.float32),
        "attention_out": normal_values(streams_of[6], (D, D), (max(D // 256, 1)) ** -0.5, 2.5, ((0, 32), (1, 2))),
        "output_bias": normal_values(streams_of[7], (D,), 0.3, 4.0, ((0, 2),), jnp.float32),
        "second_gain": jnp.clip(1.0 + 0.15 * jax.random.normal(streams_of[8], (D,), jnp.float32), 0.25, 1.75),
        "second_bias": normal_values(streams_of[9], (D,), 0.3, 4.0, ((0, 2),), jnp.float32),
        "expand_weight": normal_values(streams_of[10], (D, FF), D ** -0.5, 0.15625, ((0, 32), (1, 2))),
        "expand_bias": normal_values(streams_of[11], (FF,), 0.5, 6.0, ((0, 2),), jnp.float32),
        "contract_weight": normal_values(streams_of[12], (FF, D), FF ** -0.5, 0.078125, ((0, 32), (1, 2))),
        "contract_bias": normal_values(streams_of[13], (D,), 0.3, 4.0, ((0, 2),), jnp.float32),
        "cotangent": normal_values(streams_of[14], (SEQ_ALL, LEN, D), 1.0, 6.0, ((0, 2), (1, 32), (2, 2))),
    }


@jax.custom_vjp
def low(v):
    return lax.optimization_barrier(v.astype(jnp.bfloat16)).astype(jnp.float32)

@jax.custom_vjp
def low_back(v):
    return v

def low_keep(v):
    return (low(v), None)

def low_pass(kept, grad):
    return (grad,)

def back_keep(v):
    return (v, None)

def back_low(kept, grad):
    return (low(grad),)
low.defvjp(low_keep, low_pass)
low_back.defvjp(back_keep, back_low)

def matmul(left, right):
    return jnp.dot(left, right, precision=lax.Precision.HIGHEST, preferred_element_type=jnp.float32)

def layer_norm(values, norm_gain, norm_bias):
    averages = lax.optimization_barrier(jnp.mean(values, axis=-1, keepdims=True))
    variance = lax.optimization_barrier(jnp.mean(values * values, axis=-1, keepdims=True)) - averages * averages
    return (values - averages) * lax.rsqrt(variance + 1e-05) * norm_gain + norm_bias

def attend(queries, keys_all, values_all, seg_ids):
    block_rows = min(512, LEN)
    score_scale = HD ** (-0.5)
    positions = jnp.arange(LEN)

    def one_block(block_index):
        first_row = (block_index * block_rows).astype(jnp.int32)
        query_block = lax.dynamic_slice_in_dim(queries, first_row, block_rows, 0)
        seg_query = lax.dynamic_slice_in_dim(seg_ids, first_row, block_rows, 0)
        query_pos = first_row + jnp.arange(block_rows)
        scores = jnp.einsum('qhd,khd->hqk', query_block, keys_all, precision=lax.Precision.HIGHEST) * score_scale
        scores = low_back(scores)
        allowed = (seg_query[:, None] == seg_ids[None, :]) & (positions[None, :] <= query_pos[:, None])
        scores = jnp.where(allowed[None], scores, -1e+30)
        log_total = jax.nn.logsumexp(scores, axis=-1, keepdims=True)
        probs_low = low(jnp.exp(scores - log_total))
        mixed = jnp.einsum('hqk,khd->qhd', probs_low, values_all, precision=lax.Precision.HIGHEST)
        return low(low_back(mixed))
    blocks = lax.map(jax.checkpoint(one_block), jnp.arange(LEN // block_rows).astype(jnp.int32))
    return blocks.reshape(LEN, D)

def sequence_forward(values, seg_ids, weights):
    first_gain, first_bias, attention_in, attention_bias, attention_out, output_bias, second_gain, second_bias, expand_weight, expand_bias, contract_weight, contract_bias = weights
    normed_one = low(layer_norm(values, first_gain, first_bias))
    projected = matmul(normed_one, attention_in.reshape(D, 3 * D)).reshape(LEN, 3, D)
    queries = low(low_back(projected[:, 0] + attention_bias[0]))
    keys_all = low(low_back(projected[:, 1]))
    values_all = low(low_back(projected[:, 2] + attention_bias[1]))
    attended = attend(queries.reshape(LEN, HEADS, HD), keys_all.reshape(LEN, HEADS, HD), values_all.reshape(LEN, HEADS, HD), seg_ids)
    middle = values + low_back(matmul(attended, attention_out) + output_bias)
    normed_two = low(layer_norm(middle, second_gain, second_bias))
    pre_gelu = low_back(matmul(normed_two, expand_weight) + expand_bias)
    gelu_out = low(jax.nn.gelu(pre_gelu, approximate=True))
    return middle + low_back(matmul(gelu_out, contract_weight) + contract_bias)

def reference(tokens, segments, first_gain, first_bias, attention_in, attention_bias, attention_out, output_bias, second_gain, second_bias, expand_weight, expand_bias, contract_weight, contract_bias, cotangent):
    float_tokens = tokens.astype(jnp.float32)
    weights = (first_gain, first_bias, attention_in.astype(jnp.float32), attention_bias, attention_out.astype(jnp.float32), output_bias, second_gain, second_bias, expand_weight.astype(jnp.float32), expand_bias, contract_weight.astype(jnp.float32), contract_bias)

    def forward(inputs, params):

        def one_sequence(item):
            return sequence_forward(item[0], item[1], params)
        return lax.map(jax.checkpoint(one_sequence), (inputs, segments))
    outputs, backward = jax.vjp(forward, float_tokens, weights)
    token_grad, param_grads = backward(cotangent.astype(jnp.float32))
    return (outputs.astype(jnp.bfloat16), token_grad.astype(jnp.bfloat16), param_grads[0], param_grads[1], param_grads[2], param_grads[3], param_grads[4], param_grads[5], param_grads[6], param_grads[7], param_grads[8], param_grads[9], param_grads[10], param_grads[11])
```

```python
import functools

import jax
import jax.numpy as jnp
from jax import lax
from jax.experimental import pallas as pl
from jax.experimental.pallas import tpu as pltpu
from jax.sharding import PartitionSpec as P

MESH = pl.DeviceIdType.MESH


def coords():
    d=lax.axis_index("dev"); r=lax.axis_index("row"); c=lax.axis_index("col")
    return r//8, (r//2)%4, d*2+r%2, c
def place(z,y,x,c):
    return (x//2, (z*4+y)*2+x%2, c)
SPLIT={"q":(4,4,6,5),"o":(2,1,2,2),"e":(7,4,7,7),"c":(1,2,2,2)}
ORD=("yzx","zyx","yxz","zxy")
def cuts(name,W):
    out=[];p=0
    for n in SPLIT[name]:
        out.append((p,min(p+n*128,W))); p+=n*128
    assert out[-1][1]==W,(name,out)
    return out
def gather_kernel(names,widths,*refs):
    n=len(names)
    src=refs[:n]; dst=refs[n:2*n]; ss,rs,ls=refs[2*n:]
    z,y,x,c=coords(); xl=x%2
    def peer(ax,k):
        zz,yy,xx=z,y,x
        if ax=="z": zz=(z+k)%4
        if ax=="y": yy=(y+k)%4
        if ax=="x": xx=(x+k)%4
        return place(zz,yy,xx,c)
    peers=[("z",1),("z",3),("z",2),("y",1),("y",3),("y",2),("x",1),("x",3)]
    bar=pltpu.get_barrier_semaphore()
    for ax,k in peers: pl.semaphore_signal(bar,inc=1,device_id=peer(ax,k),device_id_type=MESH)
    pl.semaphore_wait(bar,len(peers))
    cnt=[0]; allc=[]
    FULL=slice(None)
    LO=pl.ds(0,2); HI=pl.ds(2,2)
    def send(s,d,ax,k):
        i=cnt[0]; cnt[0]+=1
        cp=pltpu.make_async_remote_copy(src_ref=s,dst_ref=d,send_sem=ss.at[i],recv_sem=rs.at[i],device_id=peer(ax,k),device_id_type=MESH)
        cp.start(); allc.append(cp); return cp
    cut=[cuts(nm,w) for nm,w in zip(names,widths)]
    def at(t,p,zi,yi,xi):
        a,b=cut[t][p]
        return dst[t].at[zi,yi,xi,:,pl.ds(a,b-a)]
    def wait(l):
        for cp in l: cp.wait_recv()
    loc=[]
    st1=[[],[],[],[]]
    for t in range(n):
        cp=pltpu.make_async_copy(src[t],dst[t].at[z,y,xl],ls.at[t]); cp.start(); loc.append(cp)
    for t in range(n):
        for p in range(4):
            a,b=cut[t][p]
            for k in (1,3,2):
                st1[p].append(send(src[t].at[:,pl.ds(a,b-a)],at(t,p,z,y,xl),ORD[p][0],k))
    def both(p,f):
        return [cp for t in range(n) for cp in f(t,p)]
    def xsend(zi,yi):
        return lambda t,p:[send(at(t,p,*zi,xl),at(t,p,*zi,xl),"x",1),send(at(t,p,*yi,xl),at(t,p,*yi,xl),"x",3)]
    def ring_a(ax,zi,yi,xi):
        return lambda t,p:[send(at(t,p,zi,yi,xi),at(t,p,zi,yi,xi),ax,k) for k in (1,3)]
    def ring_b(ax,xi):
        def f(t,p):
            if ax=="z":
                u=at(t,p,(z+3)%4,LO,xi); v=at(t,p,(z+1)%4,HI,xi)
            else:
                u=at(t,p,LO,(y+3)%4,xi); v=at(t,p,HI,(y+1)%4,xi)
            return [send(u,u,ax,1),send(v,v,ax,3)]
        return f
    for cp in loc: cp.wait()
    wait(st1[0]); A2=both(0,ring_a("z",z,FULL,xl))
    wait(st1[1]); B2=both(1,ring_a("y",FULL,y,xl))
    wait(st1[2]); C2=both(2,xsend((z,LO),(z,HI)))
    wait(st1[3]); D2=both(3,xsend((LO,y),(HI,y)))
    wait(A2); A2=both(0,ring_b("z",xl))
    wait(B2); B2=both(1,ring_b("y",xl))
    wait(C2); C3=both(2,ring_a("z",z,FULL,FULL))
    wait(D2); D3=both(3,ring_a("y",FULL,y,FULL))
    wait(A2); A3=both(0,xsend((LO,FULL),(HI,FULL)))
    wait(B2); B3=both(1,xsend((LO,FULL),(HI,FULL)))
    wait(C3); C3=both(2,ring_b("z",FULL))
    wait(D3); D3=both(3,ring_b("y",FULL))
    wait(A3);wait(B3);wait(C3);wait(D3)
    for cp in allc: cp.wait_send()
def gather(names,arrs,cid=0):
    n=len(names)
    nd=36*n
    return pl.pallas_call(functools.partial(gather_kernel,names,[a.shape[1] for a in arrs]),
      out_shape=tuple(jax.ShapeDtypeStruct((4,4,2)+a.shape,a.dtype) for a in arrs),
      in_specs=[pl.BlockSpec(memory_space=pl.ANY)]*n,out_specs=tuple([pl.BlockSpec(memory_space=pl.ANY)]*n),
      scratch_shapes=[pltpu.SemaphoreType.DMA((nd,)),pltpu.SemaphoreType.DMA((nd,)),pltpu.SemaphoreType.DMA((n,))],
      compiler_params=pltpu.CompilerParams(collective_id=cid,has_side_effects=True))(*arrs)


RSPLIT={"q":(6,7,6),"o":(2,3,2),"e":(10,7,8),"c":(2,3,2)}
AX=("xzy","yzx","zyx")
def rcuts(name,W):
    out=[];p=0
    for n in RSPLIT[name]:
        out.append((p,min(p+n*128,W))); p+=n*128
    assert out[-1][1]==W,(name,out)
    return out
def rs_kernel(names,widths,hasvec,*refs):
    n=len(names)
    it=iter(refs)
    src=[next(it) for _ in range(n)]
    vec=next(it) if hasvec else None
    out=[next(it) for _ in range(n)]
    vout=next(it) if hasvec else None
    bufs=[[ [next(it) for _ in range(14)] for p in range(3)] for t in range(n)]
    vbuf=[next(it) for _ in range(3)] if hasvec else None
    ss,rs,ls=next(it),next(it),next(it)
    z,y,x,c=coords(); xl=x%2; xh=x//2
    me={"x":x,"y":y,"z":z}
    def peer(ax,k):
        zz,yy,xx=z,y,x
        if ax=="z": zz=(z+k)%4
        if ax=="y": yy=(y+k)%4
        if ax=="x": xx=(x+k)%4
        return place(zz,yy,xx,c)
    peers=[(a,k) for a in "xyz" for k in (1,2,3)]
    bar=pltpu.get_barrier_semaphore()
    for ax,k in peers: pl.semaphore_signal(bar,inc=1,device_id=peer(ax,k),device_id_type=MESH)
    cnt=[0]; lcnt=[0]; allc=[]
    def send(s,d,ax,k):
        i=cnt[0]; cnt[0]+=1
        cp=pltpu.make_async_remote_copy(src_ref=s,dst_ref=d,send_sem=ss.at[i],recv_sem=rs.at[i],device_id=peer(ax,k),device_id_type=MESH)
        cp.start(); allc.append(cp); return cp
    def load(s,d):
        i=lcnt[0]; lcnt[0]+=1
        cp=pltpu.make_async_copy(s,d,ls.at[i]); cp.start(); return cp
    cut=[rcuts(nm,w) for nm,w in zip(names,widths)]
    items=[(t,p) for t in range(n) for p in range(3)]
    def D(t,p,k):
        a,b=cut[t][p]
        if p==0:
            h=(b-a)//2
            return src[t].at[:,:,k%2,:,pl.ds(pl.multiple_of(a+(k//2)*h,128),h)]
        if p==1: return src[t].at[:,k,:,:,pl.ds(a,b-a)]
        return src[t].at[k,:,:,:,pl.ds(a,b-a)]
    def Dh(t,p,k,i):
        a,b=cut[t][p]; s=pl.ds(2*i,2)
        if p==0:
            h=(b-a)//2
            return src[t].at[s,:,k%2,:,pl.ds(pl.multiple_of(a+(k//2)*h,128),h)]
        if p==1: return src[t].at[s,k,:,:,pl.ds(a,b-a)]
        return src[t].at[k,s,:,:,pl.ds(a,b-a)]
    ld={}
    for t,p in items:
        own,bp,bm=bufs[t][p][:3]; k=me[AX[p][0]]
        ld[t,p]=[load(Dh(t,p,(k+1)%4,0),bp),load(Dh(t,p,(k+3)%4,1),bm),load(D(t,p,k),own)]
    pl.semaphore_wait(bar,len(peers))
    R={}
    def vsend(st):
        ax="xyz"[st]; b=vbuf[st]
        for k in (1,2,3): R["v",st,k]=send(b.at[me[ax]],b.at[me[ax]],ax,k)
    def vsum(st):
        for k in (1,2,3): R["v",st,k].wait_recv()
        b=vbuf[st]
        return (b[0]+b[1])+(b[2]+b[3])
    if hasvec:
        vbuf[0][pl.ds(x,1)]=vec[...][None]
        vsend(0)
    for t,p in items:
        own,bp,bm,rlp,rlm,rm,rp=bufs[t][p][:7]; ax=AX[p][0]; k=me[ax]
        R[t,p,"a"]=[send(Dh(t,p,(k+2)%4,0),rlp,ax,1),send(Dh(t,p,(k+2)%4,1),rlm,ax,3)]
    for t,p in items:
        own,bp,bm,rlp,rlm,rm,rp=bufs[t][p][:7]; ax=AX[p][0]; k=me[ax]
        R[t,p,"b"]=[send(Dh(t,p,(k+1)%4,1),rm.at[pl.ds(2,2)],ax,1),send(Dh(t,p,(k+3)%4,0),rp.at[pl.ds(0,2)],ax,3)]
    def addin(dst,other,idx):
        cntn,f,g=idx
        def body(i,_):
            dst[f(i)]=(dst[f(i)].astype(jnp.float32)+other[g(i)].astype(jnp.float32)).astype(jnp.bfloat16)
            return 0
        lax.fori_loop(0,cntn,body,0)
    for t,p in items:
        own,bp,bm,rlp,rlm,rm,rp=bufs[t][p][:7]; ax=AX[p][0]
        m=4 if p==0 else 2
        ix=(2*m,lambda i:(i//m,i%m),lambda i:(i//m,i%m))
        ld[t,p][0].wait(); R[t,p,"a"][0].wait_recv(); addin(bp,rlp,ix)
        R[t,p,"b"].append(send(bp,rm.at[pl.ds(0,2)],ax,1))
        ld[t,p][1].wait(); R[t,p,"a"][1].wait_recv(); addin(bm,rlm,ix)
        R[t,p,"b"].append(send(bm,rp.at[pl.ds(2,2)],ax,3))
    if hasvec:
        v=vsum(0); vbuf[1][pl.ds(y,1)]=v[None]; vsend(1)
    f32=lambda a:a.astype(jnp.float32)
    for t,p in items:
        own,bp,bm,rlp,rlm,rm,rp,rl2p,rl2m,rm2,rp2,out2,r3,_=bufs[t][p]
        m=4 if p==0 else 2; hm=m//2
        ld[t,p][2].wait()
        for cp in R[t,p,"b"]: cp.wait_recv()
        def body(i,_):
            j=(i//m,i%m)
            own[j]=(f32(own[j])+(f32(rm[j])+f32(rp[j]))).astype(jnp.bfloat16)
            return 0
        lax.fori_loop(0,4*m,body,0)
        ax=AX[p][1]; k=me[ax]
        L=pl.ds(0,hm); H=pl.ds(hm,hm)
        R[t,p,"c"]=[send(own.at[(k+2)%4,L],rl2p,ax,1),send(own.at[(k+2)%4,H],rl2m,ax,3)]
        R[t,p,"d"]=[send(own.at[(k+1)%4,H],rm2.at[H],ax,1),send(own.at[(k+3)%4,L],rp2.at[L],ax,3)]
    for t,p in items:
        own,bp,bm,rlp,rlm,rm,rp,rl2p,rl2m,rm2,rp2,out2,r3,_=bufs[t][p]
        m=4 if p==0 else 2; hm=m//2
        ax=AX[p][1]; k=me[ax]
        L=pl.ds(0,hm); H=pl.ds(hm,hm)
        R[t,p,"c"][0].wait_recv()
        addin(own,rl2p,(hm,lambda i:((k+1)%4,i),lambda i:i))
        R[t,p,"d"].append(send(own.at[(k+1)%4,L],rm2.at[L],ax,1))
        R[t,p,"c"][1].wait_recv()
        addin(own,rl2m,(hm,lambda i:((k+3)%4,hm+i),lambda i:i))
        R[t,p,"d"].append(send(own.at[(k+3)%4,H],rp2.at[H],ax,3))
    if hasvec:
        v=vsum(1); vbuf[2][pl.ds(z,1)]=v[None]; vsend(2)
    for t,p in items:
        own,bp,bm,rlp,rlm,rm,rp,rl2p,rl2m,rm2,rp2,out2,r3,_=bufs[t][p]
        m=4 if p==0 else 2
        k=me[AX[p][1]]
        for cp in R[t,p,"d"]: cp.wait_recv()
        def body(i,_):
            out2[i]=(f32(own[k,i])+(f32(rm2[i])+f32(rp2[i]))).astype(jnp.bfloat16)
            return 0
        lax.fori_loop(0,m,body,0)
        ax=AX[p][2]; k=me[ax]
        if p==0:
            R[t,p,"e"]=[send(out2.at[(k+j)%4],r3.at[j-1],ax,j) for j in (1,2,3)]
        else:
            R[t,p,"e"]=[send(out2.at[(k+j)%2],r3.at[j-1],ax,j) for j in (1,2,3)]
    for t,p in sorted(items,key=lambda q:q[1]):
        own,bp,bm,rlp,rlm,rm,rp,rl2p,rl2m,rm2,rp2,out2,r3,r4=bufs[t][p]
        a,b=cut[t][p]
        for cp in R[t,p,"e"]: cp.wait_recv()
        k=me[AX[p][2]] if p==0 else xl
        s=(f32(out2[k])+f32(r3[1]))+(f32(r3[0])+f32(r3[2]))
        if p==0:
            h=(b-a)//2
            s=s.astype(jnp.bfloat16)
            r4[xh]=s
            R[t,p,"f"]=[send(r4.at[xh],r4.at[xh],"x",2)]
        else:
            out[t][:,pl.ds(a,b-a)]=s
    for t in range(n):
        a,b=cut[t][0]; h=(b-a)//2; r4=bufs[t][0][13]
        R[t,0,"f"][0].wait_recv()
        for j in range(2): out[t][:,pl.ds(a+j*h,h)]=f32(r4[j])
    if hasvec: vout[...]=vsum(2)
    for cp in allc: cp.wait_send()
def reduce_scatter(names,parts,vec=None,cid=2):
    n=len(names); widths=[a.shape[4] for a in parts]; rows=[a.shape[3] for a in parts]
    scr=[]
    for nm,w,r in zip(names,widths,rows):
        for p,(a,b) in enumerate(rcuts(nm,w)):
            m=4 if p==0 else 2; v=(b-a)//2 if p==0 else b-a; hm=m//2
            B=lambda *s:pltpu.VMEM(s+(r,v),jnp.bfloat16)
            scr+=[B(4,m),B(2,m),B(2,m),B(2,m),B(2,m),B(4,m),B(4,m),B(hm),B(hm),B(m),B(m),B(m),B(3),B(2) if p==0 else pltpu.VMEM((8,128),jnp.bfloat16)]
    hv=vec is not None
    if hv: scr+=[pltpu.VMEM((4,)+vec.shape,jnp.float32)]*3
    nd=15*3*n+n+9
    scr+=[pltpu.SemaphoreType.DMA((nd,)),pltpu.SemaphoreType.DMA((nd,)),pltpu.SemaphoreType.DMA((9*n,))]
    A=pl.BlockSpec(memory_space=pl.ANY); V=pl.BlockSpec(memory_space=pltpu.VMEM)
    return pl.pallas_call(functools.partial(rs_kernel,names,widths,hv),
      out_shape=tuple(jax.ShapeDtypeStruct((r,w),jnp.float32) for r,w in zip(rows,widths))+((jax.ShapeDtypeStruct(vec.shape,jnp.float32),) if hv else ()),
      in_specs=[A]*n+[V]*hv,out_specs=tuple([V]*(n+hv)),scratch_shapes=scr,
      compiler_params=pltpu.CompilerParams(collective_id=cid,has_side_effects=True,vmem_limit_bytes=58<<20))(*parts,*([vec] if hv else []))


HD=64; LEN=4096; NEG=-1e30; ROWS=32
FQ,FK,BQ,BK=1024,1024,512,512
def dot(a,b): return lax.dot_general(a,b,(((1,),(0,)),((),())),preferred_element_type=jnp.float32)
def dot_nt(a,b): return lax.dot_general(a,b,(((1,),(1,)),((),())),preferred_element_type=jnp.float32)
def group_barrier(d,r,c):
    bar=pltpu.get_barrier_semaphore()
    def body(i,_):
        @pl.when(i!=r*2+c)
        def _():
            pl.semaphore_signal(bar,inc=1,device_id=(d,i//2,i%2),device_id_type=MESH)
        return 0
    lax.fori_loop(0,2*ROWS,body,0)
    pl.semaphore_wait(bar,2*ROWS-1)
def push(src,dst,send_sem,recv_sem,same,target):
    @pl.when(same)
    def _():
        pltpu.make_async_copy(src,dst,recv_sem).start()
    @pl.when(jnp.logical_not(same))
    def _():
        pltpu.make_async_remote_copy(src_ref=src,dst_ref=dst,send_sem=send_sem,recv_sem=recv_sem,device_id=target,device_id_type=MESH).start()
def pushed(src,dst,send_sem,recv_sem,same,target):
    @pl.when(jnp.logical_not(same))
    def _():
        pltpu.make_async_remote_copy(src_ref=src,dst_ref=dst,send_sem=send_sem,recv_sem=recv_sem,device_id=target,device_id_type=MESH).wait_send()
def arrived(ref,sem):
    pltpu.make_async_copy(ref,ref,sem).wait()
def attn_fwd_kernel(qkv_in,start,o_recv,qkv_out,oT,lse,qkv,knt,obf,s_in,s_out,r_in,r_out,l_sem):
    d=lax.axis_index("dev"); r=lax.axis_index("row"); c=lax.axis_index("col")
    group_barrier(d,r,c)
    lanes=pl.ds(pl.multiple_of(r*128,128),128)
    def full(fn):
        def body(i,_):
            fn(qkv_in.at[i%2,:,i//2+c],qkv.at[:,:,lanes],s_in.at[i],r_in,i==r,(d,i,c))
            return 0
        lax.fori_loop(0,24,body,0)
    def halves(fn):
        rows=pl.ds(pl.multiple_of(32*c,32),32)
        for s in range(2):
            fn(qkv_in.at[s,:,12*(1-c),rows],qkv.at[:,rows,lanes],s_in.at[24+s],r_in,(r==24+s)&(c==0),(d,24+s,0))
    full(push); halves(push)
    item=(r<24)|((c==0)&(r<26))
    head=r//2+13*c; seq=r%2
    def outs(qi,fn):
        def body(i,_):
            rr=qi*(FQ//128)+i//2; cc=i%2
            fn(obf.at[:,pl.ds(pl.multiple_of(rr*128,128),128)],o_recv.at[seq,head],s_out.at[rr*2+cc],r_out,(rr==r)&(cc==c),(d,rr,cc))
            return 0
        lax.fori_loop(0,FQ//64,body,0)
    @pl.when(item)
    def _():
        arrived(qkv,r_in)
        save=pltpu.make_async_copy(qkv,qkv_out,l_sem)
        save.start()
        for a in range(LEN//512):
            sl=pl.ds(a*512,512)
            knt[sl,:]=qkv[1,:,sl].T
        iota=lax.broadcasted_iota(jnp.int32,(FK,FQ),0)
        iotl=lax.broadcasted_iota(jnp.int32,(FK,FQ),1)
        def qloop(qi,_):
            qs=pl.ds(pl.multiple_of(qi*FQ,FQ),FQ)
            q=qkv[0,:,qs]*jnp.bfloat16(0.125)
            st=start[:,qs]
            def step(kj,carry,diag):
                m,l,acc=carry
                ks=pl.ds(pl.multiple_of(kj*FK,FK),FK)
                s=dot(knt[ks,:],q)
                ok=iota>=(st-kj*FK)
                if diag: ok=ok&(iota<=iotl)
                s=jnp.where(ok,s,NEG)
                mn=jnp.maximum(m,jnp.max(s,axis=0,keepdims=True))
                p=jnp.exp(s-mn)
                al=jnp.exp(m-mn)
                l=l*al+jnp.sum(p,axis=0,keepdims=True)
                acc=acc*al+dot(qkv[2,:,ks],p.astype(jnp.bfloat16))
                return mn,l,acc
            carry=(jnp.full((1,FQ),NEG,jnp.float32),jnp.zeros((1,FQ),jnp.float32),jnp.zeros((HD,FQ),jnp.float32))
            carry=lax.fori_loop(0,qi,lambda kj,cr:step(kj,cr,False),carry)
            m,l,acc=step(qi,carry,True)
            o=acc/l
            oT[:,qs]=o
            lse[:,qs]=m+jnp.log(l)
            obf[:,qs]=o.astype(jnp.bfloat16)
            outs(qi,push)
            return 0
        lax.fori_loop(0,LEN//FQ,qloop,0)
        save.wait()
        for qi in range(LEN//FQ): outs(qi,pushed)
    full(pushed); halves(pushed)
    arrived(o_recv,r_out)
def attn_bwd_kernel(do_in,qkv,oT,start,lse,d_recv,doT,knt,vnt,dqa,delta,dout,s_in,s_out,r_in,r_out):
    d=lax.axis_index("dev"); r=lax.axis_index("row"); c=lax.axis_index("col")
    group_barrier(d,r,c)
    lanes=pl.ds(pl.multiple_of(r*128,128),128)
    def full(fn):
        def body(i,_):
            fn(do_in.at[i%2,i//2+c],doT.at[:,lanes],s_in.at[i],r_in,i==r,(d,i,c))
            return 0
        lax.fori_loop(0,24,body,0)
    def halves(fn):
        rows=pl.ds(pl.multiple_of(32*c,32),32)
        for s in range(2):
            fn(do_in.at[s,12*(1-c),rows],doT.at[rows,lanes],s_in.at[24+s],r_in,(r==24+s)&(c==0),(d,24+s,0))
    full(push); halves(push)
    item=(r<24)|((c==0)&(r<26))
    def outs(fn):
        @pl.when(r<24)
        def _():
            def body(i,_):
                fn(dout.at[:,:,pl.ds(pl.multiple_of(i*128,128),128)],d_recv.at[:,(r%2)*13+r//2+c],s_out.at[i],r_out,i==r,(d,i,c))
                return 0
            lax.fori_loop(0,ROWS,body,0)
        @pl.when(r>=24)
        def _():
            def body(i,_):
                rr=i//2; cc=i%2
                rows=pl.ds(pl.multiple_of(32*cc,32),32)
                fn(dout.at[:,rows,pl.ds(pl.multiple_of(rr*128,128),128)],d_recv.at[:,(r%2)*13+12*(1-cc),rows],s_out.at[i],r_out,(rr==r)&(cc==c),(d,rr,cc))
                return 0
            lax.fori_loop(0,2*ROWS,body,0)
    @pl.when(item)
    def _():
        for a in range(LEN//512):
            sl=pl.ds(a*512,512)
            knt[sl,:]=qkv[1,:,sl].T
            vnt[sl,:]=qkv[2,:,sl].T
        dqa[...]=jnp.zeros_like(dqa)
        arrived(doT,r_in)
        for a in range(LEN//512):
            sl=pl.ds(a*512,512)
            delta[:,sl]=jnp.sum(oT[:,sl]*doT[:,sl].astype(jnp.float32),axis=0,keepdims=True)
        iota=lax.broadcasted_iota(jnp.int32,(BK,BQ),0)
        iotl=lax.broadcasted_iota(jnp.int32,(BK,BQ),1)
        def kloop(kj,_):
            ks=pl.ds(pl.multiple_of(kj*BK,BK),BK)
            kn=knt[ks,:]; vn=vnt[ks,:]; kT=qkv[1,:,ks]
            def step(qi,carry,diag):
                dk,dv=carry
                qs=pl.ds(pl.multiple_of(qi*BQ,BQ),BQ)
                q=qkv[0,:,qs]*jnp.bfloat16(0.125)
                do=doT[:,qs]
                s=dot(kn,q)
                ok=iota>=(start[:,qs]-kj*BK)
                if diag: ok=ok&(iota<=iotl)
                p=jnp.exp(jnp.where(ok,s,NEG)-lse[:,qs])
                dp=dot(vn,do)
                ds=(p*(dp-delta[:,qs])).astype(jnp.bfloat16)
                dv=dv+dot_nt(do,p.astype(jnp.bfloat16))
                dk=dk+dot_nt(q,ds)
                dqa[:,qs]+=dot(kT,ds)
                return dk,dv
            z=jnp.zeros((HD,BK),jnp.float32)
            carry=step(kj,(z,z),True)
            dk,dv=lax.fori_loop(kj+1,LEN//BQ,lambda qi,cr:step(qi,cr,False),carry)
            dout[1,:,ks]=dk.astype(jnp.bfloat16)
            dout[2,:,ks]=dv.astype(jnp.bfloat16)
            return 0
        lax.fori_loop(0,LEN//BK,kloop,0)
        for a in range(LEN//512):
            sl=pl.ds(a*512,512)
            dout[0,:,sl]=(dqa[:,sl]*0.125).astype(jnp.bfloat16)
        outs(push)
        outs(pushed)
    full(pushed); halves(pushed)
    arrived(d_recv.at[:,pl.ds(0,25)],r_out)
VM=pl.BlockSpec(memory_space=pltpu.VMEM); ANY=pl.BlockSpec(memory_space=pl.ANY)
bf=jnp.bfloat16
def attend(qkv,start,cid=1):
    S=jax.ShapeDtypeStruct
    return pl.pallas_call(attn_fwd_kernel,
      out_shape=(S((2,25,HD,128),bf),S((3,HD,LEN),bf),S((HD,LEN),jnp.float32),S((1,LEN),jnp.float32)),
      in_specs=[VM,VM],out_specs=(ANY,ANY,VM,VM),
      scratch_shapes=[pltpu.VMEM((3,HD,LEN),bf),pltpu.VMEM((LEN,HD),bf),pltpu.VMEM((HD,LEN),bf),
        pltpu.SemaphoreType.DMA((26,)),pltpu.SemaphoreType.DMA((64,)),pltpu.SemaphoreType.DMA,pltpu.SemaphoreType.DMA,pltpu.SemaphoreType.DMA],
      compiler_params=pltpu.CompilerParams(collective_id=cid,has_side_effects=True,vmem_limit_bytes=50<<20))(qkv,start)
def attend_back(do,qkv,oT,start,lse,cid=3):
    S=jax.ShapeDtypeStruct
    return pl.pallas_call(attn_bwd_kernel,
      out_shape=S((3,26,HD,128),bf),
      in_specs=[VM]*5,out_specs=ANY,
      scratch_shapes=[pltpu.VMEM((HD,LEN),bf),pltpu.VMEM((LEN,HD),bf),pltpu.VMEM((LEN,HD),bf),pltpu.VMEM((HD,LEN),jnp.float32),pltpu.VMEM((1,LEN),jnp.float32),pltpu.VMEM((3,HD,LEN),bf),
        pltpu.SemaphoreType.DMA((26,)),pltpu.SemaphoreType.DMA((64,)),pltpu.SemaphoreType.DMA,pltpu.SemaphoreType.DMA],
      compiler_params=pltpu.CompilerParams(collective_id=cid,has_side_effects=True,vmem_limit_bytes=50<<20))(do,qkv,oT,start,lse)


D = 1600
KP = 1792


def width_sums(first_sum, second_sum):
    return lax.psum((first_sum, second_sum), "col")


def full_rows(values):
    return lax.all_gather(values, "col", axis=1, tiled=True)


def norm_forward(values, norm_gain, norm_bias):
    totals = width_sums(jnp.sum(values, axis=1), jnp.sum(values * values, axis=1))
    averages = totals[0] / D
    reciprocal = lax.rsqrt(totals[1] / D - averages * averages + 1e-05)
    normed = (values - averages[:, None]) * reciprocal[:, None]
    return (normed, reciprocal, normed * norm_gain + norm_bias)


def norm_backward(incoming, normed, reciprocal, norm_gain):
    scaled = incoming * norm_gain
    totals = width_sums(jnp.sum(scaled, axis=1), jnp.sum(scaled * normed, axis=1))
    return reciprocal[:, None] * (
        scaled - totals[0][:, None] / D - normed * (totals[1][:, None] / D)
    )


def pad_rows(block):
    return jnp.pad(block, ((0, 6), (0, 0)))


def pad_features(values):
    n = values.shape[0]
    return jnp.pad(values.reshape(n, 32, 50), ((0, 0), (0, 0), (0, 6))).reshape(n, KP)


def feature_sums(values):
    n = values.shape[0]
    values = values.astype(jnp.bfloat16).reshape(n, 32, 56)[:, :, :50].reshape(n, D)
    return lax.psum_scatter(values, "col", scatter_dimension=1, tiled=True).astype(jnp.float32)


def matmul(left, right):
    return jnp.dot(left, right, preferred_element_type=jnp.float32)


def per_device(
    tokens,
    segments,
    first_gain,
    first_bias,
    attention_in,
    attention_bias,
    attention_out,
    output_bias,
    second_gain,
    second_bias,
    expand_weight,
    expand_bias,
    contract_weight,
    contract_bias,
    cotangent,
):
    seqs, block_len, width = tokens.shape
    row_total = seqs * block_len
    row = lax.axis_index("row")
    col = lax.axis_index("col")
    gathered = gather(
        "qoec",
        (
            pad_rows(attention_in.reshape(50, 3 * width)),
            pad_rows(attention_out),
            pad_rows(expand_weight),
            contract_weight,
        ),
        0,
    )
    weight_qkv = gathered[0].reshape(KP, 3 * width)
    weight_out = gathered[1].reshape(KP, width)
    weight_expand = gathered[2].reshape(KP, 4 * width)
    weight_contract = gathered[3].reshape(4 * D, width)

    own_seg = lax.dynamic_index_in_dim(segments, row % 2, 0, keepdims=True)
    positions = jnp.arange(LEN, dtype=jnp.int32)[None]
    before = jnp.concatenate((own_seg[:, :1], own_seg[:, :-1]), axis=1)
    start = lax.cummax(jnp.where(own_seg != before, positions, 0), axis=1)

    float_tokens = tokens.astype(jnp.float32).reshape(row_total, width)
    normed_one, recip_one, hidden_one = norm_forward(float_tokens, first_gain, first_bias)
    rows_one = pad_features(full_rows(hidden_one.astype(jnp.bfloat16)))
    bias_three = jnp.concatenate(
        (attention_bias[0], jnp.zeros_like(attention_bias[0]), attention_bias[1])
    )
    projected = jnp.einsum(
        "dm,snd->smn",
        weight_qkv,
        rows_one.reshape(seqs, block_len, KP),
        preferred_element_type=jnp.float32,
    )
    projected = (projected + bias_three[None, :, None]).astype(jnp.bfloat16)
    projected = projected.reshape(seqs, 3, width, block_len)

    def head_slots(values):
        lead = [(0, 0)] * (values.ndim - 2)
        slots = jnp.where(
            col == 0,
            jnp.pad(values, lead + [(0, 32), (0, 0)]),
            jnp.pad(values, lead + [(32, 0), (0, 0)]),
        )
        return slots.reshape(values.shape[:-2] + (13, HD, block_len))

    attended, qkv_item, out_item, log_totals = attend(head_slots(projected), start, 1)
    rows_attn = jnp.pad(
        attended.reshape(seqs, 32, 50, block_len), ((0, 0), (0, 0), (0, 6), (0, 0))
    ).reshape(seqs, KP, block_len)
    middle = float_tokens + (
        jnp.einsum(
            "sfn,fd->snd", rows_attn, weight_out, preferred_element_type=jnp.float32
        ).reshape(row_total, width)
        + output_bias
    )
    normed_two, recip_two, hidden_two = norm_forward(middle, second_gain, second_bias)
    rows_two = pad_features(full_rows(hidden_two.astype(jnp.bfloat16)))
    pre_gelu = matmul(rows_two, weight_expand) + expand_bias
    gelu_out = jax.nn.gelu(pre_gelu, approximate=True)
    rows_gelu = full_rows(gelu_out.astype(jnp.bfloat16))
    branch_out = matmul(rows_gelu, weight_contract) + contract_bias
    result = (middle + branch_out).astype(jnp.bfloat16).reshape(tokens.shape)

    grad_low = cotangent.reshape(row_total, width)
    grad_float = grad_low.astype(jnp.float32)
    part_contract = matmul(rows_gelu.T, grad_low).astype(jnp.bfloat16)
    grad_gelu = lax.psum_scatter(
        matmul(grad_low, weight_contract.T).astype(jnp.bfloat16),
        "col",
        scatter_dimension=1,
        tiled=True,
    ).astype(jnp.float32)
    gelu_back = jax.vjp(lambda inner: jax.nn.gelu(inner, approximate=True), pre_gelu)[1]
    grad_pre = gelu_back(grad_gelu)[0].astype(jnp.bfloat16)
    part_expand = matmul(rows_two.T, grad_pre).astype(jnp.bfloat16)
    sum_expand, sum_contract = reduce_scatter(
        "ec",
        (part_expand.reshape(4, 4, 2, 56, 4 * width), part_contract.reshape(4, 4, 2, 200, width)),
        None,
        2,
    )
    grad_two = feature_sums(matmul(grad_pre, weight_expand.T))
    grad_middle = grad_float + norm_backward(grad_two, normed_two, recip_two, second_gain)
    grad_attn = grad_middle.astype(jnp.bfloat16)
    part_out = jnp.einsum(
        "sfn,snd->fd",
        rows_attn,
        grad_attn.reshape(seqs, block_len, width),
        preferred_element_type=jnp.float32,
    ).astype(jnp.bfloat16)
    grad_mixed = jnp.einsum(
        "snd,fd->sfn",
        grad_attn.reshape(seqs, block_len, width),
        weight_out,
        preferred_element_type=jnp.float32,
    ).astype(jnp.bfloat16)
    grad_mixed = grad_mixed.reshape(seqs, 32, 56, block_len)[:, :, :50].reshape(seqs, D, block_len)
    grad_mixed = lax.psum_scatter(grad_mixed, "col", scatter_dimension=1, tiled=True)
    grad_slots = attend_back(head_slots(grad_mixed), qkv_item, out_item, start, log_totals, 3)
    grad_qkv = lax.dynamic_slice_in_dim(
        grad_slots.reshape(3, seqs, 13 * HD, block_len), 32 * col, width, 2
    )
    grad_rows = jnp.transpose(grad_qkv, (1, 0, 2, 3)).reshape(seqs, 3 * width, block_len)
    part_qkv = jnp.einsum(
        "snd,smn->dm",
        rows_one.reshape(seqs, block_len, KP),
        grad_rows,
        preferred_element_type=jnp.float32,
    ).astype(jnp.bfloat16)
    grad_one = feature_sums(
        jnp.einsum(
            "smn,dm->snd", grad_rows, weight_qkv, preferred_element_type=jnp.float32
        ).reshape(row_total, KP)
    )
    grad_input = grad_middle + norm_backward(grad_one, normed_one, recip_one, first_gain)
    gradient_tokens = grad_input.astype(jnp.bfloat16).reshape(tokens.shape)
    qkv_sums = jnp.sum(grad_qkv.astype(jnp.float32), axis=(1, 3))
    pieces = (
        jnp.sum(grad_one * normed_one, axis=0),
        jnp.sum(grad_one, axis=0),
        qkv_sums[0],
        qkv_sums[2],
        jnp.sum(grad_attn.astype(jnp.float32), axis=0),
        jnp.sum(grad_two * normed_two, axis=0),
        jnp.sum(grad_two, axis=0),
        jnp.sum(grad_pre.astype(jnp.float32), axis=0),
        jnp.sum(grad_float, axis=0),
    )
    vector = jnp.concatenate(pieces + (jnp.zeros((640,), jnp.float32),)).reshape(80, 128)
    sum_qkv, sum_out, vector = reduce_scatter(
        "qo",
        (part_qkv.reshape(4, 4, 2, 56, 3 * width), part_out.reshape(4, 4, 2, 56, width)),
        vector,
        4,
    )
    vector = vector.reshape(-1)
    sums = []
    at = 0
    for piece in pieces:
        sums.append(vector[at : at + piece.shape[0]])
        at += piece.shape[0]
    return (
        result,
        gradient_tokens,
        sums[0],
        sums[1],
        sum_qkv[:50].reshape(50, 3, width),
        jnp.stack((sums[2], sums[3])),
        sum_out[:50],
        sums[4],
        sums[5],
        sums[6],
        sum_expand[:50],
        sums[7],
        sum_contract,
        sums[8],
    )


def solution(mesh):
    return jax.shard_map(
        per_device,
        mesh=mesh,
        in_specs=(
            P("dev", "row", "col"),
            P("dev", None),
            P("col"),
            P("col"),
            P("row", None, "col"),
            P(None, "col"),
            P("row", "col"),
            P("col"),
            P("col"),
            P("col"),
            P("row", "col"),
            P("col"),
            P("row", "col"),
            P("col"),
            P("dev", "row", "col"),
        ),
        out_specs=(
            P("dev", "row", "col"),
            P("dev", "row", "col"),
            P("col"),
            P("col"),
            P("row", None, "col"),
            P(None, "col"),
            P("row", "col"),
            P("col"),
            P("col"),
            P("col"),
            P("row", "col"),
            P("col"),
            P("row", "col"),
            P("col"),
        ),
        check_vma=False,
    )
```

```python
import functools

import jax
import jax.numpy as jnp
from jax import lax
from jax.experimental import pallas as pl
from jax.experimental.pallas import tpu as pltpu
from jax.sharding import PartitionSpec as P

MESH = pl.DeviceIdType.MESH
D = 1600
KP = 1792


def coords():
    d=lax.axis_index("dev"); r=lax.axis_index("row"); c=lax.axis_index("col")
    return r//8, (r//2)%4, d*2+r%2, c
def place(z,y,x,c):
    return (x//2, (z*4+y)*2+x%2, c)
def peer_of(ax,k):
    z,y,x,c=coords()
    if ax=="z": z=(z+k)%4
    if ax=="y": y=(y+k)%4
    if ax=="x": x=(x+k)%4
    return place(z,y,x,c)
def greet(peers):
    bar=pltpu.get_barrier_semaphore()
    for ax,k in peers: pl.semaphore_signal(bar,inc=1,device_id=peer_of(ax,k),device_id_type=MESH)
    pl.semaphore_wait(bar,len(peers))
SPLIT={"q":(4,4,6,5),"o":(2,1,2,2),"e":(7,4,7,7),"c":(1,2,2,2)}
ORD=("yzx","zyx","yxz","zxy")
GPEERS=[("z",1),("z",3),("z",2),("y",1),("y",3),("y",2),("x",1),("x",3)]
def cuts(name,W):
    out=[];p=0
    for n in SPLIT[name]:
        out.append((p,min(p+n*128,W))); p+=n*128
    assert out[-1][1]==W,(name,out)
    return out
def gather_steps(names,widths,src,dst,ss,rs,ls):
    n=len(names)
    z,y,x,c=coords(); xl=x%2
    cnt=[0]; allc=[]
    FULL=slice(None)
    LO=pl.ds(0,2); HI=pl.ds(2,2)
    def mk(s,d,ax,k):
        i=cnt[0]; cnt[0]+=1
        cp=pltpu.make_async_remote_copy(src_ref=s,dst_ref=d,send_sem=ss.at[i],recv_sem=rs.at[i],device_id=peer_of(ax,k),device_id_type=MESH)
        allc.append(cp); return cp
    cut=[cuts(nm,w) for nm,w in zip(names,widths)]
    def at(t,p,zi,yi,xi):
        a,b=cut[t][p]
        return dst[t].at[zi,yi,xi,:,pl.ds(a,b-a)]
    def wait(l):
        for cp in l: cp.wait_recv()
    def go(l):
        for cp in l: cp.start()
    loc=[pltpu.make_async_copy(src[t],dst[t].at[z,y,xl],ls.at[t]) for t in range(n)]
    st1=[[],[],[],[]]
    for t in range(n):
        for p in range(4):
            a,b=cut[t][p]
            for k in (1,3,2):
                st1[p].append(mk(src[t].at[:,pl.ds(a,b-a)],at(t,p,z,y,xl),ORD[p][0],k))
    def both(p,f):
        return [cp for t in range(n) for cp in f(t,p)]
    def xsend(zi,yi):
        return lambda t,p:[mk(at(t,p,*zi,xl),at(t,p,*zi,xl),"x",1),mk(at(t,p,*yi,xl),at(t,p,*yi,xl),"x",3)]
    def ring_a(ax,zi,yi,xi):
        return lambda t,p:[mk(at(t,p,zi,yi,xi),at(t,p,zi,yi,xi),ax,k) for k in (1,3)]
    def ring_b(ax,xi):
        def f(t,p):
            if ax=="z":
                u=at(t,p,(z+3)%4,LO,xi); v=at(t,p,(z+1)%4,HI,xi)
            else:
                u=at(t,p,LO,(y+3)%4,xi); v=at(t,p,HI,(y+1)%4,xi)
            return [mk(u,u,ax,1),mk(v,v,ax,3)]
        return f
    A2=both(0,ring_a("z",z,FULL,xl)); B2=both(1,ring_a("y",FULL,y,xl))
    C2=both(2,xsend((z,LO),(z,HI))); D2=both(3,xsend((LO,y),(HI,y)))
    A2b=both(0,ring_b("z",xl)); B2b=both(1,ring_b("y",xl))
    C3=both(2,ring_a("z",z,FULL,FULL)); D3=both(3,ring_a("y",FULL,y,FULL))
    A3=both(0,xsend((LO,FULL),(HI,FULL))); B3=both(1,xsend((LO,FULL),(HI,FULL)))
    C3b=both(2,ring_b("z",FULL)); D3b=both(3,ring_b("y",FULL))
    def f0():
        go(loc)
        for p in range(4): go(st1[p])
    def f1():
        wait_loc=[cp.wait() for cp in loc]
        wait(st1[0]); go(A2)
        wait(st1[1]); go(B2)
        wait(st1[2]); go(C2)
        wait(st1[3]); go(D2)
    def f2():
        wait(A2); go(A2b); wait(B2); go(B2b)
        wait(C2); go(C3); wait(D2); go(D3)
    def f3():
        wait(A2b); go(A3); wait(B2b); go(B3)
    def f4():
        wait(C3); go(C3b); wait(D3); go(D3b)
    def f5():
        wait(A3);wait(B3);wait(C3b);wait(D3b)
        for cp in allc: cp.wait_send()
    return [f0,f1,f2,f3,f4,f5]
def gather_sems(n):
    return [pltpu.SemaphoreType.DMA((36,)),pltpu.SemaphoreType.DMA((36,)),pltpu.SemaphoreType.DMA((1,))]*n
def gather_chains(names,widths,src,dst,sems):
    chains=[gather_steps(names[t],[widths[t]],[src[t]],[dst[t]],*sems[3*t:3*t+3]) for t in range(len(names))]
    def both(k):
        def f():
            for ch in chains: ch[k]()
        return f
    return [both(k) for k in range(6)]
def gather_kernel(names,widths,*refs):
    n=len(names)
    steps=gather_chains(names,widths,refs[:n],refs[n:2*n],refs[2*n:])
    greet(GPEERS)
    for f in steps: f()
def gather_shapes(arrs):
    return tuple(jax.ShapeDtypeStruct((4,4,2)+a.shape,a.dtype) for a in arrs)
def gather(names,arrs,cid=0):
    n=len(names)
    return pl.pallas_call(functools.partial(gather_kernel,names,[a.shape[1] for a in arrs]),
      out_shape=gather_shapes(arrs),
      in_specs=[pl.BlockSpec(memory_space=pl.ANY)]*n,out_specs=tuple([pl.BlockSpec(memory_space=pl.ANY)]*n),
      scratch_shapes=gather_sems(n),
      compiler_params=pltpu.CompilerParams(collective_id=cid,has_side_effects=True))(*arrs)


RSPLIT={"q":(6,7,6),"o":(2,3,2),"e":(10,7,8),"c":(2,3,2)}
AX=("xzy","yzx","zyx")
RPEERS=[(a,k) for a in "xyz" for k in (1,2,3)]
def rcuts(name,W):
    out=[];p=0
    for n in RSPLIT[name]:
        out.append((p,min(p+n*128,W))); p+=n*128
    assert out[-1][1]==W,(name,out)
    return out
def scatter_steps(names,widths,src,vec,out,vout,scr):
    n=len(names); hasvec=vec is not None
    it=iter(scr)
    bufs=[[ [next(it) for _ in range(14)] for p in range(3)] for t in range(n)]
    vbuf=[next(it) for _ in range(3)] if hasvec else None
    ss,rs,ls=next(it),next(it),next(it)
    z,y,x,c=coords(); xl=x%2; xh=x//2
    me={"x":x,"y":y,"z":z}
    cnt=[0]; lcnt=[0]; allc=[]
    def mk(s,d,ax,k):
        i=cnt[0]; cnt[0]+=1
        cp=pltpu.make_async_remote_copy(src_ref=s,dst_ref=d,send_sem=ss.at[i],recv_sem=rs.at[i],device_id=peer_of(ax,k),device_id_type=MESH)
        allc.append(cp); return cp
    def mkload(s,d):
        i=lcnt[0]; lcnt[0]+=1
        return pltpu.make_async_copy(s,d,ls.at[i])
    cut=[rcuts(nm,w) for nm,w in zip(names,widths)]
    items=[(t,p) for t in range(n) for p in range(3)]
    f32=lambda a:a.astype(jnp.float32)
    def Dh(t,p,k,i=None):
        a,b=cut[t][p]; s=slice(None) if i is None else pl.ds(2*i,2)
        if p==0:
            h=(b-a)//2
            return src[t].at[s,:,k%2,:,pl.ds(pl.multiple_of(a+(k//2)*h,128),h)]
        if p==1: return src[t].at[s,k,:,:,pl.ds(a,b-a)]
        return src[t].at[k,s,:,:,pl.ds(a,b-a)]
    ld={}; R={}
    for t,p in items:
        own,bp,bm,rlp,rlm,rm,rp,rl2p,rl2m,rm2,rp2,out2,r3,r4=bufs[t][p]
        k=me[AX[p][0]]; ax=AX[p][0]
        ld[t,p]=[mkload(Dh(t,p,(k+1)%4,0),bp),mkload(Dh(t,p,(k+3)%4,1),bm),mkload(Dh(t,p,k),own)]
        R[t,p,"a"]=[mk(Dh(t,p,(k+2)%4,0),rlp,ax,1),mk(Dh(t,p,(k+2)%4,1),rlm,ax,3)]
        R[t,p,"b"]=[mk(Dh(t,p,(k+1)%4,1),rm.at[pl.ds(2,2)],ax,1),mk(Dh(t,p,(k+3)%4,0),rp.at[pl.ds(0,2)],ax,3),
                    mk(bp,rm.at[pl.ds(0,2)],ax,1),mk(bm,rp.at[pl.ds(2,2)],ax,3)]
        m=4 if p==0 else 2; hm=m//2
        ax=AX[p][1]; k=me[ax]
        L=pl.ds(0,hm); H=pl.ds(hm,hm)
        R[t,p,"c"]=[mk(own.at[(k+2)%4,L],rl2p,ax,1),mk(own.at[(k+2)%4,H],rl2m,ax,3)]
        R[t,p,"d"]=[mk(own.at[(k+1)%4,H],rm2.at[H],ax,1),mk(own.at[(k+3)%4,L],rp2.at[L],ax,3),
                    mk(own.at[(k+1)%4,L],rm2.at[L],ax,1),mk(own.at[(k+3)%4,H],rp2.at[H],ax,3)]
        ax=AX[p][2]; k=me[ax]; q=4 if p==0 else 2
        R[t,p,"e"]=[mk(out2.at[(k+j)%q],r3.at[j-1],ax,j) for j in (1,2,3)]
        if p==0: R[t,p,"f"]=[mk(r4.at[xh],r4.at[xh],"x",2)]
    if hasvec:
        for st in range(3):
            ax="xyz"[st]; b=vbuf[st]
            R["v",st]=[mk(b.at[me[ax]],b.at[me[ax]],ax,k) for k in (1,2,3)]
    def vgo(st,v):
        vbuf[st][pl.ds(me["xyz"[st]],1)]=v[None]
        for cp in R["v",st]: cp.start()
    def vsum(st):
        for cp in R["v",st]: cp.wait_recv()
        b=vbuf[st]
        return (b[0]+b[1])+(b[2]+b[3])
    def addin(dst,other,cntn,f,g):
        def body(i,_):
            dst[f(i)]=(f32(dst[f(i)])+f32(other[g(i)])).astype(jnp.bfloat16)
            return 0
        lax.fori_loop(0,cntn,body,0)
    def first():
        for t,p in items:
            for cp in ld[t,p]: cp.start()
        if hasvec: vgo(0,vec[...])
        for t,p in items:
            for cp in R[t,p,"a"]: cp.start()
        for t,p in items:
            for cp in R[t,p,"b"][:2]: cp.start()
    def relay(t,p):
        def f():
            own,bp,bm,rlp,rlm=bufs[t][p][:5]
            m=4 if p==0 else 2
            ix=lambda i:(i//m,i%m)
            ld[t,p][0].wait(); R[t,p,"a"][0].wait_recv(); addin(bp,rlp,2*m,ix,ix); R[t,p,"b"][2].start()
            ld[t,p][1].wait(); R[t,p,"a"][1].wait_recv(); addin(bm,rlm,2*m,ix,ix); R[t,p,"b"][3].start()
        return f
    def sum1(t,p):
        def f():
            own,bp,bm,rlp,rlm,rm,rp=bufs[t][p][:7]
            m=4 if p==0 else 2
            ld[t,p][2].wait()
            for cp in R[t,p,"b"]: cp.wait_recv()
            def body(i,_):
                j=(i//m,i%m)
                own[j]=(f32(own[j])+(f32(rm[j])+f32(rp[j]))).astype(jnp.bfloat16)
                return 0
            lax.fori_loop(0,4*m,body,0)
            for cp in R[t,p,"c"]: cp.start()
            for cp in R[t,p,"d"][:2]: cp.start()
        return f
    def relay2(t,p):
        def f():
            own,rl2p,rl2m=bufs[t][p][0],bufs[t][p][7],bufs[t][p][8]
            m=4 if p==0 else 2; hm=m//2; k=me[AX[p][1]]
            R[t,p,"c"][0].wait_recv()
            addin(own,rl2p,hm,lambda i:((k+1)%4,i),lambda i:i)
            R[t,p,"d"][2].start()
            R[t,p,"c"][1].wait_recv()
            addin(own,rl2m,hm,lambda i:((k+3)%4,hm+i),lambda i:i)
            R[t,p,"d"][3].start()
        return f
    def sum2(t,p):
        def f():
            own,rm2,rp2,out2=bufs[t][p][0],bufs[t][p][9],bufs[t][p][10],bufs[t][p][11]
            m=4 if p==0 else 2
            k=me[AX[p][1]]
            for cp in R[t,p,"d"]: cp.wait_recv()
            def body(i,_):
                out2[i]=(f32(own[k,i])+(f32(rm2[i])+f32(rp2[i]))).astype(jnp.bfloat16)
                return 0
            lax.fori_loop(0,m,body,0)
            for cp in R[t,p,"e"]: cp.start()
        return f
    def last(t,p):
        def f():
            out2,r3,r4=bufs[t][p][11:14]
            a,b=cut[t][p]
            for cp in R[t,p,"e"]: cp.wait_recv()
            k=me[AX[p][2]] if p==0 else xl
            s=(f32(out2[k])+f32(r3[1]))+(f32(r3[0])+f32(r3[2]))
            if p==0:
                r4[xh]=s.astype(jnp.bfloat16)
                R[t,p,"f"][0].start()
            else:
                out[t][:,pl.ds(a,b-a)]=s
        return f
    def end():
        for t in range(n):
            a,b=cut[t][0]; h=(b-a)//2; r4=bufs[t][0][13]
            R[t,0,"f"][0].wait_recv()
            for j in range(2): out[t][:,pl.ds(a+j*h,h)]=f32(r4[j])
        if hasvec: vout[...]=vsum(2)
        for cp in allc: cp.wait_send()
    stages=[[first]]+[[f(t,p) for t,p in items] for f in (relay,sum1,relay2,sum2)]+[[last(t,p) for t,p in sorted(items,key=lambda q:q[1])],[end]]
    if hasvec:
        stages[2].insert(0,lambda:vgo(1,vsum(0)))
        stages[4].insert(0,lambda:vgo(2,vsum(1)))
    return stages
def staggered(chains,by=2):
    order=[]
    for tick in range(7+by*(len(chains)-1)):
        for i,ch in enumerate(chains):
            if 0<=tick-by*i<7: order.append(ch[tick-by*i])
    return order
def scatter_chains(names,widths,src,vec,out,vout,scr):
    hv=vec is not None; chains=[]; at=0
    for t in range(len(names)):
        size=42+3*(hv and t==0)+3
        chains.append(scatter_steps(names[t],[widths[t]],[src[t]],vec if t==0 else None,[out[t]],vout if t==0 else None,scr[at:at+size]))
        at+=size
    return chains
def scatter_scratch(names,parts,vec=None):
    scr=[]
    for t,nm in enumerate(names):
        r,w=parts[t].shape[3:]; hv=vec is not None and t==0
        for p,(a,b) in enumerate(rcuts(nm,w)):
            m=4 if p==0 else 2; v=(b-a)//2 if p==0 else b-a; hm=m//2
            B=lambda *s:pltpu.VMEM(s+(r,v),jnp.bfloat16)
            scr+=[B(4,m),B(2,m),B(2,m),B(2,m),B(2,m),B(4,m),B(4,m),B(hm),B(hm),B(m),B(m),B(m),B(3),B(2) if p==0 else pltpu.VMEM((8,128),jnp.bfloat16)]
        if hv: scr+=[pltpu.VMEM((4,)+vec.shape,jnp.float32)]*3
        nd=46+9*hv
        scr+=[pltpu.SemaphoreType.DMA((nd,)),pltpu.SemaphoreType.DMA((nd,)),pltpu.SemaphoreType.DMA((9,))]
    return scr
def scatter_kernel(names,widths,hasvec,*refs):
    n=len(names); h=int(hasvec)
    chains=scatter_chains(names,widths,refs[:n],refs[n] if h else None,refs[n+h:2*n+h],refs[2*n+h] if h else None,refs[2*(n+h):])
    greet(RPEERS)
    for stage in staggered(chains):
        for f in stage: f()
def scatter_shapes(parts,vec=None):
    return tuple(jax.ShapeDtypeStruct(a.shape[3:],jnp.float32) for a in parts)+((jax.ShapeDtypeStruct(vec.shape,jnp.float32),) if vec is not None else ())
def reduce_scatter(names,parts,vec=None,cid=2):
    n=len(names); hv=vec is not None
    A=pl.BlockSpec(memory_space=pl.ANY); V=pl.BlockSpec(memory_space=pltpu.VMEM)
    return pl.pallas_call(functools.partial(scatter_kernel,names,[a.shape[4] for a in parts],hv),
      out_shape=scatter_shapes(parts,vec),
      in_specs=[A]*n+[V]*hv,out_specs=tuple([V]*(n+hv)),scratch_shapes=scatter_scratch(names,parts,vec),
      compiler_params=pltpu.CompilerParams(collective_id=cid,has_side_effects=True,vmem_limit_bytes=58<<20))(*parts,*([vec] if hv else []))


HD=64; LEN=4096; NEG=-1e30; ROWS=32
FQ,FK,BQ,BK=1024,1024,512,512
def dot(a,b): return lax.dot_general(a,b,(((1,),(0,)),((),())),preferred_element_type=jnp.float32)
def dot_nt(a,b): return lax.dot_general(a,b,(((1,),(1,)),((),())),preferred_element_type=jnp.float32)
def group_barrier(d,r,c,across):
    bar=pltpu.get_barrier_semaphore()
    for rr in across: pl.semaphore_signal(bar,inc=1,device_id=(1-d,rr,c),device_id_type=MESH)
    def body(i,_):
        @pl.when(i!=r*2+c)
        def _():
            pl.semaphore_signal(bar,inc=1,device_id=(d,i//2,i%2),device_id_type=MESH)
        return 0
    lax.fori_loop(0,2*ROWS,body,0)
    pl.semaphore_wait(bar,2*ROWS-1+len(across))
def push(src,dst,send_sem,recv_sem,same,target):
    @pl.when(same)
    def _():
        pltpu.make_async_copy(src,dst,recv_sem).start()
    @pl.when(jnp.logical_not(same))
    def _():
        pltpu.make_async_remote_copy(src_ref=src,dst_ref=dst,send_sem=send_sem,recv_sem=recv_sem,device_id=target,device_id_type=MESH).start()
def pushed(src,dst,send_sem,recv_sem,same,target):
    @pl.when(jnp.logical_not(same))
    def _():
        pltpu.make_async_remote_copy(src_ref=src,dst_ref=dst,send_sem=send_sem,recv_sem=recv_sem,device_id=target,device_id_type=MESH).wait_send()
def arrived(ref,sem):
    pltpu.make_async_copy(ref,ref,sem).wait()
FWD_AT=((1,2),(2,3))
BWD_AT=((0,3),(1,4),(2,5),(3,7),(4,8),(5,9))
def attn_fwd_kernel(names,widths,*refs):
    n=len(names)
    qkv_in,start=refs[:2]
    o_recv,qkv_out,oT,lse=refs[2+n:6+n]
    qkv,knt,obf,s_in,s_out,r_in,r_out,l_sem=refs[6+2*n:14+2*n]
    steps=gather_chains(names,widths,refs[2:2+n],refs[6+n:6+2*n],refs[14+2*n:])
    d=lax.axis_index("dev"); r=lax.axis_index("row"); c=lax.axis_index("col")
    group_barrier(d,r,c,[r+1-2*(r%2)])
    lanes=pl.ds(pl.multiple_of(r*128,128),128)
    def full(fn):
        def body(i,_):
            fn(qkv_in.at[i%2,:,i//2+c],qkv.at[:,:,lanes],s_in.at[i],r_in,i==r,(d,i,c))
            return 0
        lax.fori_loop(0,24,body,0)
    def halves(fn):
        rows=pl.ds(pl.multiple_of(32*c,32),32)
        for s in range(2):
            fn(qkv_in.at[s,:,12*(1-c),rows],qkv.at[:,rows,lanes],s_in.at[24+s],r_in,(r==24+s)&(c==0),(d,24+s,0))
    full(push); halves(push)
    steps[0]()
    item=(r<24)|((c==0)&(r<26))
    head=r//2+13*c; seq=r%2
    def outs(qi,fn):
        def body(i,_):
            rr=qi*(FQ//128)+i//2; cc=i%2
            fn(obf.at[:,pl.ds(pl.multiple_of(rr*128,128),128)],o_recv.at[seq,head],s_out.at[rr*2+cc],r_out,(rr==r)&(cc==c),(d,rr,cc))
            return 0
        lax.fori_loop(0,FQ//64,body,0)
    save=pltpu.make_async_copy(qkv,qkv_out,l_sem)
    @pl.when(item)
    def _():
        arrived(qkv,r_in)
        save.start()
        for a in range(LEN//512):
            sl=pl.ds(a*512,512)
            knt[sl,:]=qkv[1,:,sl].T
    steps[1]()
    def qloop(qi,_):
        @pl.when(item)
        def _():
            iota=lax.broadcasted_iota(jnp.int32,(FK,FQ),0)
            iotl=lax.broadcasted_iota(jnp.int32,(FK,FQ),1)
            qs=pl.ds(pl.multiple_of(qi*FQ,FQ),FQ)
            q=qkv[0,:,qs]*jnp.bfloat16(0.125)
            st=start[:,qs]
            def step(kj,carry,diag):
                m,l,acc=carry
                ks=pl.ds(pl.multiple_of(kj*FK,FK),FK)
                s=dot(knt[ks,:],q)
                ok=iota>=(st-kj*FK)
                if diag: ok=ok&(iota<=iotl)
                s=jnp.where(ok,s,NEG)
                mn=jnp.maximum(m,jnp.max(s,axis=0,keepdims=True))
                p=jnp.exp(s-mn)
                al=jnp.exp(m-mn)
                l=l*al+jnp.sum(p,axis=0,keepdims=True)
                acc=acc*al+dot(qkv[2,:,ks],p.astype(jnp.bfloat16))
                return mn,l,acc
            carry=(jnp.full((1,FQ),NEG,jnp.float32),jnp.zeros((1,FQ),jnp.float32),jnp.zeros((HD,FQ),jnp.float32))
            carry=lax.fori_loop(0,qi,lambda kj,cr:step(kj,cr,False),carry)
            m,l,acc=step(qi,carry,True)
            o=acc/l
            oT[:,qs]=o
            lse[:,qs]=m+jnp.log(l)
            obf[:,qs]=o.astype(jnp.bfloat16)
            outs(qi,push)
        for at,f in FWD_AT:
            pl.when(qi==at)(steps[f])
        return 0
    lax.fori_loop(0,LEN//FQ,qloop,0)
    for f in range(FWD_AT[-1][1]+1,6): steps[f]()
    @pl.when(item)
    def _():
        save.wait()
        for qi in range(LEN//FQ): outs(qi,pushed)
    full(pushed); halves(pushed)
    arrived(o_recv,r_out)
def attn_bwd_kernel(names,widths,*refs):
    n=len(names)
    do_in,qkv,oT,start,lse=refs[:5]
    d_recv=refs[5+n]
    doT,knt,vnt,dqa,delta,dout,s_in,s_out,r_in,r_out=refs[6+2*n:16+2*n]
    order=staggered(scatter_chains(names,widths,refs[5:5+n],None,refs[6+n:6+2*n],None,refs[16+2*n:]))
    d=lax.axis_index("dev"); r=lax.axis_index("row"); c=lax.axis_index("col")
    group_barrier(d,r,c,[r+1-2*(r%2),r])
    lanes=pl.ds(pl.multiple_of(r*128,128),128)
    def full(fn):
        def body(i,_):
            fn(do_in.at[i%2,i//2+c],doT.at[:,lanes],s_in.at[i],r_in,i==r,(d,i,c))
            return 0
        lax.fori_loop(0,24,body,0)
    def halves(fn):
        rows=pl.ds(pl.multiple_of(32*c,32),32)
        for s in range(2):
            fn(do_in.at[s,12*(1-c),rows],doT.at[rows,lanes],s_in.at[24+s],r_in,(r==24+s)&(c==0),(d,24+s,0))
    full(push); halves(push)
    order[0][0]()
    item=(r<24)|((c==0)&(r<26))
    def outs(fn):
        @pl.when(r<24)
        def _():
            def body(i,_):
                fn(dout.at[:,:,pl.ds(pl.multiple_of(i*128,128),128)],d_recv.at[:,(r%2)*13+r//2+c],s_out.at[i],r_out,i==r,(d,i,c))
                return 0
            lax.fori_loop(0,ROWS,body,0)
        @pl.when(r>=24)
        def _():
            def body(i,_):
                rr=i//2; cc=i%2
                rows=pl.ds(pl.multiple_of(32*cc,32),32)
                fn(dout.at[:,rows,pl.ds(pl.multiple_of(rr*128,128),128)],d_recv.at[:,(r%2)*13+12*(1-cc),rows],s_out.at[i],r_out,(rr==r)&(cc==c),(d,rr,cc))
                return 0
            lax.fori_loop(0,2*ROWS,body,0)
    @pl.when(item)
    def _():
        for a in range(LEN//512):
            sl=pl.ds(a*512,512)
            knt[sl,:]=qkv[1,:,sl].T
            vnt[sl,:]=qkv[2,:,sl].T
        dqa[...]=jnp.zeros_like(dqa)
        arrived(doT,r_in)
        for a in range(LEN//512):
            sl=pl.ds(a*512,512)
            delta[:,sl]=jnp.sum(oT[:,sl]*doT[:,sl].astype(jnp.float32),axis=0,keepdims=True)
    def kloop(kj,_):
        @pl.when(item)
        def _():
            iota=lax.broadcasted_iota(jnp.int32,(BK,BQ),0)
            iotl=lax.broadcasted_iota(jnp.int32,(BK,BQ),1)
            ks=pl.ds(pl.multiple_of(kj*BK,BK),BK)
            kn=knt[ks,:]; vn=vnt[ks,:]; kT=qkv[1,:,ks]
            def step(qi,carry,diag):
                dk,dv=carry
                qs=pl.ds(pl.multiple_of(qi*BQ,BQ),BQ)
                q=qkv[0,:,qs]*jnp.bfloat16(0.125)
                do=doT[:,qs]
                s=dot(kn,q)
                ok=iota>=(start[:,qs]-kj*BK)
                if diag: ok=ok&(iota<=iotl)
                p=jnp.exp(jnp.where(ok,s,NEG)-lse[:,qs])
                dp=dot(vn,do)
                ds=(p*(dp-delta[:,qs])).astype(jnp.bfloat16)
                dv=dv+dot_nt(do,p.astype(jnp.bfloat16))
                dk=dk+dot_nt(q,ds)
                dqa[:,qs]+=dot(kT,ds)
                return dk,dv
            z=jnp.zeros((HD,BK),jnp.float32)
            carry=step(kj,(z,z),True)
            dk,dv=lax.fori_loop(kj+1,LEN//BQ,lambda qi,cr:step(qi,cr,False),carry)
            dout[1,:,ks]=dk.astype(jnp.bfloat16)
            dout[2,:,ks]=dv.astype(jnp.bfloat16)
        at=1
        for step,to in BWD_AT:
            for stage in order[at:to]:
                for f in stage: pl.when(kj==step)(f)
            at=to
        return 0
    lax.fori_loop(0,LEN//BK,kloop,0)
    @pl.when(item)
    def _():
        for a in range(LEN//512):
            sl=pl.ds(a*512,512)
            dout[0,:,sl]=(dqa[:,sl]*0.125).astype(jnp.bfloat16)
        outs(push)
    for stage in order[BWD_AT[-1][1]:]:
        for f in stage: f()
    pl.when(item)(lambda:outs(pushed))
    full(pushed); halves(pushed)
    arrived(d_recv.at[:,pl.ds(0,25)],r_out)
VM=pl.BlockSpec(memory_space=pltpu.VMEM); ANY=pl.BlockSpec(memory_space=pl.ANY)
bf=jnp.bfloat16
def attend(qkv,start,names,arrs,cid=1):
    S=jax.ShapeDtypeStruct; n=len(names)
    out=pl.pallas_call(functools.partial(attn_fwd_kernel,names,[a.shape[1] for a in arrs]),
      out_shape=(S((2,25,HD,128),bf),S((3,HD,LEN),bf),S((HD,LEN),jnp.float32),S((1,LEN),jnp.float32))+gather_shapes(arrs),
      in_specs=[VM,VM]+[ANY]*n,out_specs=(ANY,ANY,VM,VM)+(ANY,)*n,
      scratch_shapes=[pltpu.VMEM((3,HD,LEN),bf),pltpu.VMEM((LEN,HD),bf),pltpu.VMEM((HD,LEN),bf),
        pltpu.SemaphoreType.DMA((26,)),pltpu.SemaphoreType.DMA((64,)),pltpu.SemaphoreType.DMA,pltpu.SemaphoreType.DMA,pltpu.SemaphoreType.DMA]+gather_sems(n),
      compiler_params=pltpu.CompilerParams(collective_id=cid,has_side_effects=True,vmem_limit_bytes=50<<20))(qkv,start,*arrs)
    return out[0],out[1:4],out[4:]
def attend_back(do,kept,start,names,parts,cid=3):
    S=jax.ShapeDtypeStruct; n=len(names)
    qkv,oT,lse=kept
    out=pl.pallas_call(functools.partial(attn_bwd_kernel,names,[a.shape[4] for a in parts]),
      out_shape=(S((3,26,HD,128),bf),)+scatter_shapes(parts),
      in_specs=[VM]*5+[ANY]*n,out_specs=(ANY,)+(VM,)*n,
      scratch_shapes=[pltpu.VMEM((HD,LEN),bf),pltpu.VMEM((LEN,HD),bf),pltpu.VMEM((LEN,HD),bf),pltpu.VMEM((HD,LEN),jnp.float32),pltpu.VMEM((1,LEN),jnp.float32),pltpu.VMEM((3,HD,LEN),bf),
        pltpu.SemaphoreType.DMA((26,)),pltpu.SemaphoreType.DMA((64,)),pltpu.SemaphoreType.DMA,pltpu.SemaphoreType.DMA]+scatter_scratch(names,parts),
      compiler_params=pltpu.CompilerParams(collective_id=cid,has_side_effects=True,vmem_limit_bytes=60<<20))(do,qkv,oT,start,lse,*parts)
    return out[0],out[1:]


TT=256; WC=800; FH=3200; TF=640; KH=896
GC=0.7978845608028654
def dot_tn(a,b): return lax.dot_general(a,b,(((0,),(0,)),((),())),preferred_element_type=jnp.float32)
def mlp_kernel(h2,we,eb,wc,mid,cb,g,result,part_c,part_e,dh2,dsum,
        wev,wcv,pre,a_own,a_recv,da_send,da_recv,dpre,dh_send,dh_recv,stage_e,stage_c,w_sem,s_sem,r_sem,e_sem,c_sem):
    c=lax.axis_index("col"); other=1-c
    partner=(lax.axis_index("dev"),lax.axis_index("row"),other)
    loads=[pltpu.make_async_copy(wc,wcv,w_sem.at[0]),pltpu.make_async_copy(we,wev,w_sem.at[1])]
    for cp in loads: cp.start()
    bar=pltpu.get_barrier_semaphore()
    pl.semaphore_signal(bar,inc=1,device_id=partner,device_id_type=MESH)
    pl.semaphore_wait(bar,1)
    def swap(i,s,d):
        return pltpu.make_async_remote_copy(src_ref=s,dst_ref=d,send_sem=s_sem.at[i],recv_sem=r_sem.at[i],device_id=partner,device_id_type=MESH)
    x_da,x_a,x_dh=swap(0,da_send,da_recv),swap(1,a_own,a_recv),swap(2,dh_send,dh_recv)
    lanes=lambda k,n:pl.ds(pl.multiple_of(k*n,128),n)
    rows=lambda base,k,n:pl.ds(pl.multiple_of(base+k*n,128),n)
    f32=lambda v:v.astype(jnp.float32)
    NT=FH//TF
    def loop(n,f):
        def body(k,_):
            f(k)
            return 0
        lax.fori_loop(0,n,body,0)
    loads[0].wait()
    def f(k): da_send[:,lanes(k,TF)]=dot_nt(g[...],wcv[rows(other*FH,k,TF),:]).astype(bf)
    loop(NT,f)
    x_da.start()
    loads[1].wait()
    def f(k):
        p=dot(h2[...],wev[:,lanes(k,TF)])+eb[:,lanes(k,TF)]
        pre[:,lanes(k,TF)]=p
        a_own[:,lanes(k,TF)]=(p*(0.5*(1.0+jnp.tanh(GC*(p+0.044715*(p*p*p)))))).astype(bf)
    loop(NT,f)
    x_a.start()
    x_da.wait_recv()
    def f(k):
        sl=lanes(k,TF)
        d=dot_nt(g[...],wcv[rows(c*FH,k,TF),:])+f32(da_recv[:,sl])
        p=pre[:,sl]
        t=jnp.tanh(GC*(p+0.044715*(p*p*p)))
        slope=0.5*(1.0+t)+p*(0.5*(1.0-t*t)*(GC*(1.0+(3*0.044715)*(p*p))))
        dp=(d*slope).astype(bf)
        dpre[:,sl]=dp
        dsum[:,sl]=jnp.sum(f32(dp),axis=0,keepdims=True)
    loop(NT,f)
    def f(k): dh_send[:,lanes(k,128)]=dot_nt(dpre[...],wev[rows(other*KH,k,128),:]).astype(bf)
    loop(KH//128,f)
    x_dh.start()
    def f(k): dh2[:,lanes(k,128)]=dot_nt(dpre[...],wev[rows(c*KH,k,128),:])
    loop(KH//128,f)
    def emit(i,stage,sem,dst,value):
        slot=i%2
        cp=pltpu.make_async_copy(stage.at[slot],dst,sem.at[slot])
        if i>=2: prev[slot].wait()
        stage[slot]=value
        cp.start(); prev[slot]=cp
    prev={}
    for j in range(KP//256):
        emit(j,stage_e,e_sem,part_e.at[pl.ds(256*j,256)],dot_tn(h2[:,256*j:256*j+256],dpre[...]).astype(bf))
    for cp in prev.values(): cp.wait()
    x_a.wait_recv()
    br=dot(a_own[...],wcv[rows(c*FH,0,FH),:])+dot(a_recv[...],wcv[rows(other*FH,0,FH),:])
    result[...]=(mid[...]+(br+cb[...])).astype(bf)
    prev={}
    for i in range(2*NT):
        a,b,k=(a_own,c,i) if i<NT else (a_recv,other,i-NT)
        emit(i,stage_c,c_sem,part_c.at[rows(b*FH,k,TF)],dot_tn(a[:,k*TF:k*TF+TF],g[...]).astype(bf))
    x_dh.wait_recv()
    dh2[...]=dh2[...]+f32(dh_recv[...])
    for cp in prev.values(): cp.wait()
    for cp in (x_da,x_a,x_dh): cp.wait_send()
def mlp(h2,we,eb,wc,mid,cb,g,cid=4):
    S=jax.ShapeDtypeStruct; f=jnp.float32; V=pltpu.VMEM
    return pl.pallas_call(mlp_kernel,
      out_shape=(S((TT,WC),bf),S((6400,WC),bf),S((KP,FH),bf),S((TT,KH),f),S((1,FH),f)),
      in_specs=[VM,ANY,VM,ANY,VM,VM,VM],out_specs=(VM,ANY,ANY,VM,VM),
      scratch_shapes=[V((KP,FH),bf),V((6400,WC),bf),V((TT,FH),f)]+[V((TT,FH),bf)]*5+[V((TT,KH),bf)]*2+[V((2,256,FH),bf),V((2,TF,WC),bf)]+[pltpu.SemaphoreType.DMA((n,)) for n in (2,3,3,2,2)],
      compiler_params=pltpu.CompilerParams(collective_id=cid,has_side_effects=True,vmem_limit_bytes=58<<20))(h2,we,eb,wc,mid,cb,g)
def pair_dot_kernel(v,w,out,send,recv,s_sem,r_sem):
    c=lax.axis_index("col"); other=1-c
    partner=(lax.axis_index("dev"),lax.axis_index("row"),other)
    bar=pltpu.get_barrier_semaphore()
    pl.semaphore_signal(bar,inc=1,device_id=partner,device_id_type=MESH)
    for k in range(KH//128):
        send[:,128*k:128*k+128]=dot_nt(v[...],w[pl.ds(pl.multiple_of(other*KH+128*k,128),128),:]).astype(bf)
    pl.semaphore_wait(bar,1)
    cp=pltpu.make_async_remote_copy(src_ref=send,dst_ref=recv,send_sem=s_sem,recv_sem=r_sem,device_id=partner,device_id_type=MESH)
    cp.start()
    for k in range(KH//128):
        out[:,128*k:128*k+128]=dot_nt(v[...],w[pl.ds(pl.multiple_of(c*KH+128*k,128),128),:])
    cp.wait()
    out[...]=out[...]+recv[...].astype(jnp.float32)
def pair_dot(v,w,cid):
    return pl.pallas_call(pair_dot_kernel,out_shape=jax.ShapeDtypeStruct((TT,KH),jnp.float32),in_specs=[VM,VM],out_specs=VM,
      scratch_shapes=[pltpu.VMEM((TT,KH),bf)]*2+[pltpu.SemaphoreType.DMA]*2,
      compiler_params=pltpu.CompilerParams(collective_id=cid,has_side_effects=True,vmem_limit_bytes=40<<20))(v,w)
def outer_kernel(a,b,o):
    o[...]=dot_tn(a[...],b[...]).astype(bf)
def outer(a,b):
    m=a.shape[1]; n=b.shape[1]
    return pl.pallas_call(outer_kernel,out_shape=jax.ShapeDtypeStruct((m,n),bf),grid=(m//256,),
      in_specs=[pl.BlockSpec((TT,256),lambda i:(0,i)),pl.BlockSpec((TT,n),lambda i:(0,0))],out_specs=pl.BlockSpec((256,n),lambda i:(i,0)),
      compiler_params=pltpu.CompilerParams(vmem_limit_bytes=32<<20))(a,b)


def width_sums(first_sum, second_sum):
    return lax.psum((first_sum, second_sum), "col")


def full_rows(values):
    return lax.all_gather(values, "col", axis=1, tiled=True)


def norm_forward(values, norm_gain, norm_bias):
    totals = width_sums(jnp.sum(values, axis=1), jnp.sum(values * values, axis=1))
    averages = totals[0] / D
    reciprocal = lax.rsqrt(totals[1] / D - averages * averages + 1e-05)
    normed = (values - averages[:, None]) * reciprocal[:, None]
    return (normed, reciprocal, normed * norm_gain + norm_bias)


def norm_backward(incoming, normed, reciprocal, norm_gain):
    scaled = incoming * norm_gain
    totals = width_sums(jnp.sum(scaled, axis=1), jnp.sum(scaled * normed, axis=1))
    return reciprocal[:, None] * (
        scaled - totals[0][:, None] / D - normed * (totals[1][:, None] / D)
    )


def pad_rows(block):
    return jnp.pad(block, ((0, 6), (0, 0)))


def pad_features(values):
    n = values.shape[0]
    return jnp.pad(values.reshape(n, 32, 50), ((0, 0), (0, 0), (0, 6))).reshape(n, KP)


def unpad_features(values):
    n = values.shape[0]
    return values.reshape(n, 16, 56)[:, :, :50].reshape(n, 800)


def per_device(
    tokens,
    segments,
    first_gain,
    first_bias,
    attention_in,
    attention_bias,
    attention_out,
    output_bias,
    second_gain,
    second_bias,
    expand_weight,
    expand_bias,
    contract_weight,
    contract_bias,
    cotangent,
):
    seqs, block_len, width = tokens.shape
    row_total = seqs * block_len
    row = lax.axis_index("row")
    col = lax.axis_index("col")
    weight_qkv, weight_expand = gather(
        "qe", (pad_rows(attention_in.reshape(50, 3 * width)), pad_rows(expand_weight)), 0
    )
    weight_qkv = weight_qkv.reshape(KP, 3 * width)

    own_seg = lax.dynamic_index_in_dim(segments, row % 2, 0, keepdims=True)
    positions = jnp.arange(LEN, dtype=jnp.int32)[None]
    before = jnp.concatenate((own_seg[:, :1], own_seg[:, :-1]), axis=1)
    start = lax.cummax(jnp.where(own_seg != before, positions, 0), axis=1)

    float_tokens = tokens.astype(jnp.float32).reshape(row_total, width)
    normed_one, recip_one, hidden_one = norm_forward(float_tokens, first_gain, first_bias)
    rows_one = pad_features(full_rows(hidden_one.astype(jnp.bfloat16)))
    bias_three = jnp.concatenate(
        (attention_bias[0], jnp.zeros_like(attention_bias[0]), attention_bias[1])
    )
    projected = jnp.einsum(
        "dm,snd->smn",
        weight_qkv,
        rows_one.reshape(seqs, block_len, KP),
        preferred_element_type=jnp.float32,
    )
    projected = (projected + bias_three[None, :, None]).astype(jnp.bfloat16)
    projected = projected.reshape(seqs, 3, width, block_len)

    def head_slots(values):
        lead = [(0, 0)] * (values.ndim - 2)
        slots = jnp.where(
            col == 0,
            jnp.pad(values, lead + [(0, 32), (0, 0)]),
            jnp.pad(values, lead + [(32, 0), (0, 0)]),
        )
        return slots.reshape(values.shape[:-2] + (13, HD, block_len))

    attended, kept, gathered = attend(
        head_slots(projected),
        start,
        "co",
        (contract_weight, pad_rows(attention_out)),
        1,
    )
    weight_out = gathered[1].reshape(KP, width)
    weight_expand = weight_expand.reshape(KP, 4 * width)
    weight_contract = gathered[0].reshape(4 * D, width)
    rows_attn = jnp.pad(
        attended.reshape(seqs, 32, 50, block_len), ((0, 0), (0, 0), (0, 6), (0, 0))
    ).reshape(seqs, KP, block_len)
    middle = float_tokens + (
        jnp.einsum(
            "sfn,fd->snd", rows_attn, weight_out, preferred_element_type=jnp.float32
        ).reshape(row_total, width)
        + output_bias
    )
    normed_two, recip_two, hidden_two = norm_forward(middle, second_gain, second_bias)
    rows_two = pad_features(full_rows(hidden_two.astype(jnp.bfloat16)))
    grad_low = cotangent.reshape(row_total, width)
    grad_float = grad_low.astype(jnp.float32)
    result, part_contract, part_expand, grad_two, expand_sums = mlp(
        rows_two, weight_expand, expand_bias[None], weight_contract, middle, contract_bias[None], grad_low, 4
    )
    result = result.reshape(tokens.shape)
    grad_two = unpad_features(grad_two)
    grad_middle = grad_float + norm_backward(grad_two, normed_two, recip_two, second_gain)
    grad_attn = grad_middle.astype(jnp.bfloat16)
    part_out = outer(jnp.transpose(rows_attn, (0, 2, 1)).reshape(row_total, KP), grad_attn)
    grad_mixed = unpad_features(pair_dot(grad_attn, weight_out, 5).astype(jnp.bfloat16))
    grad_mixed = jnp.transpose(grad_mixed.reshape(seqs, block_len, width), (0, 2, 1))
    grad_slots, (sum_contract, sum_expand) = attend_back(
        head_slots(grad_mixed),
        kept,
        start,
        "ce",
        (part_contract.reshape(4, 4, 2, 200, width), part_expand.reshape(4, 4, 2, 56, 4 * width)),
        2,
    )
    grad_qkv = lax.dynamic_slice_in_dim(
        grad_slots.reshape(3, seqs, 13 * HD, block_len), 32 * col, width, 2
    )
    grad_rows = jnp.transpose(grad_qkv, (1, 3, 0, 2)).reshape(row_total, 3 * width)
    part_qkv = outer(rows_one, grad_rows)
    grad_one = unpad_features(pair_dot(grad_rows, weight_qkv, 6))
    grad_input = grad_middle + norm_backward(grad_one, normed_one, recip_one, first_gain)
    gradient_tokens = grad_input.astype(jnp.bfloat16).reshape(tokens.shape)
    qkv_sums = jnp.sum(grad_qkv.astype(jnp.float32), axis=(1, 3))
    pieces = (
        jnp.sum(grad_one * normed_one, axis=0),
        jnp.sum(grad_one, axis=0),
        qkv_sums[0],
        qkv_sums[2],
        jnp.sum(grad_attn.astype(jnp.float32), axis=0),
        jnp.sum(grad_two * normed_two, axis=0),
        jnp.sum(grad_two, axis=0),
        expand_sums[0],
        jnp.sum(grad_float, axis=0),
    )
    vector = jnp.concatenate(pieces + (jnp.zeros((640,), jnp.float32),)).reshape(80, 128)
    sum_qkv, sum_out, vector = reduce_scatter(
        "qo",
        (part_qkv.reshape(4, 4, 2, 56, 3 * width), part_out.reshape(4, 4, 2, 56, width)),
        vector,
        3,
    )
    vector = vector.reshape(-1)
    sums = []
    at = 0
    for piece in pieces:
        sums.append(vector[at : at + piece.shape[0]])
        at += piece.shape[0]
    return (
        result,
        gradient_tokens,
        sums[0],
        sums[1],
        sum_qkv[:50].reshape(50, 3, width),
        jnp.stack((sums[2], sums[3])),
        sum_out[:50],
        sums[4],
        sums[5],
        sums[6],
        sum_expand[:50],
        sums[7],
        sum_contract,
        sums[8],
    )


def solution(mesh):
    return jax.shard_map(
        per_device,
        mesh=mesh,
        in_specs=(
            P("dev", "row", "col"),
            P("dev", None),
            P("col"),
            P("col"),
            P("row", None, "col"),
            P(None, "col"),
            P("row", "col"),
            P("col"),
            P("col"),
            P("col"),
            P("row", "col"),
            P("col"),
            P("row", "col"),
            P("col"),
            P("dev", "row", "col"),
        ),
        out_specs=(
            P("dev", "row", "col"),
            P("dev", "row", "col"),
            P("col"),
            P("col"),
            P("row", None, "col"),
            P(None, "col"),
            P("row", "col"),
            P("col"),
            P("col"),
            P("col"),
            P("row", "col"),
            P("col"),
            P("row", "col"),
            P("col"),
        ),
        check_vma=False,
    )
```

```python
import functools

import jax
import jax.numpy as jnp
from jax import lax
from jax.experimental import pallas as pl
from jax.experimental.pallas import tpu as pltpu
from jax.sharding import PartitionSpec as P

MESH = pl.DeviceIdType.MESH
D = 1600
KP = 1792


def coords():
    d=lax.axis_index("dev"); r=lax.axis_index("row"); c=lax.axis_index("col")
    return r//8, (r//2)%4, d*2+r%2, c
def place(z,y,x,c):
    return (x//2, (z*4+y)*2+x%2, c)
def peer_of(ax,k):
    z,y,x,c=coords()
    if ax=="z": z=(z+k)%4
    if ax=="y": y=(y+k)%4
    if ax=="x": x=(x+k)%4
    return place(z,y,x,c)
def greet(peers):
    bar=pltpu.get_barrier_semaphore()
    for ax,k in peers: pl.semaphore_signal(bar,inc=1,device_id=peer_of(ax,k),device_id_type=MESH)
    pl.semaphore_wait(bar,len(peers))
SPLIT={"q":(4,4,6,5),"o":(2,1,2,2),"e":(7,4,7,7),"c":(1,2,2,2)}
ORD=("yzx","zyx","yxz","zxy")
GPEERS=[("z",1),("z",3),("z",2),("y",1),("y",3),("y",2),("x",1),("x",3)]
def cuts(name,W):
    out=[];p=0
    for n in SPLIT[name]:
        out.append((p,min(p+n*128,W))); p+=n*128
    assert out[-1][1]==W,(name,out)
    return out
def gather_steps(names,widths,src,dst,ss,rs,ls):
    n=len(names)
    z,y,x,c=coords(); xl=x%2
    cnt=[0]; allc=[]
    FULL=slice(None)
    LO=pl.ds(0,2); HI=pl.ds(2,2)
    def mk(s,d,ax,k):
        i=cnt[0]; cnt[0]+=1
        cp=pltpu.make_async_remote_copy(src_ref=s,dst_ref=d,send_sem=ss.at[i],recv_sem=rs.at[i],device_id=peer_of(ax,k),device_id_type=MESH)
        allc.append(cp); return cp
    cut=[cuts(nm,w) for nm,w in zip(names,widths)]
    def at(t,p,zi,yi,xi):
        a,b=cut[t][p]
        return dst[t].at[zi,yi,xi,:,pl.ds(a,b-a)]
    def wait(l):
        for cp in l: cp.wait_recv()
    def go(l):
        for cp in l: cp.start()
    loc=[pltpu.make_async_copy(src[t],dst[t].at[z,y,xl],ls.at[t]) for t in range(n)]
    st1=[[],[],[],[]]
    for t in range(n):
        for p in range(4):
            a,b=cut[t][p]
            for k in (1,3,2):
                st1[p].append(mk(src[t].at[:,pl.ds(a,b-a)],at(t,p,z,y,xl),ORD[p][0],k))
    def both(p,f):
        return [cp for t in range(n) for cp in f(t,p)]
    def xsend(zi,yi):
        return lambda t,p:[mk(at(t,p,*zi,xl),at(t,p,*zi,xl),"x",1),mk(at(t,p,*yi,xl),at(t,p,*yi,xl),"x",3)]
    def ring_a(ax,zi,yi,xi):
        return lambda t,p:[mk(at(t,p,zi,yi,xi),at(t,p,zi,yi,xi),ax,k) for k in (1,3)]
    def ring_b(ax,xi):
        def f(t,p):
            if ax=="z":
                u=at(t,p,(z+3)%4,LO,xi); v=at(t,p,(z+1)%4,HI,xi)
            else:
                u=at(t,p,LO,(y+3)%4,xi); v=at(t,p,HI,(y+1)%4,xi)
            return [mk(u,u,ax,1),mk(v,v,ax,3)]
        return f
    A2=both(0,ring_a("z",z,FULL,xl)); B2=both(1,ring_a("y",FULL,y,xl))
    C2=both(2,xsend((z,LO),(z,HI))); D2=both(3,xsend((LO,y),(HI,y)))
    A2b=both(0,ring_b("z",xl)); B2b=both(1,ring_b("y",xl))
    C3=both(2,ring_a("z",z,FULL,FULL)); D3=both(3,ring_a("y",FULL,y,FULL))
    A3=both(0,xsend((LO,FULL),(HI,FULL))); B3=both(1,xsend((LO,FULL),(HI,FULL)))
    C3b=both(2,ring_b("z",FULL)); D3b=both(3,ring_b("y",FULL))
    def f0():
        go(loc)
        for p in range(4): go(st1[p])
    def f1():
        wait_loc=[cp.wait() for cp in loc]
        wait(st1[0]); go(A2)
        wait(st1[1]); go(B2)
        wait(st1[2]); go(C2)
        wait(st1[3]); go(D2)
    def f2():
        wait(A2); go(A2b); wait(B2); go(B2b)
        wait(C2); go(C3); wait(D2); go(D3)
    def f3():
        wait(A2b); go(A3); wait(B2b); go(B3)
    def f4():
        wait(C3); go(C3b); wait(D3); go(D3b)
    def f5():
        wait(A3);wait(B3);wait(C3b);wait(D3b)
        for cp in allc: cp.wait_send()
    return [f0,f1,f2,f3,f4,f5]
def gather_sems(n):
    return [pltpu.SemaphoreType.DMA((36,)),pltpu.SemaphoreType.DMA((36,)),pltpu.SemaphoreType.DMA((1,))]*n
def gather_chains(names,widths,src,dst,sems):
    chains=[gather_steps(names[t],[widths[t]],[src[t]],[dst[t]],*sems[3*t:3*t+3]) for t in range(len(names))]
    def both(k):
        def f():
            for ch in chains: ch[k]()
        return f
    return [both(k) for k in range(6)]
def gather_kernel(names,widths,*refs):
    n=len(names)
    steps=gather_chains(names,widths,refs[:n],refs[n:2*n],refs[2*n:])
    greet(GPEERS)
    for f in steps: f()
def gather_shapes(arrs):
    return tuple(jax.ShapeDtypeStruct((4,4,2)+a.shape,a.dtype) for a in arrs)
def gather(names,arrs,cid=0):
    n=len(names)
    return pl.pallas_call(functools.partial(gather_kernel,names,[a.shape[1] for a in arrs]),
      out_shape=gather_shapes(arrs),
      in_specs=[pl.BlockSpec(memory_space=pl.ANY)]*n,out_specs=tuple([pl.BlockSpec(memory_space=pl.ANY)]*n),
      scratch_shapes=gather_sems(n),
      compiler_params=pltpu.CompilerParams(collective_id=cid,has_side_effects=True))(*arrs)


RSPLIT={"q":(6,7,6),"o":(2,3,2),"e":(10,7,8),"c":(2,3,2)}
AX=("xzy","yzx","zyx")
RPEERS=[(a,k) for a in "xyz" for k in (1,2,3)]
def rcuts(name,W):
    out=[];p=0
    for n in RSPLIT[name]:
        out.append((p,min(p+n*128,W))); p+=n*128
    assert out[-1][1]==W,(name,out)
    return out
def scatter_steps(nm,width,src,out,bufs,sems):
    ss,rs,ls=sems
    z,y,x,c=coords(); xl=x%2; xh=x//2
    me={"x":x,"y":y,"z":z}
    cnt=[0]; lcnt=[0]; allc=[]
    def mk(s,d,ax,k,keep=True):
        i=cnt[0]; cnt[0]+=1
        cp=pltpu.make_async_remote_copy(src_ref=s,dst_ref=d,send_sem=ss.at[i],recv_sem=rs.at[i],device_id=peer_of(ax,k),device_id_type=MESH)
        if keep: allc.append(cp)
        return cp
    def mkload(s,d):
        i=lcnt[0]; lcnt[0]+=1
        return pltpu.make_async_copy(s,d,ls.at[i])
    cut=rcuts(nm,width)
    f32=lambda a:a.astype(jnp.float32)
    def D(p,k,i=None):
        a,b=cut[p]; s=slice(None) if i is None else pl.ds(2*i,2)
        if p==0:
            h=(b-a)//2
            return src.at[s,:,k%2,:,pl.ds(pl.multiple_of(a+(k//2)*h,128),h)]
        if p==1: return src.at[s,k,:,:,pl.ds(a,b-a)]
        return src.at[k,s,:,:,pl.ds(a,b-a)]
    M=(4,2,2); P3=(0,1,2)
    ld={}; R={}
    for p in P3:
        own,rlp,rlm,rm,rp,rl2p,rl2m,rm2,rp2,out2,r3,r4=bufs[p]
        k=me[AX[p][0]]; ax=AX[p][0]
        bp=own.at[pl.ds(0,2)]; bm=own.at[pl.ds(2,2)]
        ld[p]=[mkload(D(p,(k+1)%4,0),bp),mkload(D(p,(k+3)%4,1),bm),mkload(D(p,k),own)]
        R[p,"a"]=[mk(D(p,(k+2)%4,0),rlp,ax,1),mk(D(p,(k+2)%4,1),rlm,ax,3)]
        R[p,"b"]=[mk(D(p,(k+1)%4,1),rm.at[pl.ds(2,2)],ax,1),mk(D(p,(k+3)%4,0),rp.at[pl.ds(0,2)],ax,3),
                  mk(bp,rm.at[pl.ds(0,2)],ax,1,False),mk(bm,rp.at[pl.ds(2,2)],ax,3,False)]
        m=M[p]; hm=m//2
        ax=AX[p][1]; k=me[ax]
        L=pl.ds(0,hm); H=pl.ds(hm,hm)
        R[p,"c"]=[mk(own.at[(k+2)%4,L],rl2p,ax,1),mk(own.at[(k+2)%4,H],rl2m,ax,3)]
        R[p,"d"]=[mk(own.at[(k+1)%4,H],rm2.at[H],ax,1),mk(own.at[(k+3)%4,L],rp2.at[L],ax,3),
                  mk(own.at[(k+1)%4,L],rm2.at[L],ax,1),mk(own.at[(k+3)%4,H],rp2.at[H],ax,3)]
        ax=AX[p][2]; k=me[ax]; q=4 if p==0 else 2
        R[p,"e"]=[mk(out2.at[(k+j)%q],r3.at[j-1],ax,j) for j in (1,2,3)]
        if p==0: R[p,"f"]=[mk(r4.at[xh],r4.at[xh],"x",2)]
    def addin(dst,other,cntn,f,g):
        def body(i,_):
            dst[f(i)]=(f32(dst[f(i)])+f32(other[g(i)])).astype(jnp.bfloat16)
            return 0
        lax.fori_loop(0,cntn,body,0)
    def first():
        for p in P3:
            for cp in ld[p][:2]: cp.start()
        for p in P3:
            for cp in R[p,"a"]: cp.start()
        for p in P3:
            for cp in R[p,"b"][:2]: cp.start()
    def relay(p):
        def f():
            own,rlp,rlm=bufs[p][:3]
            m=M[p]
            ld[p][0].wait(); R[p,"a"][0].wait_recv(); addin(own,rlp,2*m,lambda i:(i//m,i%m),lambda i:(i//m,i%m)); R[p,"b"][2].start()
            ld[p][1].wait(); R[p,"a"][1].wait_recv(); addin(own,rlm,2*m,lambda i:(2+i//m,i%m),lambda i:(i//m,i%m)); R[p,"b"][3].start()
        return f
    def reload(p):
        def f():
            for cp in R[p,"b"][2:]: cp.wait_send()
            ld[p][2].start()
        return f
    def sum1(p):
        def f():
            own,rm,rp=bufs[p][0],bufs[p][3],bufs[p][4]
            m=M[p]
            ld[p][2].wait()
            for cp in R[p,"b"]: cp.wait_recv()
            def body(i,_):
                j=(i//m,i%m)
                own[j]=(f32(own[j])+(f32(rm[j])+f32(rp[j]))).astype(jnp.bfloat16)
                return 0
            lax.fori_loop(0,4*m,body,0)
            for cp in R[p,"c"]: cp.start()
            for cp in R[p,"d"][:2]: cp.start()
        return f
    def relay2(p):
        def f():
            own,rl2p,rl2m=bufs[p][0],bufs[p][5],bufs[p][6]
            hm=M[p]//2; k=me[AX[p][1]]
            R[p,"c"][0].wait_recv()
            addin(own,rl2p,hm,lambda i:((k+1)%4,i),lambda i:i)
            R[p,"d"][2].start()
            R[p,"c"][1].wait_recv()
            addin(own,rl2m,hm,lambda i:((k+3)%4,hm+i),lambda i:i)
            R[p,"d"][3].start()
        return f
    def sum2(p):
        def f():
            own,rm2,rp2,out2=bufs[p][0],bufs[p][7],bufs[p][8],bufs[p][9]
            k=me[AX[p][1]]
            for cp in R[p,"d"]: cp.wait_recv()
            def body(i,_):
                out2[i]=(f32(own[k,i])+(f32(rm2[i])+f32(rp2[i]))).astype(jnp.bfloat16)
                return 0
            lax.fori_loop(0,M[p],body,0)
            for cp in R[p,"e"]: cp.start()
        return f
    def last(p):
        def f():
            out2,r3,r4=bufs[p][9:12]
            a,b=cut[p]
            for cp in R[p,"e"]: cp.wait_recv()
            k=me[AX[p][2]] if p==0 else xl
            s=(f32(out2[k])+f32(r3[1]))+(f32(r3[0])+f32(r3[2]))
            if p==0:
                r4[xh]=s.astype(jnp.bfloat16)
                R[p,"f"][0].start()
            else:
                out[:,pl.ds(a,b-a)]=s
        return f
    def end():
        a,b=cut[0]; h=(b-a)//2; r4=bufs[0][11]
        R[0,"f"][0].wait_recv()
        for j in range(2): out[:,pl.ds(a+j*h,h)]=f32(r4[j])
        for cp in allc: cp.wait_send()
    return [[first]]+[[f(p) for p in P3] for f in (relay,reload,sum1,relay2,sum2,last)]+[[end]]
STAGES=8
def staggered(chains,by):
    return [[f for i,ch in enumerate(chains) if 0<=tick-by*i<STAGES for f in ch[tick-by*i]] for tick in range(STAGES+by*(len(chains)-1))]
def scatter_bufs(nm,r,w):
    scr=[]
    for p,(a,b) in enumerate(rcuts(nm,w)):
        m=4 if p==0 else 2; v=(b-a)//2 if p==0 else b-a; hm=m//2
        B=lambda *s:pltpu.VMEM(s+(r,v),jnp.bfloat16)
        scr+=[B(4,m),B(2,m),B(2,m),B(4,m),B(4,m),B(hm),B(hm),B(m),B(m),B(m),B(3),B(2) if p==0 else pltpu.VMEM((8,128),jnp.bfloat16)]
    return scr
def scatter_sems():
    return [pltpu.SemaphoreType.DMA((46,)),pltpu.SemaphoreType.DMA((46,)),pltpu.SemaphoreType.DMA((9,))]
def by_part(refs):
    return [refs[12*p:12*p+12] for p in range(3)]
def narrowed(bufs,nm,w):
    out=[]
    for p,(a,b) in enumerate(rcuts(nm,w)):
        v=(b-a)//2 if p==0 else b-a
        out.append([ref if ref.shape[-1]==v or ref.shape==(8,128) else ref.at[(slice(None),)*(len(ref.shape)-1)+(pl.ds(0,v),)] for ref in bufs[p]])
    return out
def vector_steps(vbuf,sems):
    z,y,x,c=coords(); me=(x,y,z)
    ss,rs=sems
    R=[[pltpu.make_async_remote_copy(src_ref=vbuf[st].at[me[st]],dst_ref=vbuf[st].at[me[st]],send_sem=ss.at[3*st+k-1],recv_sem=rs.at[3*st+k-1],device_id=peer_of("xyz"[st],k),device_id_type=MESH) for k in (1,2,3)] for st in range(3)]
    def go(st,v):
        vbuf[st][pl.ds(me[st],1)]=v[None]
        for cp in R[st]: cp.start()
    def total(st):
        for cp in R[st]: cp.wait_recv()
        b=vbuf[st]
        return (b[0]+b[1])+(b[2]+b[3])
    def end():
        for l in R:
            for cp in l: cp.wait_send()
    return go,total,end


TT=256; KH=896; HD=64; LEN=4096; NEG=-1e30; ROWS=32
FQ,FK,BQ,BK=1024,1024,512,512
def dot(a,b): return lax.dot_general(a,b,(((1,),(0,)),((),())),preferred_element_type=jnp.float32)
def dot_nt(a,b): return lax.dot_general(a,b,(((1,),(1,)),((),())),preferred_element_type=jnp.float32)
def group_greet(d,r,c,across):
    bar=pltpu.get_barrier_semaphore()
    for rr in across: pl.semaphore_signal(bar,inc=1,device_id=(1-d,rr,c),device_id_type=MESH)
    def body(i,_):
        @pl.when(i!=r*2+c)
        def _():
            pl.semaphore_signal(bar,inc=1,device_id=(d,i//2,i%2),device_id_type=MESH)
        return 0
    lax.fori_loop(0,2*ROWS,body,0)
def group_wait(across):
    pl.semaphore_wait(pltpu.get_barrier_semaphore(),2*ROWS-1+across)
def push(src,dst,send_sem,recv_sem,same,target):
    @pl.when(same)
    def _():
        pltpu.make_async_copy(src,dst,recv_sem).start()
    @pl.when(jnp.logical_not(same))
    def _():
        pltpu.make_async_remote_copy(src_ref=src,dst_ref=dst,send_sem=send_sem,recv_sem=recv_sem,device_id=target,device_id_type=MESH).start()
def pushed(src,dst,send_sem,recv_sem,same,target):
    @pl.when(jnp.logical_not(same))
    def _():
        pltpu.make_async_remote_copy(src_ref=src,dst_ref=dst,send_sem=send_sem,recv_sem=recv_sem,device_id=target,device_id_type=MESH).wait_send()
def arrived(ref,sem):
    pltpu.make_async_copy(ref,ref,sem).wait()
FWD_AT=((1,2),(2,3))
BWD_AT=((0,3),(1,4),(2,5),(3,7),(4,8),(5,9))
def attn_fwd_kernel(names,widths,*refs):
    n=len(names)
    qkv_in,start=refs[:2]
    o_recv,qkv_out,oT,lse=refs[2+n:6+n]
    qkv,knt,obf,s_in,s_out,r_in,r_out,l_sem=refs[6+2*n:14+2*n]
    steps=gather_chains(names,widths,refs[2:2+n],refs[6+n:6+2*n],refs[14+2*n:])
    d=lax.axis_index("dev"); r=lax.axis_index("row"); c=lax.axis_index("col")
    group_greet(d,r,c,[r+1-2*(r%2)])
    group_wait(1)
    lanes=pl.ds(pl.multiple_of(r*128,128),128)
    def full(fn):
        def body(k,_):
            i=(r+k)%24
            fn(qkv_in.at[i%2,:,i//2+c],qkv.at[:,:,lanes],s_in.at[i],r_in,i==r,(d,i,c))
            return 0
        lax.fori_loop(0,24,body,0)
    def halves(fn):
        rows=pl.ds(pl.multiple_of(32*c,32),32)
        for s in range(2):
            fn(qkv_in.at[s,:,12*(1-c),rows],qkv.at[:,rows,lanes],s_in.at[24+s],r_in,(r==24+s)&(c==0),(d,24+s,0))
    full(push); halves(push)
    steps[0]()
    item=(r<24)|((c==0)&(r<26))
    head=r//2+13*c; seq=r%2
    def outs(qi,fn):
        def body(i,_):
            rr=qi*(FQ//128)+(r+i//2)%(FQ//128); cc=i%2
            fn(obf.at[:,pl.ds(pl.multiple_of(rr*128,128),128)],o_recv.at[seq,head],s_out.at[rr*2+cc],r_out,(rr==r)&(cc==c),(d,rr,cc))
            return 0
        lax.fori_loop(0,FQ//64,body,0)
    save=pltpu.make_async_copy(qkv,qkv_out,l_sem)
    @pl.when(item)
    def _():
        arrived(qkv,r_in)
        save.start()
        for a in range(LEN//512):
            sl=pl.ds(a*512,512)
            knt[sl,:]=qkv[1,:,sl].T
    steps[1]()
    def qloop(qi,_):
        @pl.when(item)
        def _():
            iota=lax.broadcasted_iota(jnp.int32,(FK,FQ),0)
            iotl=lax.broadcasted_iota(jnp.int32,(FK,FQ),1)
            qs=pl.ds(pl.multiple_of(qi*FQ,FQ),FQ)
            q=qkv[0,:,qs]*jnp.bfloat16(0.125)
            st=start[:,qs]
            def step(kj,carry,diag):
                m,l,acc=carry
                ks=pl.ds(pl.multiple_of(kj*FK,FK),FK)
                s=dot(knt[ks,:],q)
                ok=iota>=(st-kj*FK)
                if diag: ok=ok&(iota<=iotl)
                s=jnp.where(ok,s,NEG)
                mn=jnp.maximum(m,jnp.max(s,axis=0,keepdims=True))
                p=jnp.exp(s-mn)
                al=jnp.exp(m-mn)
                l=l*al+jnp.sum(p,axis=0,keepdims=True)
                acc=acc*al+dot(qkv[2,:,ks],p.astype(jnp.bfloat16))
                return mn,l,acc
            carry=(jnp.full((1,FQ),NEG,jnp.float32),jnp.zeros((1,FQ),jnp.float32),jnp.zeros((HD,FQ),jnp.float32))
            carry=lax.fori_loop(0,qi,lambda kj,cr:step(kj,cr,False),carry)
            m,l,acc=step(qi,carry,True)
            o=acc/l
            oT[:,qs]=o
            lse[:,qs]=m+jnp.log(l)
            obf[:,qs]=o.astype(jnp.bfloat16)
            outs(qi,push)
        for at,f in FWD_AT:
            pl.when(qi==at)(steps[f])
        return 0
    lax.fori_loop(0,LEN//FQ,qloop,0)
    for f in range(FWD_AT[-1][1]+1,6): steps[f]()
    @pl.when(item)
    def _():
        save.wait()
        for qi in range(LEN//FQ): outs(qi,pushed)
    full(pushed); halves(pushed)
    arrived(o_recv,r_out)
BWD_AT=((0,1),(1,2),(3,3),(5,4),(7,5))
KQ=2432
def back_kernel(names,widths,*refs):
    it=iter(refs)
    take=lambda n:[next(it) for _ in range(n)]
    n=len(names)
    do_in,qkv,oT,start,lse,h1t,normt,vec_in,wq=take(9)
    parts=take(n)
    part_q,dh1t,sum_q,vec_out=take(4)
    sums=take(n)
    doT,knt,vnt,dqa,delta,dout,dq,stage,wblk,dh_send,dh_recv=take(11)
    vbuf=take(3); vtmp=next(it)
    s_in,s_out,r_in,r_out,q_sem,w_sem,x_sem,free=take(8)
    v_sems=take(2)
    bufs=[by_part(take(36)) for _ in range(n)]
    chains=[scatter_steps(names[t],widths[t],parts[t],sums[t],bufs[t],take(3)) for t in range(n)]
    chain_q=scatter_steps("q",KQ,part_q,sum_q,narrowed(bufs[0],"q",KQ),take(3))
    ticks=staggered(chains,1)
    v_go,v_total,v_end=vector_steps(vbuf,v_sems)
    d=lax.axis_index("dev"); r=lax.axis_index("row"); c=lax.axis_index("col")
    item=(r<24)|((c==0)&(r<26))
    group_greet(d,r,c,[r+1-2*(r%2),r])
    @pl.when(item)
    def _():
        for a in range(LEN//512):
            sl=pl.ds(a*512,512)
            knt[sl,:]=qkv[1,:,sl].T
            vnt[sl,:]=qkv[2,:,sl].T
        dqa[...]=jnp.zeros_like(dqa)
    stage[...]=jnp.zeros_like(stage)
    group_wait(2)
    lanes=pl.ds(pl.multiple_of(r*128,128),128)
    def full(fn):
        def body(k,_):
            i=(r+k)%24
            fn(do_in.at[i%2,i//2+c],doT.at[:,lanes],s_in.at[i],r_in,i==r,(d,i,c))
            return 0
        lax.fori_loop(0,24,body,0)
    def halves(fn):
        rows=pl.ds(pl.multiple_of(32*c,32),32)
        for s in range(2):
            fn(do_in.at[s,12*(1-c),rows],doT.at[rows,lanes],s_in.at[24+s],r_in,(r==24+s)&(c==0),(d,24+s,0))
    full(push); halves(push)
    def tick(k):
        for f in ticks[k]: f()
    tick(0)
    def outs(fn):
        seq=pl.ds(pl.multiple_of((r%2)*128,128),128)
        @pl.when(r<24)
        def _():
            def body(k,_):
                i=(r+k)%ROWS
                fn(dout.at[:,:,pl.ds(pl.multiple_of(i*128,128),128)],dq.at[:,pl.ds(pl.multiple_of(64*(r//2)+32*c,32),64),seq],s_out.at[i],r_out,i==r,(d,i,c))
                return 0
            lax.fori_loop(0,ROWS,body,0)
        @pl.when(r>=24)
        def _():
            def body(k,_):
                rr=(r+k//2)%ROWS; cc=k%2
                fn(dout.at[:,pl.ds(pl.multiple_of(32*cc,32),32),pl.ds(pl.multiple_of(rr*128,128),128)],dq.at[:,pl.ds(pl.multiple_of(768*(1-cc),32),32),seq],s_out.at[2*rr+cc],r_out,(rr==r)&(cc==c),(d,rr,cc))
                return 0
            lax.fori_loop(0,2*ROWS,body,0)
    @pl.when(item)
    def _():
        arrived(doT,r_in)
        for a in range(LEN//512):
            sl=pl.ds(a*512,512)
            delta[:,sl]=jnp.sum(oT[:,sl]*doT[:,sl].astype(jnp.float32),axis=0,keepdims=True)
    def kloop(kj,_):
        @pl.when(item)
        def _():
            iota=lax.broadcasted_iota(jnp.int32,(BK,BQ),0)
            iotl=lax.broadcasted_iota(jnp.int32,(BK,BQ),1)
            ks=pl.ds(pl.multiple_of(kj*BK,BK),BK)
            kn=knt[ks,:]; vn=vnt[ks,:]; kT=qkv[1,:,ks]
            def step(qi,carry,diag):
                dk,dv=carry
                qs=pl.ds(pl.multiple_of(qi*BQ,BQ),BQ)
                q=qkv[0,:,qs]*jnp.bfloat16(0.125)
                do=doT[:,qs]
                s=dot(kn,q)
                ok=iota>=(start[:,qs]-kj*BK)
                if diag: ok=ok&(iota<=iotl)
                p=jnp.exp(jnp.where(ok,s,NEG)-lse[:,qs])
                dp=dot(vn,do)
                ds=(p*(dp-delta[:,qs])).astype(jnp.bfloat16)
                dv=dv+dot_nt(do,p.astype(jnp.bfloat16))
                dk=dk+dot_nt(q,ds)
                dqa[:,qs]+=dot(kT,ds)
                return dk,dv
            z=jnp.zeros((HD,BK),jnp.float32)
            carry=step(kj,(z,z),True)
            dk,dv=lax.fori_loop(kj+1,LEN//BQ,lambda qi,cr:step(qi,cr,False),carry)
            dout[1,:,ks]=dk.astype(jnp.bfloat16)
            dout[2,:,ks]=dv.astype(jnp.bfloat16)
        for step,k in BWD_AT:
            pl.when(kj==step)(functools.partial(tick,k))
        return 0
    lax.fori_loop(0,LEN//BK,kloop,0)
    @pl.when(item)
    def _():
        for a in range(LEN//512):
            sl=pl.ds(a*512,512)
            dout[0,:,sl]=(dqa[:,sl]*0.125).astype(jnp.bfloat16)
        outs(push)
    for k in range(BWD_AT[-1][1]+1,STAGES): tick(k)
    for ax,k in RPEERS: pl.semaphore_signal(free,inc=1,device_id=peer_of(ax,k),device_id_type=MESH)
    arrived(dq,r_out)
    grads=dq[...].reshape(2400,TT)
    prev={}
    for b in range(8):
        slot=b%2
        if b>=2: prev[slot].wait()
        stage[slot,:,:,:,pl.ds(0,2400)]=dot_nt(h1t[pl.ds(224*b,224),:],grads).reshape(2,2,56,2400).astype(bf)
        prev[slot]=pltpu.make_async_copy(stage.at[slot],part_q.at[b//2,pl.ds(2*(b%2),2)],q_sem.at[slot])
        prev[slot].start()
    partner=(d,r,1-c)
    half=lambda base,k:wq.at[pl.ds(pl.multiple_of(base*KH+128*k,128),128)]
    blocks=[half(1-c,k) for k in range(7)]+[half(c,k) for k in range(7)]
    loads=[pltpu.make_async_copy(blocks[k],wblk.at[k%2],w_sem.at[k%2]) for k in range(14)]
    loads[0].start(); loads[1].start()
    for cp in prev.values(): cp.wait()
    pl.semaphore_wait(free,len(RPEERS))
    def go_q(k):
        for f in chain_q[k]: f()
    go_q(0)
    swap=pltpu.make_async_remote_copy(src_ref=dh_send,dst_ref=dh_recv,send_sem=x_sem.at[0],recv_sem=x_sem.at[1],device_id=partner,device_id_type=MESH)
    for k in range(14):
        loads[k].wait()
        v=dot(wblk[k%2],grads)
        if k<7: dh_send[pl.ds(128*k,128),:]=v.astype(bf)
        else: dh1t[pl.ds(128*(k-7),128),:]=v
        if k<12: loads[k+2].start()
        if k==6: swap.start()
    go_q(1)
    for k in range(STAGES,len(ticks)): tick(k)
    swap.wait()
    dh1t[...]=dh1t[...]+dh_recv[...].astype(jnp.float32)
    def token_sums(v,precision=None):
        return lax.dot_general(jnp.ones((8,TT),v.dtype),v,(((1,),(1,)),((),())),precision=precision,preferred_element_type=jnp.float32)[:1]
    gain=token_sums(dh1t[...]*normt[...],lax.Precision.HIGHEST)
    bias=token_sums(dh1t[...],lax.Precision.HIGHEST)
    both=token_sums(grads)
    both=jnp.concatenate((both,jnp.zeros((1,32),jnp.float32)),axis=1)
    vtmp[pl.ds(0,40),:]=jnp.zeros((40,128),jnp.float32)
    vtmp[pl.ds(40,vec_in.shape[0]),:]=vec_in[...]
    for at,row,cnt in ((0,gain,7),(7,bias,7),(14,both,19)):
        for k in range(cnt): vtmp[pl.ds(at+k,1),:]=row[:,128*k:128*k+128]
    v_go(0,vtmp[...])
    go_q(2); go_q(3)
    v_go(1,v_total(0))
    go_q(4)
    v_go(2,v_total(1))
    go_q(5); go_q(6)
    vec_out[...]=v_total(2)
    go_q(7)
    v_end()
    pl.when(item)(lambda:outs(pushed))
    full(pushed); halves(pushed)
VM=pl.BlockSpec(memory_space=pltpu.VMEM); ANY=pl.BlockSpec(memory_space=pl.ANY)
bf=jnp.bfloat16
def attend(qkv,start,names,arrs,cid=1):
    S=jax.ShapeDtypeStruct; n=len(names)
    out=pl.pallas_call(functools.partial(attn_fwd_kernel,names,[a.shape[1] for a in arrs]),
      out_shape=(S((2,25,HD,128),bf),S((3,HD,LEN),bf),S((HD,LEN),jnp.float32),S((1,LEN),jnp.float32))+gather_shapes(arrs),
      in_specs=[VM,VM]+[ANY]*n,out_specs=(ANY,ANY,VM,VM)+(ANY,)*n,
      scratch_shapes=[pltpu.VMEM((3,HD,LEN),bf),pltpu.VMEM((LEN,HD),bf),pltpu.VMEM((HD,LEN),bf),
        pltpu.SemaphoreType.DMA((26,)),pltpu.SemaphoreType.DMA((64,)),pltpu.SemaphoreType.DMA,pltpu.SemaphoreType.DMA,pltpu.SemaphoreType.DMA]+gather_sems(n),
      compiler_params=pltpu.CompilerParams(collective_id=cid,has_side_effects=True,vmem_limit_bytes=50<<20))(qkv,start,*arrs)
    return out[0],out[1:4],out[4:]
def attend_back(do,kept,start,h1t,normt,vec,wq,names,parts,cid=2):
    S=jax.ShapeDtypeStruct; n=len(names); f=jnp.float32; V=pltpu.VMEM; DM=pltpu.SemaphoreType.DMA
    qkv,oT,lse=kept
    rows=40+vec.shape[0]
    out=pl.pallas_call(functools.partial(back_kernel,names,[a.shape[4] for a in parts]),
      out_shape=(S((4,4,2,56,KQ),bf),S((KH,TT),f),S((56,KQ),f),S((rows,128),f))+tuple(S(a.shape[3:],f) for a in parts),
      in_specs=[VM]*8+[ANY]*(1+n),out_specs=(ANY,VM,VM,VM)+(VM,)*n,
      scratch_shapes=[V((HD,LEN),bf),V((LEN,HD),bf),V((LEN,HD),bf),V((HD,LEN),f),V((1,LEN),f),V((3,HD,LEN),bf),
        V((3,800,TT),bf),V((2,2,2,56,KQ),bf),V((2,128,2400),bf),V((KH,TT),bf),V((KH,TT),bf)]+[V((4,rows,128),f)]*3+[V((rows,128),f)]+
        [DM((26,)),DM((64,)),DM,DM,DM((2,)),DM((2,)),DM((2,)),pltpu.SemaphoreType.REGULAR,DM((9,)),DM((9,))]+
        sum([scatter_bufs(nm,*a.shape[3:]) for nm,a in zip(names,parts)],[])+scatter_sems()*(n+1),
      compiler_params=pltpu.CompilerParams(collective_id=cid,has_side_effects=True,vmem_limit_bytes=VMEM_BACK))(do,qkv,oT,start,lse,h1t,normt,vec,wq,*parts)
    return out[1],out[2],out[3],out[4:]
VMEM_BACK=62<<20


WC=800; FH=3200; TF=640
GC=0.7978845608028654
def dot_tn(a,b): return lax.dot_general(a,b,(((0,),(0,)),((),())),preferred_element_type=jnp.float32)
def mlp_kernel(h2,we,eb,wc,mid,cb,g,result,part_c,part_e,dh2,dsum,
        wev,wcv,pre,a_own,a_recv,da_send,da_recv,dpre,dh_send,dh_recv,stage_e,stage_c,w_sem,s_sem,r_sem,e_sem,c_sem):
    c=lax.axis_index("col"); other=1-c
    partner=(lax.axis_index("dev"),lax.axis_index("row"),other)
    loads=[pltpu.make_async_copy(wc,wcv,w_sem.at[0]),pltpu.make_async_copy(we,wev,w_sem.at[1])]
    for cp in loads: cp.start()
    bar=pltpu.get_barrier_semaphore()
    pl.semaphore_signal(bar,inc=1,device_id=partner,device_id_type=MESH)
    pl.semaphore_wait(bar,1)
    def swap(i,s,d):
        return pltpu.make_async_remote_copy(src_ref=s,dst_ref=d,send_sem=s_sem.at[i],recv_sem=r_sem.at[i],device_id=partner,device_id_type=MESH)
    x_da,x_a,x_dh=swap(0,da_send,da_recv),swap(1,a_own,a_recv),swap(2,dh_send,dh_recv)
    lanes=lambda k,n:pl.ds(pl.multiple_of(k*n,128),n)
    rows=lambda base,k,n:pl.ds(pl.multiple_of(base+k*n,128),n)
    f32=lambda v:v.astype(jnp.float32)
    NT=FH//TF
    def loop(n,f):
        def body(k,_):
            f(k)
            return 0
        lax.fori_loop(0,n,body,0)
    loads[0].wait()
    def f(k): da_send[:,lanes(k,TF)]=dot_nt(g[...],wcv[rows(other*FH,k,TF),:]).astype(bf)
    loop(NT,f)
    x_da.start()
    loads[1].wait()
    def f(k):
        p=dot(h2[...],wev[:,lanes(k,TF)])+eb[:,lanes(k,TF)]
        pre[:,lanes(k,TF)]=p
        a_own[:,lanes(k,TF)]=(p*(0.5*(1.0+jnp.tanh(GC*(p+0.044715*(p*p*p)))))).astype(bf)
    loop(NT,f)
    x_a.start()
    x_da.wait_recv()
    def f(k):
        sl=lanes(k,TF)
        d=dot_nt(g[...],wcv[rows(c*FH,k,TF),:])+f32(da_recv[:,sl])
        p=pre[:,sl]
        t=jnp.tanh(GC*(p+0.044715*(p*p*p)))
        slope=0.5*(1.0+t)+p*(0.5*(1.0-t*t)*(GC*(1.0+(3*0.044715)*(p*p))))
        dp=(d*slope).astype(bf)
        dpre[:,sl]=dp
        dsum[:,sl]=jnp.sum(f32(dp),axis=0,keepdims=True)
    loop(NT,f)
    def f(k): dh_send[:,lanes(k,128)]=dot_nt(dpre[...],wev[rows(other*KH,k,128),:]).astype(bf)
    loop(KH//128,f)
    x_dh.start()
    def f(k): dh2[:,lanes(k,128)]=dot_nt(dpre[...],wev[rows(c*KH,k,128),:])
    loop(KH//128,f)
    def emit(i,stage,sem,dst,value):
        slot=i%2
        cp=pltpu.make_async_copy(stage.at[slot],dst,sem.at[slot])
        if i>=2: prev[slot].wait()
        stage[slot]=value
        cp.start(); prev[slot]=cp
    prev={}
    for j in range(KP//256):
        emit(j,stage_e,e_sem,part_e.at[pl.ds(256*j,256)],dot_tn(h2[:,256*j:256*j+256],dpre[...]).astype(bf))
    for cp in prev.values(): cp.wait()
    x_a.wait_recv()
    br=dot(a_own[...],wcv[rows(c*FH,0,FH),:])+dot(a_recv[...],wcv[rows(other*FH,0,FH),:])
    result[...]=(mid[...]+(br+cb[...])).astype(bf)
    prev={}
    for i in range(2*NT):
        a,b,k=(a_own,c,i) if i<NT else (a_recv,other,i-NT)
        emit(i,stage_c,c_sem,part_c.at[rows(b*FH,k,TF)],dot_tn(a[:,k*TF:k*TF+TF],g[...]).astype(bf))
    x_dh.wait_recv()
    dh2[...]=dh2[...]+f32(dh_recv[...])
    for cp in prev.values(): cp.wait()
    for cp in (x_da,x_a,x_dh): cp.wait_send()
def mlp(h2,we,eb,wc,mid,cb,g,cid=4):
    S=jax.ShapeDtypeStruct; f=jnp.float32; V=pltpu.VMEM
    return pl.pallas_call(mlp_kernel,
      out_shape=(S((TT,WC),bf),S((6400,WC),bf),S((KP,FH),bf),S((TT,KH),f),S((1,FH),f)),
      in_specs=[VM,ANY,VM,ANY,VM,VM,VM],out_specs=(VM,ANY,ANY,VM,VM),
      scratch_shapes=[V((KP,FH),bf),V((6400,WC),bf),V((TT,FH),f)]+[V((TT,FH),bf)]*5+[V((TT,KH),bf)]*2+[V((2,256,FH),bf),V((2,TF,WC),bf)]+[pltpu.SemaphoreType.DMA((n,)) for n in (2,3,3,2,2)],
      compiler_params=pltpu.CompilerParams(collective_id=cid,has_side_effects=True,vmem_limit_bytes=58<<20))(h2,we,eb,wc,mid,cb,g)
def pair_dot_kernel(v,w,out,send,recv,s_sem,r_sem):
    c=lax.axis_index("col"); other=1-c
    partner=(lax.axis_index("dev"),lax.axis_index("row"),other)
    bar=pltpu.get_barrier_semaphore()
    pl.semaphore_signal(bar,inc=1,device_id=partner,device_id_type=MESH)
    for k in range(KH//128):
        send[:,128*k:128*k+128]=dot_nt(v[...],w[pl.ds(pl.multiple_of(other*KH+128*k,128),128),:]).astype(bf)
    pl.semaphore_wait(bar,1)
    cp=pltpu.make_async_remote_copy(src_ref=send,dst_ref=recv,send_sem=s_sem,recv_sem=r_sem,device_id=partner,device_id_type=MESH)
    cp.start()
    for k in range(KH//128):
        out[:,128*k:128*k+128]=dot_nt(v[...],w[pl.ds(pl.multiple_of(c*KH+128*k,128),128),:])
    cp.wait()
    out[...]=out[...]+recv[...].astype(jnp.float32)
def pair_dot(v,w,cid):
    return pl.pallas_call(pair_dot_kernel,out_shape=jax.ShapeDtypeStruct((TT,KH),jnp.float32),in_specs=[VM,VM],out_specs=VM,
      scratch_shapes=[pltpu.VMEM((TT,KH),bf)]*2+[pltpu.SemaphoreType.DMA]*2,
      compiler_params=pltpu.CompilerParams(collective_id=cid,has_side_effects=True,vmem_limit_bytes=40<<20))(v,w)
def outer_kernel(a,b,o):
    o[...]=dot_tn(a[...],b[...]).astype(bf)
def outer(a,b):
    m=a.shape[1]; n=b.shape[1]
    return pl.pallas_call(outer_kernel,out_shape=jax.ShapeDtypeStruct((m,n),bf),grid=(m//256,),
      in_specs=[pl.BlockSpec((TT,256),lambda i:(0,i)),pl.BlockSpec((TT,n),lambda i:(0,0))],out_specs=pl.BlockSpec((256,n),lambda i:(i,0)),
      compiler_params=pltpu.CompilerParams(vmem_limit_bytes=32<<20))(a,b)


def width_sums(first_sum, second_sum):
    return lax.psum((first_sum, second_sum), "col")


def full_rows(values):
    return lax.all_gather(values, "col", axis=1, tiled=True)


def norm_forward(values, norm_gain, norm_bias):
    totals = width_sums(jnp.sum(values, axis=1), jnp.sum(values * values, axis=1))
    averages = totals[0] / D
    reciprocal = lax.rsqrt(totals[1] / D - averages * averages + 1e-05)
    normed = (values - averages[:, None]) * reciprocal[:, None]
    return (normed, reciprocal, normed * norm_gain + norm_bias)


def norm_backward(incoming, normed, reciprocal, norm_gain):
    scaled = incoming * norm_gain
    totals = width_sums(jnp.sum(scaled, axis=1), jnp.sum(scaled * normed, axis=1))
    return reciprocal[:, None] * (
        scaled - totals[0][:, None] / D - normed * (totals[1][:, None] / D)
    )


def pad_rows(block):
    return jnp.pad(block, ((0, 6), (0, 0)))


def pad_features(values):
    n = values.shape[0]
    return jnp.pad(values.reshape(n, 32, 50), ((0, 0), (0, 0), (0, 6))).reshape(n, KP)


def unpad_features(values):
    n = values.shape[0]
    return values.reshape(n, 16, 56)[:, :, :50].reshape(n, 800)


def per_device(
    tokens,
    segments,
    first_gain,
    first_bias,
    attention_in,
    attention_bias,
    attention_out,
    output_bias,
    second_gain,
    second_bias,
    expand_weight,
    expand_bias,
    contract_weight,
    contract_bias,
    cotangent,
):
    seqs, block_len, width = tokens.shape
    row_total = seqs * block_len
    row = lax.axis_index("row")
    col = lax.axis_index("col")
    weight_qkv, weight_expand = gather(
        "qe", (pad_rows(attention_in.reshape(50, 3 * width)), pad_rows(expand_weight)), 0
    )
    weight_qkv = weight_qkv.reshape(KP, 3 * width)

    own_seg = lax.dynamic_index_in_dim(segments, row % 2, 0, keepdims=True)
    positions = jnp.arange(LEN, dtype=jnp.int32)[None]
    before = jnp.concatenate((own_seg[:, :1], own_seg[:, :-1]), axis=1)
    start = lax.cummax(jnp.where(own_seg != before, positions, 0), axis=1)

    float_tokens = tokens.astype(jnp.float32).reshape(row_total, width)
    normed_one, recip_one, hidden_one = norm_forward(float_tokens, first_gain, first_bias)
    rows_one = pad_features(full_rows(hidden_one.astype(jnp.bfloat16)))
    bias_three = jnp.concatenate(
        (attention_bias[0], jnp.zeros_like(attention_bias[0]), attention_bias[1])
    )
    projected = jnp.einsum(
        "dm,snd->smn",
        weight_qkv,
        rows_one.reshape(seqs, block_len, KP),
        preferred_element_type=jnp.float32,
    )
    projected = (projected + bias_three[None, :, None]).astype(jnp.bfloat16)
    projected = projected.reshape(seqs, 3, width, block_len)

    def head_slots(values):
        lead = [(0, 0)] * (values.ndim - 2)
        slots = jnp.where(
            col == 0,
            jnp.pad(values, lead + [(0, 32), (0, 0)]),
            jnp.pad(values, lead + [(32, 0), (0, 0)]),
        )
        return slots.reshape(values.shape[:-2] + (13, HD, block_len))

    attended, kept, gathered = attend(
        head_slots(projected),
        start,
        "co",
        (contract_weight, pad_rows(attention_out)),
        1,
    )
    weight_out = gathered[1].reshape(KP, width)
    weight_expand = weight_expand.reshape(KP, 4 * width)
    weight_contract = gathered[0].reshape(4 * D, width)
    rows_attn = jnp.pad(
        attended.reshape(seqs, 32, 50, block_len), ((0, 0), (0, 0), (0, 6), (0, 0))
    ).reshape(seqs, KP, block_len)
    middle = float_tokens + (
        jnp.einsum(
            "sfn,fd->snd", rows_attn, weight_out, preferred_element_type=jnp.float32
        ).reshape(row_total, width)
        + output_bias
    )
    normed_two, recip_two, hidden_two = norm_forward(middle, second_gain, second_bias)
    rows_two = pad_features(full_rows(hidden_two.astype(jnp.bfloat16)))
    grad_low = cotangent.reshape(row_total, width)
    grad_float = grad_low.astype(jnp.float32)
    result, part_contract, part_expand, grad_two, expand_sums = mlp(
        rows_two, weight_expand, expand_bias[None], weight_contract, middle, contract_bias[None], grad_low, 4
    )
    result = result.reshape(tokens.shape)
    grad_two = unpad_features(grad_two)
    grad_middle = grad_float + norm_backward(grad_two, normed_two, recip_two, second_gain)
    grad_attn = grad_middle.astype(jnp.bfloat16)
    part_out = outer(jnp.transpose(rows_attn, (0, 2, 1)).reshape(row_total, KP), grad_attn)
    grad_mixed = unpad_features(pair_dot(grad_attn, weight_out, 5).astype(jnp.bfloat16))
    grad_mixed = jnp.transpose(grad_mixed.reshape(seqs, block_len, width), (0, 2, 1))
    sums_rest = (
        jnp.sum(grad_attn.astype(jnp.float32), axis=0),
        jnp.sum(grad_two * normed_two, axis=0),
        jnp.sum(grad_two, axis=0),
        jnp.sum(grad_float, axis=0),
        expand_sums[0],
    )
    grad_one, sum_qkv, vector, (sum_expand, sum_contract, sum_out) = attend_back(
        head_slots(grad_mixed),
        kept,
        start,
        rows_one.T,
        jnp.pad(normed_one.reshape(row_total, 16, 50), ((0, 0), (0, 0), (0, 6))).reshape(row_total, KH).T,
        jnp.concatenate(sums_rest).reshape(50, 128),
        weight_qkv,
        "eco",
        (
            part_expand.reshape(4, 4, 2, 56, 4 * width),
            part_contract.reshape(4, 4, 2, 200, width),
            part_out.reshape(4, 4, 2, 56, width),
        ),
        2,
    )
    grad_one = unpad_features(grad_one.T)
    grad_input = grad_middle + norm_backward(grad_one, normed_one, recip_one, first_gain)
    gradient_tokens = grad_input.astype(jnp.bfloat16).reshape(tokens.shape)
    first = unpad_features(vector[:14].reshape(2, KH))
    qkv_sums = vector[14:33].reshape(-1)[: 3 * width].reshape(3, width)
    rest = vector[40:].reshape(-1)
    sums = [rest[width * k : width * (k + 1)] for k in range(4)] + [rest[4 * width :]]
    return (
        result,
        gradient_tokens,
        first[0],
        first[1],
        sum_qkv[:50, : 3 * width].reshape(50, 3, width),
        jnp.stack((qkv_sums[0], qkv_sums[2])),
        sum_out[:50],
        sums[0],
        sums[1],
        sums[2],
        sum_expand[:50],
        sums[4],
        sum_contract,
        sums[3],
    )


def solution(mesh):
    return jax.shard_map(
        per_device,
        mesh=mesh,
        in_specs=(
            P("dev", "row", "col"),
            P("dev", None),
            P("col"),
            P("col"),
            P("row", None, "col"),
            P(None, "col"),
            P("row", "col"),
            P("col"),
            P("col"),
            P("col"),
            P("row", "col"),
            P("col"),
            P("row", "col"),
            P("col"),
            P("dev", "row", "col"),
        ),
        out_specs=(
            P("dev", "row", "col"),
            P("dev", "row", "col"),
            P("col"),
            P("col"),
            P("row", None, "col"),
            P(None, "col"),
            P("row", "col"),
            P("col"),
            P("col"),
            P("col"),
            P("row", "col"),
            P("col"),
            P("row", "col"),
            P("col"),
        ),
        check_vma=False,
    )
```

```python
import functools

import jax
import jax.numpy as jnp
from jax import lax
from jax.experimental import pallas as pl
from jax.experimental.pallas import tpu as pltpu
from jax.sharding import PartitionSpec as P

MESH = pl.DeviceIdType.MESH
D = 1600
KP = 1792


def coords():
    d=lax.axis_index("dev"); r=lax.axis_index("row"); c=lax.axis_index("col")
    return r//8, (r//2)%4, d*2+r%2, c
def place(z,y,x,c):
    return (x//2, (z*4+y)*2+x%2, c)
def peer_of(ax,k):
    z,y,x,c=coords()
    if ax=="z": z=(z+k)%4
    if ax=="y": y=(y+k)%4
    if ax=="x": x=(x+k)%4
    return place(z,y,x,c)
def greet(peers):
    bar=pltpu.get_barrier_semaphore()
    for ax,k in peers: pl.semaphore_signal(bar,inc=1,device_id=peer_of(ax,k),device_id_type=MESH)
    pl.semaphore_wait(bar,len(peers))
SPLIT={"q":(4,4,6,5),"o":(2,1,2,2),"e":(7,4,7,7),"c":(1,2,2,2)}
ORD=("yzx","zyx","yxz","zxy")
GPEERS=[("z",1),("z",3),("z",2),("y",1),("y",3),("y",2),("x",1),("x",3)]
def cuts(name,W):
    out=[];p=0
    for n in SPLIT[name]:
        out.append((p,min(p+n*128,W))); p+=n*128
    assert out[-1][1]==W
    return out
def gather_steps(names,widths,src,dst,ss,rs,ls):
    n=len(names)
    z,y,x,c=coords(); xl=x%2
    cnt=[0]; allc=[]
    FULL=slice(None)
    LO=pl.ds(0,2); HI=pl.ds(2,2)
    def mk(s,d,ax,k):
        i=cnt[0]; cnt[0]+=1
        cp=pltpu.make_async_remote_copy(src_ref=s,dst_ref=d,send_sem=ss.at[i],recv_sem=rs.at[i],device_id=peer_of(ax,k),device_id_type=MESH)
        allc.append(cp); return cp
    cut=[cuts(nm,w) for nm,w in zip(names,widths)]
    def at(t,p,zi,yi,xi):
        a,b=cut[t][p]
        return dst[t].at[zi,yi,xi,:,pl.ds(a,b-a)]
    def wait(l):
        for cp in l: cp.wait_recv()
    def go(l):
        for cp in l: cp.start()
    loc=[pltpu.make_async_copy(src[t],dst[t].at[z,y,xl],ls.at[t]) for t in range(n)]
    st1=[[],[],[],[]]
    for t in range(n):
        for p in range(4):
            a,b=cut[t][p]
            for k in (1,3,2):
                st1[p].append(mk(src[t].at[:,pl.ds(a,b-a)],at(t,p,z,y,xl),ORD[p][0],k))
    def both(p,f):
        return [cp for t in range(n) for cp in f(t,p)]
    def xsend(zi,yi):
        return lambda t,p:[mk(at(t,p,*zi,xl),at(t,p,*zi,xl),"x",1),mk(at(t,p,*yi,xl),at(t,p,*yi,xl),"x",3)]
    def ring_a(ax,zi,yi,xi):
        return lambda t,p:[mk(at(t,p,zi,yi,xi),at(t,p,zi,yi,xi),ax,k) for k in (1,3)]
    def ring_b(ax,xi):
        def f(t,p):
            if ax=="z":
                u=at(t,p,(z+3)%4,LO,xi); v=at(t,p,(z+1)%4,HI,xi)
            else:
                u=at(t,p,LO,(y+3)%4,xi); v=at(t,p,HI,(y+1)%4,xi)
            return [mk(u,u,ax,1),mk(v,v,ax,3)]
        return f
    A2=both(0,ring_a("z",z,FULL,xl)); B2=both(1,ring_a("y",FULL,y,xl))
    C2=both(2,xsend((z,LO),(z,HI))); D2=both(3,xsend((LO,y),(HI,y)))
    A2b=both(0,ring_b("z",xl)); B2b=both(1,ring_b("y",xl))
    C3=both(2,ring_a("z",z,FULL,FULL)); D3=both(3,ring_a("y",FULL,y,FULL))
    A3=both(0,xsend((LO,FULL),(HI,FULL))); B3=both(1,xsend((LO,FULL),(HI,FULL)))
    C3b=both(2,ring_b("z",FULL)); D3b=both(3,ring_b("y",FULL))
    def f0():
        go(loc)
        for p in range(4): go(st1[p])
    def f1():
        wait_loc=[cp.wait() for cp in loc]
        wait(st1[0]); go(A2)
        wait(st1[1]); go(B2)
        wait(st1[2]); go(C2)
        wait(st1[3]); go(D2)
    def f2():
        wait(A2); go(A2b); wait(B2); go(B2b)
        wait(C2); go(C3); wait(D2); go(D3)
    def f3():
        wait(A2b); go(A3); wait(B2b); go(B3)
    def f4():
        wait(C3); go(C3b); wait(D3); go(D3b)
    def f5():
        wait(A3);wait(B3);wait(C3b);wait(D3b)
        for cp in allc: cp.wait_send()
    return [f0,f1,f2,f3,f4,f5]
def gather_sems(n):
    return [pltpu.SemaphoreType.DMA((36,)),pltpu.SemaphoreType.DMA((36,)),pltpu.SemaphoreType.DMA((1,))]*n
def gather_chains(names,widths,src,dst,sems):
    chains=[gather_steps(names[t],[widths[t]],[src[t]],[dst[t]],*sems[3*t:3*t+3]) for t in range(len(names))]
    def both(k):
        def f():
            for ch in chains: ch[k]()
        return f
    return [both(k) for k in range(6)]
def gather_kernel(names,widths,*refs):
    n=len(names)
    steps=gather_chains(names,widths,refs[:n],refs[n:2*n],refs[2*n:])
    greet(GPEERS)
    for f in steps: f()
def gather_shapes(arrs):
    return tuple(jax.ShapeDtypeStruct((4,4,2)+a.shape,a.dtype) for a in arrs)
def gather(names,arrs,cid=0):
    n=len(names)
    return pl.pallas_call(functools.partial(gather_kernel,names,[a.shape[1] for a in arrs]),
      out_shape=gather_shapes(arrs),
      in_specs=[pl.BlockSpec(memory_space=pl.ANY)]*n,out_specs=tuple([pl.BlockSpec(memory_space=pl.ANY)]*n),
      scratch_shapes=gather_sems(n),
      compiler_params=pltpu.CompilerParams(collective_id=cid,has_side_effects=True))(*arrs)


RSPLIT={"q":(6,7,6),"o":(2,3,2),"e":(10,7,8),"c":(2,3,2)}
AX=("xzy","yzx","zyx")
RPEERS=[(a,k) for a in "xyz" for k in (1,2,3)]
def rcuts(name,W):
    out=[];p=0
    for n in RSPLIT[name]:
        out.append((p,min(p+n*128,W))); p+=n*128
    assert out[-1][1]==W
    return out
def scatter_steps(nm,width,src,out,bufs,sems):
    ss,rs,ls=sems
    z,y,x,c=coords(); xl=x%2; xh=x//2
    me={"x":x,"y":y,"z":z}
    cnt=[0]; lcnt=[0]; allc=[]
    def mk(s,d,ax,k,keep=True):
        i=cnt[0]; cnt[0]+=1
        cp=pltpu.make_async_remote_copy(src_ref=s,dst_ref=d,send_sem=ss.at[i],recv_sem=rs.at[i],device_id=peer_of(ax,k),device_id_type=MESH)
        if keep: allc.append(cp)
        return cp
    def mkload(s,d):
        i=lcnt[0]; lcnt[0]+=1
        return pltpu.make_async_copy(s,d,ls.at[i])
    cut=rcuts(nm,width)
    f32=lambda a:a.astype(jnp.float32)
    def D(p,k,i=None):
        a,b=cut[p]; s=slice(None) if i is None else pl.ds(2*i,2)
        if p==0:
            h=(b-a)//2
            return src.at[s,:,k%2,:,pl.ds(pl.multiple_of(a+(k//2)*h,128),h)]
        if p==1: return src.at[s,k,:,:,pl.ds(a,b-a)]
        return src.at[k,s,:,:,pl.ds(a,b-a)]
    M=(4,2,2); P3=(0,1,2)
    ld={}; R={}
    for p in P3:
        own,rlp,rlm,rm,rp,rl2p,rl2m,rm2,rp2,out2,r3,r4=bufs[p]
        k=me[AX[p][0]]; ax=AX[p][0]
        bp=own.at[pl.ds(0,2)]; bm=own.at[pl.ds(2,2)]
        ld[p]=[mkload(D(p,(k+1)%4,0),bp),mkload(D(p,(k+3)%4,1),bm),mkload(D(p,k),own)]
        R[p,"a"]=[mk(D(p,(k+2)%4,0),rlp,ax,1),mk(D(p,(k+2)%4,1),rlm,ax,3)]
        R[p,"b"]=[mk(D(p,(k+1)%4,1),rm.at[pl.ds(2,2)],ax,1),mk(D(p,(k+3)%4,0),rp.at[pl.ds(0,2)],ax,3),
                  mk(bp,rm.at[pl.ds(0,2)],ax,1,False),mk(bm,rp.at[pl.ds(2,2)],ax,3,False)]
        m=M[p]; hm=m//2
        ax=AX[p][1]; k=me[ax]
        L=pl.ds(0,hm); H=pl.ds(hm,hm)
        R[p,"c"]=[mk(own.at[(k+2)%4,L],rl2p,ax,1),mk(own.at[(k+2)%4,H],rl2m,ax,3)]
        R[p,"d"]=[mk(own.at[(k+1)%4,H],rm2.at[H],ax,1),mk(own.at[(k+3)%4,L],rp2.at[L],ax,3),
                  mk(own.at[(k+1)%4,L],rm2.at[L],ax,1),mk(own.at[(k+3)%4,H],rp2.at[H],ax,3)]
        ax=AX[p][2]; k=me[ax]; q=4 if p==0 else 2
        R[p,"e"]=[mk(out2.at[(k+j)%q],r3.at[j-1],ax,j) for j in (1,2,3)]
        if p==0: R[p,"f"]=[mk(r4.at[xh],r4.at[xh],"x",2)]
    def addin(dst,other,cntn,f,g):
        def body(i,_):
            dst[f(i)]=(f32(dst[f(i)])+f32(other[g(i)])).astype(jnp.bfloat16)
            return 0
        lax.fori_loop(0,cntn,body,0)
    def first():
        for p in P3:
            for cp in ld[p][:2]: cp.start()
        for p in P3:
            for cp in R[p,"a"]: cp.start()
        for p in P3:
            for cp in R[p,"b"][:2]: cp.start()
    def relay(p):
        def f():
            own,rlp,rlm=bufs[p][:3]
            m=M[p]
            ld[p][0].wait(); R[p,"a"][0].wait_recv(); addin(own,rlp,2*m,lambda i:(i//m,i%m),lambda i:(i//m,i%m)); R[p,"b"][2].start()
            ld[p][1].wait(); R[p,"a"][1].wait_recv(); addin(own,rlm,2*m,lambda i:(2+i//m,i%m),lambda i:(i//m,i%m)); R[p,"b"][3].start()
        return f
    def reload(p):
        def f():
            for cp in R[p,"b"][2:]: cp.wait_send()
            ld[p][2].start()
        return f
    def sum1(p):
        def f():
            own,rm,rp=bufs[p][0],bufs[p][3],bufs[p][4]
            m=M[p]
            ld[p][2].wait()
            for cp in R[p,"b"]: cp.wait_recv()
            def body(i,_):
                j=(i//m,i%m)
                own[j]=(f32(own[j])+(f32(rm[j])+f32(rp[j]))).astype(jnp.bfloat16)
                return 0
            lax.fori_loop(0,4*m,body,0)
            for cp in R[p,"c"]: cp.start()
            for cp in R[p,"d"][:2]: cp.start()
        return f
    def relay2(p):
        def f():
            own,rl2p,rl2m=bufs[p][0],bufs[p][5],bufs[p][6]
            hm=M[p]//2; k=me[AX[p][1]]
            R[p,"c"][0].wait_recv()
            addin(own,rl2p,hm,lambda i:((k+1)%4,i),lambda i:i)
            R[p,"d"][2].start()
            R[p,"c"][1].wait_recv()
            addin(own,rl2m,hm,lambda i:((k+3)%4,hm+i),lambda i:i)
            R[p,"d"][3].start()
        return f
    def sum2(p):
        def f():
            own,rm2,rp2,out2=bufs[p][0],bufs[p][7],bufs[p][8],bufs[p][9]
            k=me[AX[p][1]]
            for cp in R[p,"d"]: cp.wait_recv()
            def body(i,_):
                out2[i]=(f32(own[k,i])+(f32(rm2[i])+f32(rp2[i]))).astype(jnp.bfloat16)
                return 0
            lax.fori_loop(0,M[p],body,0)
            for cp in R[p,"e"]: cp.start()
        return f
    def last(p):
        def f():
            out2,r3,r4=bufs[p][9:12]
            a,b=cut[p]
            for cp in R[p,"e"]: cp.wait_recv()
            k=me[AX[p][2]] if p==0 else xl
            s=(f32(out2[k])+f32(r3[1]))+(f32(r3[0])+f32(r3[2]))
            if p==0:
                r4[xh]=s.astype(jnp.bfloat16)
                R[p,"f"][0].start()
            else:
                out[:,pl.ds(a,b-a)]=s[0:out.shape[0],:]
        return f
    def end():
        a,b=cut[0]; h=(b-a)//2; r4=bufs[0][11]
        R[0,"f"][0].wait_recv()
        for j in range(2): out[:,pl.ds(a+j*h,h)]=f32(r4[j])[0:out.shape[0],:]
        for cp in allc: cp.wait_send()
    return [[first]]+[[f(p) for p in P3] for f in (relay,reload,sum1,relay2,sum2,last)]+[[end]]
STAGES=8
def staggered(chains,by):
    return [[f for i,ch in enumerate(chains) if 0<=tick-by*i<STAGES for f in ch[tick-by*i]] for tick in range(STAGES+by*(len(chains)-1))]
def scatter_bufs(nm,r,w):
    scr=[]
    for p,(a,b) in enumerate(rcuts(nm,w)):
        m=4 if p==0 else 2; v=(b-a)//2 if p==0 else b-a; hm=m//2
        B=lambda *s:pltpu.VMEM(s+(r,v),jnp.bfloat16)
        scr+=[B(4,m),B(2,m),B(2,m),B(4,m),B(4,m),B(hm),B(hm),B(m),B(m),B(m),B(3),B(2) if p==0 else pltpu.VMEM((8,128),jnp.bfloat16)]
    return scr
def scatter_sems():
    return [pltpu.SemaphoreType.DMA((46,)),pltpu.SemaphoreType.DMA((46,)),pltpu.SemaphoreType.DMA((9,))]
def by_part(refs):
    return [refs[12*p:12*p+12] for p in range(3)]
def narrowed(bufs,nm,w):
    out=[]
    for p,(a,b) in enumerate(rcuts(nm,w)):
        v=(b-a)//2 if p==0 else b-a
        out.append([ref if ref.shape[-1]==v or ref.shape==(8,128) else ref.at[(slice(None),)*(len(ref.shape)-1)+(pl.ds(0,v),)] for ref in bufs[p]])
    return out
def vector_steps(vbuf,sems):
    z,y,x,c=coords(); me=(x,y,z)
    ss,rs=sems
    R=[[pltpu.make_async_remote_copy(src_ref=vbuf[st].at[me[st]],dst_ref=vbuf[st].at[me[st]],send_sem=ss.at[3*st+k-1],recv_sem=rs.at[3*st+k-1],device_id=peer_of("xyz"[st],k),device_id_type=MESH) for k in (1,2,3)] for st in range(3)]
    def go(st,v):
        vbuf[st][pl.ds(me[st],1)]=v[None]
        for cp in R[st]: cp.start()
    def total(st):
        for cp in R[st]: cp.wait_recv()
        b=vbuf[st]
        return (b[0]+b[1])+(b[2]+b[3])
    def end():
        for l in R:
            for cp in l: cp.wait_send()
    return go,total,end


TT=256; KH=896; HD=64; LEN=4096; NEG=-1e30; ROWS=32
FQ,FK,BQ,BK=1024,1024,512,512
def dot(a,b): return lax.dot_general(a,b,(((1,),(0,)),((),())),preferred_element_type=jnp.float32)
def dot_nt(a,b): return lax.dot_general(a,b,(((1,),(1,)),((),())),preferred_element_type=jnp.float32)
def group_greet(d,r,c,across):
    bar=pltpu.get_barrier_semaphore()
    for rr in across: pl.semaphore_signal(bar,inc=1,device_id=(1-d,rr,c),device_id_type=MESH)
    def body(i,_):
        @pl.when(i!=r*2+c)
        def _():
            pl.semaphore_signal(bar,inc=1,device_id=(d,i//2,i%2),device_id_type=MESH)
        return 0
    lax.fori_loop(0,2*ROWS,body,0)
def group_wait(across):
    pl.semaphore_wait(pltpu.get_barrier_semaphore(),2*ROWS-1+across)
def push(src,dst,send_sem,recv_sem,same,target):
    @pl.when(same)
    def _():
        pltpu.make_async_copy(src,dst,recv_sem).start()
    @pl.when(jnp.logical_not(same))
    def _():
        pltpu.make_async_remote_copy(src_ref=src,dst_ref=dst,send_sem=send_sem,recv_sem=recv_sem,device_id=target,device_id_type=MESH).start()
def pushed(src,dst,send_sem,recv_sem,same,target):
    @pl.when(jnp.logical_not(same))
    def _():
        pltpu.make_async_remote_copy(src_ref=src,dst_ref=dst,send_sem=send_sem,recv_sem=recv_sem,device_id=target,device_id_type=MESH).wait_send()
def arrived(ref,sem):
    pltpu.make_async_copy(ref,ref,sem).wait()
def steps(text):
    return [text[k:k+2] for k in range(0,len(text),2)]
FWD_BEFORE=steps("q1o0q2e1q3o1q4e2q5")
FWD_LOAD=steps("c0e3o2")
FWD_PROJ=steps("c1o3")
FWD_SENT=steps("e4c2o4")
FWD_AT=((1,"c3"),)
FWD_THEN=steps("o5e5")
FWD_LATE=steps("c4")
FWD_END=steps("c5")
QW=2432
GC=0.7978845608028654
def dot_tn(a,b): return lax.dot_general(a,b,(((0,),(0,)),((),())),preferred_element_type=jnp.float32)
def attn_fwd_kernel(names,widths,*refs):
    it=iter(refs)
    take=lambda n:[next(it) for _ in range(n)]
    n=len(names)
    xt,cols,bias,eb,segs=take(5)
    src=take(n)
    qkv_out,oT,lse,start,op,h1t,norm1t,norm2t,recips,h2t,mid,pre,a_own,a_other=take(14)
    dst=take(n)
    o_recv,qkv,knt,obf,wv,wov,acc,pt,of,mt,stat_s,stat_r,s_in,s_out,r_in,r_out,l_sem,w_sem,x_sem=take(19)
    chains={nm:gather_steps(nm,[widths[t]],[src[t]],[dst[t]],*take(3)) for t,nm in enumerate(names)}
    def run(which):
        for k in which: chains[k[0]][int(k[1])]()
    d=lax.axis_index("dev"); r=lax.axis_index("row"); c=lax.axis_index("col")
    partner=(d,r,1-c)
    def swap(k,s,t):
        cp=pltpu.make_async_remote_copy(src_ref=s,dst_ref=t,send_sem=x_sem.at[2*k],recv_sem=x_sem.at[2*k+1],device_id=partner,device_id_type=MESH)
        cp.start()
        return cp
    def norm(k,v,gain,shift,normed,hidden):
        stat_s[k,0:1,:]=jnp.sum(v,axis=0,keepdims=True)
        stat_s[k,1:2,:]=jnp.sum(v*v,axis=0,keepdims=True)
        swap(2*k,stat_s.at[k],stat_r.at[k]).wait()
        m=(stat_s[k,0:1,:]+stat_r[k,0:1,:])*(1.0/D)
        recip=lax.rsqrt((stat_s[k,1:2,:]+stat_r[k,1:2,:])*(1.0/D)-m*m+1e-5)
        xhat=(v-m)*recip
        normed[...]=xhat
        recips[k:k+1,:]=recip
        own=pl.ds(pl.multiple_of(16*c,16),16)
        hidden[own]=(xhat*gain+shift).reshape(16,56,TT).astype(bf)
        return swap(2*k+1,hidden.at[own],hidden.at[own])
    group_greet(d,r,c,[r+1-2*(r%2)])
    acc[...]=jnp.broadcast_to(bias[...],acc.shape)
    pre[...]=jnp.broadcast_to(eb[...],pre.shape)
    seg=jnp.broadcast_to(jnp.where(r%2==0,segs[0:1,:],segs[1:2,:]),(8,LEN))
    pos=lax.broadcasted_iota(jnp.int32,(8,LEN),1)
    first=jnp.where((seg!=pltpu.roll(seg,1,1))&(pos>0),pos,0)
    for k in range(12):
        first=jnp.maximum(first,jnp.where(pos>=2**k,pltpu.roll(first,2**k,1),0))
    start[...]=first[0:1,:]
    group_wait(1)
    run(["q0","e0"])
    sent=norm(0,xt[...].astype(jnp.float32),cols[:,1:2],cols[:,3:4],norm1t,h1t)
    run(FWD_BEFORE)
    wq=wv.at[:,:,:,:,pl.ds(0,QW)]
    load=pltpu.make_async_copy(dst[0],wq,w_sem.at[0])
    load.start()
    run(FWD_LOAD)
    sent.wait()
    load.wait()
    def over_blocks(total,tile,hidden,weight):
        n=total.shape[1]
        def body(k,_):
            hk=jnp.concatenate([hidden[4*k+b] for b in range(4)],axis=0)
            for a0 in range(0,n,tile):
                sl=pl.ds(a0,min(tile,n-a0))
                wk=jnp.concatenate([weight[k//2,(k%2)*2+b//2,b%2,:,sl] for b in range(4)],axis=0)
                total[:,sl]+=dot_tn(hk,wk)
            return 0
        lax.fori_loop(0,8,body,0)
    over_blocks(acc,512,h1t,wv)
    run(FWD_PROJ)
    for a0 in range(0,2400,128):
        piece=acc[:,a0:min(a0+128,2400)].T.astype(bf)
        at=a0
        while at<min(a0+128,2400):
            t=at//800; end=min(a0+128,2400,(t+1)*800)
            pt[t,at-800*t:end-800*t,:]=piece[at-a0:end-a0]
            at=end
    lanes=pl.ds(pl.multiple_of(r*128,128),128)
    def full(fn):
        def body(k,_):
            i=(r+k)%24
            fn(pt.at[:,pl.ds(pl.multiple_of(64*(i//2)+32*c,32),64),pl.ds(pl.multiple_of((i%2)*128,128),128)],qkv.at[:,:,lanes],s_in.at[i],r_in,i==r,(d,i,c))
            return 0
        lax.fori_loop(0,24,body,0)
    def halves(fn):
        rows=pl.ds(pl.multiple_of(32*c,32),32)
        for s in range(2):
            fn(pt.at[:,pl.ds(pl.multiple_of(768*(1-c),32),32),pl.ds(s*128,128)],qkv.at[:,rows,lanes],s_in.at[24+s],r_in,(r==24+s)&(c==0),(d,24+s,0))
    full(push); halves(push)
    run(FWD_SENT)
    item=(r<24)|((c==0)&(r<26))
    head=r//2+13*c; seq=r%2
    def outs(qi,fn):
        def body(i,_):
            rr=qi*(FQ//128)+(r+i//2)%(FQ//128); cc=i%2
            fn(obf.at[:,pl.ds(pl.multiple_of(rr*128,128),128)],o_recv.at[seq,head],s_out.at[rr*2+cc],r_out,(rr==r)&(cc==c),(d,rr,cc))
            return 0
        lax.fori_loop(0,FQ//64,body,0)
    save=pltpu.make_async_copy(qkv,qkv_out,l_sem)
    @pl.when(item)
    def _():
        arrived(qkv,r_in)
        save.start()
        for a in range(LEN//512):
            sl=pl.ds(a*512,512)
            knt[sl,:]=qkv[1,:,sl].T
    def qloop(qi,_):
        @pl.when(item)
        def _():
            iota=lax.broadcasted_iota(jnp.int32,(FK,FQ),0)
            iotl=lax.broadcasted_iota(jnp.int32,(FK,FQ),1)
            qs=pl.ds(pl.multiple_of(qi*FQ,FQ),FQ)
            q=qkv[0,:,qs]*jnp.bfloat16(0.125)
            st=start[:,qs]
            def step(kj,carry,diag):
                m,l,acc=carry
                ks=pl.ds(pl.multiple_of(kj*FK,FK),FK)
                s=dot(knt[ks,:],q)
                ok=iota>=(st-kj*FK)
                if diag: ok=ok&(iota<=iotl)
                s=jnp.where(ok,s,NEG)
                mn=jnp.maximum(m,jnp.max(s,axis=0,keepdims=True))
                p=jnp.exp(s-mn)
                al=jnp.exp(m-mn)
                l=l*al+jnp.sum(p,axis=0,keepdims=True)
                acc=acc*al+dot(qkv[2,:,ks],p.astype(jnp.bfloat16))
                return mn,l,acc
            carry=(jnp.full((1,FQ),NEG,jnp.float32),jnp.zeros((1,FQ),jnp.float32),jnp.zeros((HD,FQ),jnp.float32))
            carry=lax.fori_loop(0,qi,lambda kj,cr:step(kj,cr,False),carry)
            m,l,acc=step(qi,carry,True)
            o=acc/l
            oT[:,qs]=o
            lse[:,qs]=m+jnp.log(l)
            obf[:,qs]=o.astype(jnp.bfloat16)
            outs(qi,push)
        for at,k in FWD_AT:
            pl.when(qi==at)(functools.partial(run,steps(k)))
        return 0
    lax.fori_loop(0,LEN//FQ,qloop,0)
    run(FWD_THEN)
    loads=[pltpu.make_async_copy(dst[3],wov,w_sem.at[0]),pltpu.make_async_copy(dst[1],wv,w_sem.at[1])]
    for cp in loads: cp.start()
    arrived(o_recv,r_out)
    for s in range(2): of[:,pl.ds(128*s,128)]=o_recv[s].reshape(1600,128).astype(jnp.float32)
    for k in range(ROWS):
        op[k,0:50,:]=of[50*k:50*k+50,:].astype(bf)
        op[k,50:56,:]=jnp.zeros((6,TT),bf)
    loads[0].wait()
    mid[...]=jnp.zeros_like(mid)
    over_blocks(mid,512,op,wov)
    run(FWD_LATE)
    for k in range(7):
        sl=pl.ds(128*k,128)
        mt[sl,:]=mid[:,sl].T+cols[sl,5:6]+xt[sl,:].astype(jnp.float32)
        mid[:,sl]=mt[sl,:].T
    norm(1,mt[...],cols[:,0:1],cols[:,4:5],norm2t,h2t).wait()
    loads[1].wait()
    over_blocks(pre,640,h2t,wv)
    for a0 in range(0,3200,640):
        p=pre[:,a0:a0+640]
        a_own[:,a0:a0+640]=(p*(0.5*(1.0+jnp.tanh(GC*(p+0.044715*(p*p*p)))))).astype(bf)
    sent=swap(4,a_own,a_other)
    run(FWD_END)
    sent.wait()
    @pl.when(item)
    def _():
        save.wait()
        for qi in range(LEN//FQ): outs(qi,pushed)
    full(pushed); halves(pushed)
BWD_START="e0"
BWD_AT=((0,"e1o0"),(1,"e2o1"),(2,"c0"),(3,"e3"),(4,"o2"),(5,"c1"),(7,"e4o3"))
BWD_THEN="e5c2e6o4e7"
BWD_LAST="q0**c3q1o5c4q2--q3c5o6q4c6q5c7o7q6++q7"
BR=224
KQ=2432
def unpad_rows(dst,v):
    for g in range(16): dst[50*g:50*g+50,:]=v[56*g:56*g+50,:]
def token_sums(v):
    if v.dtype==bf: return lax.dot_general(jnp.ones((8,TT),bf),v,(((1,),(1,)),((),())),preferred_element_type=jnp.float32)[:1]
    v=v[:,:128]+v[:,128:]
    return jnp.concatenate([jnp.sum(v[128*k:128*k+128,:].T,axis=0,keepdims=True) for k in range(v.shape[0]//128)],axis=1)
def back_kernel(names,widths,*refs):
    it=iter(refs)
    take=lambda n:[next(it) for _ in range(n)]
    n=len(names)
    dh2t,norm2t,gt,cols,recips,op,wo,qkv,oT,start,lse,h1t,normt,vec_in,wq=take(15)
    parts=take(n)
    part_o,part_q,gtok,sum_o,sum_q,vec_out=take(6)
    sums=take(n)
    doT,knt,vnt,dqa,delta,dout,dq,stage,wblk,dh_send,dh_recv,do_recv,lhs,nbuf,dh,gmid,gat,dflat,dot_,stat_s,stat_r=take(21)
    vbuf=take(3); vtmp=next(it)
    s_in,s_out,r_in,r_out,q_sem,w_sem,x_sem,l_sem,free=take(9)
    v_sems=take(2)
    chains={}
    for t in range(n):
        b=by_part(take(36))
        if t==0: first_bufs=b
        chains[names[t]]=scatter_steps(names[t],widths[t],parts[t],sums[t],b,take(3))
    chains["o"]=scatter_steps("o",KH,part_o,sum_o,by_part(take(36)),take(3))
    chains["q"]=scatter_steps("q",KQ,part_q,sum_q,narrowed(first_bufs,"q",KQ),take(3))
    def run(which):
        for k in steps(which):
            for f in chains[k[0]][int(k[1])]: f()
    v_go,v_total,v_end=vector_steps(vbuf,v_sems)
    d=lax.axis_index("dev"); r=lax.axis_index("row"); c=lax.axis_index("col")
    partner=(d,r,1-c)
    item=(r<24)|((c==0)&(r<26))
    loads=[pltpu.make_async_copy(s,t,l_sem.at[k]) for k,(s,t) in enumerate(((dh2t,dh),(norm2t,nbuf),(op,lhs),(normt,nbuf),(h1t,lhs)))]
    for cp in loads[:3]: cp.start()
    group_greet(d,r,c,[r+1-2*(r%2),r])
    @pl.when(item)
    def _():
        for a in range(LEN//512):
            sl=pl.ds(a*512,512)
            knt[sl,:]=qkv[1,:,sl].T
            vnt[sl,:]=qkv[2,:,sl].T
        dqa[...]=jnp.zeros_like(dqa)
    stage[...]=jnp.zeros_like(stage)
    vtmp[...]=jnp.zeros_like(vtmp)
    vtmp[pl.ds(35,vec_in.shape[0]),:]=vec_in[...]
    def vec_rows(at,row):
        for k in range(row.shape[1]//128): vtmp[pl.ds(at+k,1),:]=row[:,128*k:128*k+128]
    def norm_back(k,incoming,normed,gain,recip):
        e=incoming*gain
        stat_s[k,0:1,:]=jnp.sum(e,axis=0,keepdims=True)
        stat_s[k,1:2,:]=jnp.sum(e*normed,axis=0,keepdims=True)
        cp=pltpu.make_async_remote_copy(src_ref=stat_s.at[k],dst_ref=stat_r.at[k],send_sem=x_sem.at[2*k],recv_sem=x_sem.at[2*k+1],device_id=partner,device_id_type=MESH)
        cp.start()
        cp.wait()
        s1=stat_s[k,0:1,:]+stat_r[k,0:1,:]
        s2=stat_s[k,1:2,:]+stat_r[k,1:2,:]
        return recip*(e-s1*(1.0/D)-normed*(s2*(1.0/D)))
    group_wait(2)
    run(BWD_START)
    loads[0].wait(); loads[1].wait()
    vec_rows(14,token_sums(dh[...]*nbuf[...]))
    vec_rows(21,token_sums(dh[...]))
    gmid[...]=(gt[...].astype(jnp.float32)+norm_back(0,dh[...],nbuf[...],cols[:,0:1],recips[0:1,:]))*cols[:,2:3]
    gat[...]=gmid[...].astype(bf)
    vec_rows(28,token_sums(gat[...]))
    loads[3].start()
    half=lambda w,base,k:w.at[pl.ds(pl.multiple_of(base*KH+BR*k,32),BR)]
    nb=KH//BR
    def pair_product(w,wide,rhs,recv,sem):
        blocks=[half(w,1-c,k) for k in range(nb)]+[half(w,c,k) for k in range(nb)]
        slot=lambda k:wblk.at[k%2,:,pl.ds(0,wide)] if wide<QW else wblk.at[k%2]
        ld=[pltpu.make_async_copy(blocks[k],slot(k),w_sem.at[k%2]) for k in range(2*nb)]
        ld[0].start(); ld[1].start()
        swap=pltpu.make_async_remote_copy(src_ref=dh_send,dst_ref=recv,send_sem=x_sem.at[sem],recv_sem=x_sem.at[sem+1],device_id=partner,device_id_type=MESH)
        for k in range(2*nb):
            ld[k].wait()
            v=dot(wblk[k%2,:,0:rhs.shape[0]],rhs)
            if k<nb: dh_send[pl.ds(BR*k,BR),:]=v.astype(bf)
            else: dh[pl.ds(BR*(k-nb),BR),:]=v
            if k<2*nb-2: ld[k+2].start()
            if k==nb-1: swap.start()
        return swap
    swap=pair_product(wo,KH,gat[...],do_recv,4)
    swap.wait()
    unpad_rows(dflat,dh[...]+do_recv[...].astype(jnp.float32))
    dot_[...]=dflat[...].astype(bf)
    lanes=pl.ds(pl.multiple_of(r*128,128),128)
    def full(fn):
        def body(k,_):
            i=(r+k)%24
            fn(dot_.at[pl.ds(pl.multiple_of(64*(i//2)+32*c,32),64),pl.ds(pl.multiple_of((i%2)*128,128),128)],doT.at[:,lanes],s_in.at[i],r_in,i==r,(d,i,c))
            return 0
        lax.fori_loop(0,24,body,0)
    def halves(fn):
        rows=pl.ds(pl.multiple_of(32*c,32),32)
        for s in range(2):
            fn(dot_.at[pl.ds(pl.multiple_of(768*(1-c),32),32),pl.ds(s*128,128)],doT.at[rows,lanes],s_in.at[24+s],r_in,(r==24+s)&(c==0),(d,24+s,0))
    full(push); halves(push)
    def emit(part,cols_,rhs):
        prev={}
        for b in range(8):
            slot=b%2
            if b>=2: prev[slot].wait()
            stage[slot,:,:,:,0:cols_]=dot_nt(lhs[pl.ds(224*b,224),:],rhs).reshape(2,2,56,cols_).astype(bf)
            src=stage.at[slot] if cols_==2400 else stage.at[slot,:,:,:,pl.ds(0,cols_)]
            prev[slot]=pltpu.make_async_copy(src,part.at[b//2,pl.ds(2*(b%2),2)],q_sem.at[slot])
            prev[slot].start()
        return prev
    loads[2].wait()
    for cp in emit(part_o,KH,gat[...]).values(): cp.wait()
    loads[4].start()
    def outs(fn):
        seq=pl.ds(pl.multiple_of((r%2)*128,128),128)
        @pl.when(r<24)
        def _():
            def body(k,_):
                i=(r+k)%ROWS
                fn(dout.at[:,:,pl.ds(pl.multiple_of(i*128,128),128)],dq.at[:,pl.ds(pl.multiple_of(64*(r//2)+32*c,32),64),seq],s_out.at[i],r_out,i==r,(d,i,c))
                return 0
            lax.fori_loop(0,ROWS,body,0)
        @pl.when(r>=24)
        def _():
            def body(k,_):
                rr=(r+k//2)%ROWS; cc=k%2
                fn(dout.at[:,pl.ds(pl.multiple_of(32*cc,32),32),pl.ds(pl.multiple_of(rr*128,128),128)],dq.at[:,pl.ds(pl.multiple_of(768*(1-cc),32),32),seq],s_out.at[2*rr+cc],r_out,(rr==r)&(cc==c),(d,rr,cc))
                return 0
            lax.fori_loop(0,2*ROWS,body,0)
    @pl.when(item)
    def _():
        arrived(doT,r_in)
        for a in range(LEN//512):
            sl=pl.ds(a*512,512)
            delta[:,sl]=jnp.sum(oT[:,sl]*doT[:,sl].astype(jnp.float32),axis=0,keepdims=True)
    def kloop(kj,_):
        @pl.when(item)
        def _():
            iota=lax.broadcasted_iota(jnp.int32,(BK,BQ),0)
            iotl=lax.broadcasted_iota(jnp.int32,(BK,BQ),1)
            ks=pl.ds(pl.multiple_of(kj*BK,BK),BK)
            kn=knt[ks,:]; vn=vnt[ks,:]; kT=qkv[1,:,ks]
            def step(qi,carry,diag):
                dk,dv=carry
                qs=pl.ds(pl.multiple_of(qi*BQ,BQ),BQ)
                q=qkv[0,:,qs]*jnp.bfloat16(0.125)
                do=doT[:,qs]
                s=dot(kn,q)
                ok=iota>=(start[:,qs]-kj*BK)
                if diag: ok=ok&(iota<=iotl)
                p=jnp.exp(jnp.where(ok,s,NEG)-lse[:,qs])
                dp=dot(vn,do)
                ds=(p*(dp-delta[:,qs])).astype(jnp.bfloat16)
                dv=dv+dot_nt(do,p.astype(jnp.bfloat16))
                dk=dk+dot_nt(q,ds)
                dqa[:,qs]+=dot(kT,ds)
                return dk,dv
            z=jnp.zeros((HD,BK),jnp.float32)
            carry=step(kj,(z,z),True)
            dk,dv=lax.fori_loop(kj+1,LEN//BQ,lambda qi,cr:step(qi,cr,False),carry)
            dout[1,:,ks]=dk.astype(jnp.bfloat16)
            dout[2,:,ks]=dv.astype(jnp.bfloat16)
        for step,which in BWD_AT:
            pl.when(kj==step)(functools.partial(run,which))
        return 0
    lax.fori_loop(0,LEN//BK,kloop,0)
    @pl.when(item)
    def _():
        for a in range(LEN//512):
            sl=pl.ds(a*512,512)
            dout[0,:,sl]=(dqa[:,sl]*0.125).astype(jnp.bfloat16)
        outs(push)
    run(BWD_THEN)
    for ax,k in RPEERS: pl.semaphore_signal(free,inc=1,device_id=peer_of(ax,k),device_id_type=MESH)
    arrived(dq,r_out)
    grads=dq[...].reshape(2400,TT)
    loads[4].wait()
    for cp in emit(part_q,2400,grads).values(): cp.wait()
    pl.semaphore_wait(free,len(RPEERS))
    def late_product():
        chains["swap"]=pair_product(wq,QW,grads,dh_recv,6)
    def late_norm():
        chains["swap"].wait()
        dh[...]=dh[...]+dh_recv[...].astype(jnp.float32)
        loads[3].wait()
        vec_rows(0,token_sums(dh[...]*nbuf[...]))
        vec_rows(7,token_sums(dh[...]))
        vec_rows(67,jnp.concatenate((token_sums(grads),jnp.zeros((1,32),jnp.float32)),axis=1))
        v_go(0,vtmp[...])
        gtok[...]=(gmid[...]+norm_back(1,dh[...],nbuf[...],cols[:,1:2],recips[1:2,:])).astype(bf)
        v_go(1,v_total(0))
    def late_vec():
        v_go(2,v_total(1))
    for k in steps(BWD_LAST):
        if k=="**": late_product()
        elif k=="--": late_norm()
        elif k=="++": late_vec()
        else: run(k)
    vec_out[...]=v_total(2)
    v_end()
    pl.when(item)(lambda:outs(pushed))
    full(pushed); halves(pushed)
VM=pl.BlockSpec(memory_space=pltpu.VMEM); ANY=pl.BlockSpec(memory_space=pl.ANY)
bf=jnp.bfloat16
def attend(xt,cols,bias,eb,segs,names,arrs,cid=1):
    S=jax.ShapeDtypeStruct; n=len(names); V=pltpu.VMEM; DM=pltpu.SemaphoreType.DMA; f=jnp.float32
    FH=eb.shape[1]
    out=pl.pallas_call(functools.partial(attn_fwd_kernel,names,[a.shape[1] for a in arrs]),
      out_shape=(S((3,HD,LEN),bf),S((HD,LEN),f),S((1,LEN),f),S((1,LEN),jnp.int32),S((32,56,TT),bf),S((32,56,TT),bf),S((KH,TT),f),S((KH,TT),f),S((8,TT),f),S((32,56,TT),bf),
        S((TT,KH),f),S((TT,FH),f),S((TT,FH),bf),S((TT,FH),bf))+gather_shapes(arrs),
      in_specs=[VM]*5+[ANY]*n,out_specs=(ANY,)+(VM,)*12+(ANY,)+(ANY,)*n,
      scratch_shapes=[V((2,25,HD,128),bf),V((3,HD,LEN),bf),V((LEN,HD),bf),V((HD,LEN),bf),V((4,4,2,56,FH),bf),V((4,4,2,56,KH),bf),V((TT,2400),f),V((3,800,TT),bf),V((1600,TT),f),V((KH,TT),f),
        V((2,8,TT),f),V((2,8,TT),f),DM((26,)),DM((64,)),DM,DM,DM,DM((2,)),DM((10,))]+gather_sems(n),
      compiler_params=pltpu.CompilerParams(collective_id=cid,has_side_effects=True,vmem_limit_bytes=62<<20))(xt,cols,bias,eb,segs,*arrs)
    return out[:4],out[4:14],out[14:]
def attend_back(front,kept,h1t,normt,vec,wq,names,parts,cid=2):
    S=jax.ShapeDtypeStruct; n=len(names); f=jnp.float32; V=pltpu.VMEM; DM=pltpu.SemaphoreType.DMA
    qkv,oT,lse,start=kept
    rows=88
    out=pl.pallas_call(functools.partial(back_kernel,names,[a.shape[4] for a in parts]),
      out_shape=(S((4,4,2,56,KH),bf),S((4,4,2,56,KQ),bf),S((KH,TT),bf),S((50,KH),f),S((50,KQ),f),S((rows,128),f))+tuple(S((50 if a.shape[3]==56 else a.shape[3],a.shape[4]),f) for a in parts),
      in_specs=[ANY,ANY,VM,VM,VM,ANY,ANY,VM,VM,VM,VM,ANY,ANY,VM]+[ANY]*(1+n),out_specs=(ANY,ANY,VM,VM,VM,VM)+(VM,)*n,
      scratch_shapes=[V((HD,LEN),bf),V((LEN,HD),bf),V((LEN,HD),bf),V((HD,LEN),f),V((1,LEN),f),V((3,HD,LEN),bf),
        V((3,800,TT),bf),V((2,2,2,56,KQ),bf),V((2,BR,QW),bf),V((KH,TT),bf),V((KH,TT),bf),V((KH,TT),bf),V((KP,TT),bf),
        V((KH,TT),f),V((KH,TT),f),V((KH,TT),f),V((KH,TT),bf),V((800,TT),f),V((800,TT),bf),V((2,8,TT),f),V((2,8,TT),f)]+[V((4,rows,128),f)]*3+[V((rows,128),f)]+
        [DM((26,)),DM((64,)),DM,DM,DM((2,)),DM((2,)),DM((8,)),DM((5,)),pltpu.SemaphoreType.REGULAR,DM((9,)),DM((9,))]+
        sum([scatter_bufs(nm,*a.shape[3:])+scatter_sems() for nm,a in zip(names,parts)],[])+scatter_bufs("o",56,KH)+scatter_sems()*2,
      compiler_params=pltpu.CompilerParams(collective_id=cid,has_side_effects=True,vmem_limit_bytes=VMEM_BACK))(*front,qkv,oT,start,lse,h1t,normt,vec,wq,*parts)
    return out[2],out[3],out[4],out[5],out[6:]
VMEM_BACK=63<<20


FH=3200; TF=640
def mlp_kernel(h2t,we,wc,pre,a_own,a_other,mid,cb,g,result,part_c,part_e,dh2,dsum,
        wev,wcv,da_send,da_recv,dpre,dh_send,dh_recv,stage_e,stage_c,w_sem,s_sem,r_sem,e_sem,c_sem):
    c=lax.axis_index("col"); other=1-c
    partner=(lax.axis_index("dev"),lax.axis_index("row"),other)
    loads=[pltpu.make_async_copy(wc,wcv,w_sem.at[0]),pltpu.make_async_copy(we,wev,w_sem.at[1])]
    for cp in loads: cp.start()
    bar=pltpu.get_barrier_semaphore()
    pl.semaphore_signal(bar,inc=1,device_id=partner,device_id_type=MESH)
    pl.semaphore_wait(bar,1)
    def swap(i,s,d):
        return pltpu.make_async_remote_copy(src_ref=s,dst_ref=d,send_sem=s_sem.at[i],recv_sem=r_sem.at[i],device_id=partner,device_id_type=MESH)
    x_da,x_dh=swap(0,da_send,da_recv),swap(1,dh_send,dh_recv)
    lanes=lambda k,n:pl.ds(pl.multiple_of(k*n,128),n)
    rows=lambda base,k,n:pl.ds(pl.multiple_of(base+k*n,64),n)
    f32=lambda v:v.astype(jnp.float32)
    NT=FH//TF
    def loop(n,f):
        def body(k,_):
            f(k)
            return 0
        lax.fori_loop(0,n,body,0)
    loads[0].wait()
    def f(k): da_send[:,lanes(k,TF)]=dot_nt(g[...],wcv[rows(other*FH,k,TF),:]).astype(bf)
    loop(NT,f)
    x_da.start()
    def emit(i,stage,sem,dst,value):
        slot=i%2
        cp=pltpu.make_async_copy(stage.at[slot],dst,sem.at[slot])
        if i>=2: prev[slot].wait()
        stage[slot]=value
        cp.start(); prev[slot]=cp
    prev={}
    for i in range(2*NT):
        a,b,k=(a_own,c,i) if i<NT else (a_other,other,i-NT)
        emit(i,stage_c,c_sem,part_c.at[rows(b*FH,k,TF)],dot_tn(a[:,k*TF:k*TF+TF],g[...]).astype(bf))
    prev_c=prev
    x_da.wait_recv()
    def f(k):
        sl=lanes(k,TF)
        d=dot_nt(g[...],wcv[rows(c*FH,k,TF),:])+f32(da_recv[:,sl])
        p=pre[:,sl]
        t=jnp.tanh(GC*(p+0.044715*(p*p*p)))
        slope=0.5*(1.0+t)+p*(0.5*(1.0-t*t)*(GC*(1.0+(3*0.044715)*(p*p))))
        dp=(d*slope).astype(bf)
        dpre[:,sl]=dp
        dsum[:,sl]=jnp.sum(f32(dp),axis=0,keepdims=True)
    loop(NT,f)
    loads[1].wait()
    def f(k): dh_send[rows(0,k,448),:]=dot_nt(wev[rows(other*KH,k,448),:],dpre[...]).astype(bf)
    loop(2,f)
    x_dh.start()
    def f(k): dh2[rows(0,k,448),:]=dot_nt(wev[rows(c*KH,k,448),:],dpre[...])
    loop(2,f)
    prev={}
    for j in range(KP//256):
        emit(j,stage_e,e_sem,part_e.at[pl.ds(256*j,256)],dot(h2t[256*j:256*j+256,:],dpre[...]).astype(bf))
    br=dot(a_own[...],wcv[rows(c*FH,0,FH),:])+dot(a_other[...],wcv[rows(other*FH,0,FH),:])
    result[...]=(mid[...]+(br+cb[...])).astype(bf)
    x_dh.wait_recv()
    dh2[...]=dh2[...]+f32(dh_recv[...])
    for cp in list(prev.values())+list(prev_c.values()): cp.wait()
    for cp in (x_da,x_dh): cp.wait_send()
def mlp(h2t,we,wc,pre,a_own,a_other,mid,cb,g,cid=4):
    S=jax.ShapeDtypeStruct; f=jnp.float32; V=pltpu.VMEM
    return pl.pallas_call(mlp_kernel,
      out_shape=(S((TT,KH),bf),S((6400,KH),bf),S((KP,FH),bf),S((KH,TT),f),S((1,FH),f)),
      in_specs=[VM,ANY,ANY]+[VM]*6,out_specs=(VM,ANY,ANY,VM,VM),
      scratch_shapes=[V((KP,FH),bf),V((6400,KH),bf)]+[V((TT,FH),bf)]*3+[V((KH,TT),bf)]*2+[V((2,256,FH),bf),V((2,TF,KH),bf)]+[pltpu.SemaphoreType.DMA((n,)) for n in (2,2,2,2,2)],
      compiler_params=pltpu.CompilerParams(collective_id=cid,has_side_effects=True,vmem_limit_bytes=58<<20))(h2t,we,wc,pre,a_own,a_other,mid,cb,g)


def pad_rows(block):
    return jnp.pad(block, ((0, 6), (0, 0)))


def pad_columns(values):
    n = values.shape[0]
    return jnp.pad(values.reshape(n, 16, 50), ((0, 0), (0, 0), (0, 6))).reshape(n, KH)


def unpad_features(values):
    n = values.shape[0]
    return values.reshape(n, 16, 56)[:, :, :50].reshape(n, 800)


def per_device(
    tokens,
    segments,
    first_gain,
    first_bias,
    attention_in,
    attention_bias,
    attention_out,
    output_bias,
    second_gain,
    second_bias,
    expand_weight,
    expand_bias,
    contract_weight,
    contract_bias,
    cotangent,
):
    seqs, block_len, width = tokens.shape
    row_total = seqs * block_len
    grad_low = pad_columns(cotangent.reshape(row_total, width))
    grad_sums = jnp.sum(grad_low.astype(jnp.float32), axis=0)
    tokens_back = pad_columns(tokens.reshape(row_total, width)).T
    zeros = jnp.zeros_like(first_gain)
    small = jnp.concatenate(
        (second_gain, first_gain, zeros + 1.0, first_bias, second_bias, output_bias, contract_bias, zeros)
    )
    small = pad_columns(small.reshape(8, width))
    columns = small.T
    bias_three = jnp.concatenate((attention_bias[0], zeros, attention_bias[1]))
    kept, saved, gathered = attend(
        tokens_back,
        columns,
        bias_three[None],
        expand_bias[None],
        segments,
        "qeco",
        (
            jnp.pad(attention_in.reshape(50, 3 * width), ((0, 6), (0, 32))),
            pad_rows(expand_weight),
            pad_columns(contract_weight),
            pad_rows(pad_columns(attention_out)),
        ),
        1,
    )
    rows_attn, rows_one, normed_one, normed_two, recips, rows_two, middle, pre_gelu, gelu_own, gelu_other = saved
    weight_qkv = gathered[0].reshape(KP, QW)
    weight_expand = gathered[1].reshape(KP, 4 * width)
    weight_contract = gathered[2].reshape(4 * D, KH)
    weight_out = gathered[3].reshape(KP, KH)
    result, part_contract, part_expand, grad_two, expand_sums = mlp(
        rows_two.reshape(KP, row_total),
        weight_expand,
        weight_contract,
        pre_gelu,
        gelu_own,
        gelu_other,
        middle,
        small[6:7],
        grad_low,
        4,
    )
    result = unpad_features(result).reshape(tokens.shape)
    gradient_tokens, sum_out, sum_qkv, vector, (sum_expand, sum_contract) = attend_back(
        (
            grad_two,
            normed_two,
            grad_low.T,
            columns,
            jnp.stack((recips[1], recips[0])),
            rows_attn.reshape(KP, row_total),
            weight_out,
        ),
        kept,
        rows_one.reshape(KP, row_total),
        normed_one,
        jnp.concatenate((grad_sums, expand_sums[0])).reshape(32, 128),
        weight_qkv,
        "ec",
        (
            part_expand.reshape(4, 4, 2, 56, 4 * width),
            part_contract.reshape(4, 4, 2, 200, KH),
        ),
        2,
    )
    gradient_tokens = unpad_features(gradient_tokens.T).reshape(tokens.shape)
    padded = unpad_features(vector[:42].reshape(6, KH)).reshape(-1)
    sums = [padded[width * k : width * (k + 1)] for k in range(6)]
    qkv_sums = vector[67:86].reshape(-1)
    return (
        result,
        gradient_tokens,
        sums[0],
        sums[1],
        sum_qkv[:, : 3 * width].reshape(50, 3, width),
        jnp.concatenate((qkv_sums[:width], qkv_sums[2 * width : 3 * width])).reshape(2, width),
        unpad_features(sum_out),
        sums[4],
        sums[2],
        sums[3],
        sum_expand,
        vector[42:67].reshape(-1),
        unpad_features(sum_contract),
        sums[5],
    )


def solution(mesh):
    return jax.shard_map(
        per_device,
        mesh=mesh,
        in_specs=(
            P("dev", "row", "col"),
            P("dev", None),
            P("col"),
            P("col"),
            P("row", None, "col"),
            P(None, "col"),
            P("row", "col"),
            P("col"),
            P("col"),
            P("col"),
            P("row", "col"),
            P("col"),
            P("row", "col"),
            P("col"),
            P("dev", "row", "col"),
        ),
        out_specs=(
            P("dev", "row", "col"),
            P("dev", "row", "col"),
            P("col"),
            P("col"),
            P("row", None, "col"),
            P(None, "col"),
            P("row", "col"),
            P("col"),
            P("col"),
            P("col"),
            P("row", "col"),
            P("col"),
            P("row", "col"),
            P("col"),
        ),
        check_vma=False,
    )
```

```python
import functools

import jax
import jax.numpy as jnp
from jax import lax
from jax.experimental import pallas as pl
from jax.experimental.pallas import tpu as pltpu
from jax.sharding import PartitionSpec as P

MESH = pl.DeviceIdType.MESH
D = 1600
KP = 1792


def coords():
    d=lax.axis_index("dev"); r=lax.axis_index("row"); c=lax.axis_index("col")
    return r//8, (r//2)%4, d*2+r%2, c
def place(z,y,x,c):
    return (x//2, (z*4+y)*2+x%2, c)
def peer_of(ax,k):
    z,y,x,c=coords()
    if ax=="z": z=(z+k)%4
    if ax=="y": y=(y+k)%4
    if ax=="x": x=(x+k)%4
    return place(z,y,x,c)
def greet(peers):
    bar=pltpu.get_barrier_semaphore()
    for ax,k in peers: pl.semaphore_signal(bar,inc=1,device_id=peer_of(ax,k),device_id_type=MESH)
    pl.semaphore_wait(bar,len(peers))
SPLIT={"q":(4,4,6,5),"o":(2,1,2,2),"e":(7,4,7,7),"c":(1,2,2,2)}
ORD=("yzx","zyx","yxz","zxy")
GPEERS=[("z",1),("z",3),("z",2),("y",1),("y",3),("y",2),("x",1),("x",3)]
def cuts(name,W):
    out=[];p=0
    for n in SPLIT[name]:
        out.append((p,min(p+n*128,W))); p+=n*128
    assert out[-1][1]==W
    return out
def gather_steps(names,widths,src,dst,ss,rs,ls):
    n=len(names)
    z,y,x,c=coords(); xl=x%2
    cnt=[0]; allc=[]
    FULL=slice(None)
    LO=pl.ds(0,2); HI=pl.ds(2,2)
    def mk(s,d,ax,k):
        i=cnt[0]; cnt[0]+=1
        cp=pltpu.make_async_remote_copy(src_ref=s,dst_ref=d,send_sem=ss.at[i],recv_sem=rs.at[i],device_id=peer_of(ax,k),device_id_type=MESH)
        allc.append(cp); return cp
    cut=[cuts(nm,w) for nm,w in zip(names,widths)]
    def at(t,p,zi,yi,xi):
        a,b=cut[t][p]
        return dst[t].at[zi,yi,xi,:,pl.ds(a,b-a)]
    def wait(l):
        for cp in l: cp.wait_recv()
    def go(l):
        for cp in l: cp.start()
    loc=[pltpu.make_async_copy(src[t],dst[t].at[z,y,xl],ls.at[t]) for t in range(n)]
    st1=[[],[],[],[]]
    for t in range(n):
        for p in range(4):
            a,b=cut[t][p]
            for k in (1,3,2):
                st1[p].append(mk(src[t].at[:,pl.ds(a,b-a)],at(t,p,z,y,xl),ORD[p][0],k))
    def both(p,f):
        return [cp for t in range(n) for cp in f(t,p)]
    def xsend(zi,yi):
        return lambda t,p:[mk(at(t,p,*zi,xl),at(t,p,*zi,xl),"x",1),mk(at(t,p,*yi,xl),at(t,p,*yi,xl),"x",3)]
    def ring_a(ax,zi,yi,xi):
        return lambda t,p:[mk(at(t,p,zi,yi,xi),at(t,p,zi,yi,xi),ax,k) for k in (1,3)]
    def ring_b(ax,xi):
        def f(t,p):
            if ax=="z":
                u=at(t,p,(z+3)%4,LO,xi); v=at(t,p,(z+1)%4,HI,xi)
            else:
                u=at(t,p,LO,(y+3)%4,xi); v=at(t,p,HI,(y+1)%4,xi)
            return [mk(u,u,ax,1),mk(v,v,ax,3)]
        return f
    A2=both(0,ring_a("z",z,FULL,xl)); B2=both(1,ring_a("y",FULL,y,xl))
    C2=both(2,xsend((z,LO),(z,HI))); D2=both(3,xsend((LO,y),(HI,y)))
    A2b=both(0,ring_b("z",xl)); B2b=both(1,ring_b("y",xl))
    C3=both(2,ring_a("z",z,FULL,FULL)); D3=both(3,ring_a("y",FULL,y,FULL))
    A3=both(0,xsend((LO,FULL),(HI,FULL))); B3=both(1,xsend((LO,FULL),(HI,FULL)))
    C3b=both(2,ring_b("z",FULL)); D3b=both(3,ring_b("y",FULL))
    def f0():
        go(loc)
        for p in range(4): go(st1[p])
    def f1():
        wait_loc=[cp.wait() for cp in loc]
        wait(st1[0]); go(A2)
        wait(st1[1]); go(B2)
        wait(st1[2]); go(C2)
        wait(st1[3]); go(D2)
    def f2():
        wait(A2); go(A2b); wait(B2); go(B2b)
        wait(C2); go(C3); wait(D2); go(D3)
    def f3():
        wait(A2b); go(A3); wait(B2b); go(B3)
    def f4():
        wait(C3); go(C3b); wait(D3); go(D3b)
    def f5():
        wait(A3);wait(B3);wait(C3b);wait(D3b)
        for cp in allc: cp.wait_send()
    return [f0,f1,f2,f3,f4,f5]
def gather_sems(n):
    return [pltpu.SemaphoreType.DMA((36,)),pltpu.SemaphoreType.DMA((36,)),pltpu.SemaphoreType.DMA((1,))]*n
def gather_chains(names,widths,src,dst,sems):
    chains=[gather_steps(names[t],[widths[t]],[src[t]],[dst[t]],*sems[3*t:3*t+3]) for t in range(len(names))]
    def both(k):
        def f():
            for ch in chains: ch[k]()
        return f
    return [both(k) for k in range(6)]
def gather_kernel(names,widths,*refs):
    n=len(names)
    steps=gather_chains(names,widths,refs[:n],refs[n:2*n],refs[2*n:])
    greet(GPEERS)
    for f in steps: f()
def gather_shapes(arrs):
    return tuple(jax.ShapeDtypeStruct((4,4,2)+a.shape,a.dtype) for a in arrs)
def gather(names,arrs,cid=0):
    n=len(names)
    return pl.pallas_call(functools.partial(gather_kernel,names,[a.shape[1] for a in arrs]),
      out_shape=gather_shapes(arrs),
      in_specs=[pl.BlockSpec(memory_space=pl.ANY)]*n,out_specs=tuple([pl.BlockSpec(memory_space=pl.ANY)]*n),
      scratch_shapes=gather_sems(n),
      compiler_params=pltpu.CompilerParams(collective_id=cid,has_side_effects=True))(*arrs)


RSPLIT={"q":(6,7,6),"o":(2,3,2),"e":(10,7,8),"c":(2,3,2)}
AX=("xzy","yzx","zyx")
RPEERS=[(a,k) for a in "xyz" for k in (1,2,3)]
def rcuts(name,W):
    out=[];p=0
    for n in RSPLIT[name]:
        out.append((p,min(p+n*128,W))); p+=n*128
    assert out[-1][1]==W
    return out
def scatter_steps(nm,width,src,out,bufs,sems):
    ss,rs,ls=sems
    z,y,x,c=coords(); xl=x%2; xh=x//2
    me={"x":x,"y":y,"z":z}
    cnt=[0]; lcnt=[0]; allc=[]
    def mk(s,d,ax,k,keep=True):
        i=cnt[0]; cnt[0]+=1
        cp=pltpu.make_async_remote_copy(src_ref=s,dst_ref=d,send_sem=ss.at[i],recv_sem=rs.at[i],device_id=peer_of(ax,k),device_id_type=MESH)
        if keep: allc.append(cp)
        return cp
    def mkload(s,d):
        i=lcnt[0]; lcnt[0]+=1
        return pltpu.make_async_copy(s,d,ls.at[i])
    cut=rcuts(nm,width)
    f32=lambda a:a.astype(jnp.float32)
    def D(p,k,i=None):
        a,b=cut[p]; s=slice(None) if i is None else pl.ds(2*i,2)
        if p==0:
            h=(b-a)//2
            return src.at[s,:,k%2,:,pl.ds(pl.multiple_of(a+(k//2)*h,128),h)]
        if p==1: return src.at[s,k,:,:,pl.ds(a,b-a)]
        return src.at[k,s,:,:,pl.ds(a,b-a)]
    M=(4,2,2); P3=(0,1,2)
    ld={}; R={}
    for p in P3:
        own,rlp,rlm,rm,rp,rl2p,rl2m,rm2,rp2,out2,r3,r4=bufs[p]
        k=me[AX[p][0]]; ax=AX[p][0]
        bp=own.at[pl.ds(0,2)]; bm=own.at[pl.ds(2,2)]
        ld[p]=[mkload(D(p,(k+1)%4,0),bp),mkload(D(p,(k+3)%4,1),bm),mkload(D(p,k),own)]
        R[p,"a"]=[mk(D(p,(k+2)%4,0),rlp,ax,1),mk(D(p,(k+2)%4,1),rlm,ax,3)]
        R[p,"b"]=[mk(D(p,(k+1)%4,1),rm.at[pl.ds(2,2)],ax,1),mk(D(p,(k+3)%4,0),rp.at[pl.ds(0,2)],ax,3),
                  mk(bp,rm.at[pl.ds(0,2)],ax,1,False),mk(bm,rp.at[pl.ds(2,2)],ax,3,False)]
        m=M[p]; hm=m//2
        ax=AX[p][1]; k=me[ax]
        L=pl.ds(0,hm); H=pl.ds(hm,hm)
        R[p,"c"]=[mk(own.at[(k+2)%4,L],rl2p,ax,1),mk(own.at[(k+2)%4,H],rl2m,ax,3)]
        R[p,"d"]=[mk(own.at[(k+1)%4,H],rm2.at[H],ax,1),mk(own.at[(k+3)%4,L],rp2.at[L],ax,3),
                  mk(own.at[(k+1)%4,L],rm2.at[L],ax,1),mk(own.at[(k+3)%4,H],rp2.at[H],ax,3)]
        ax=AX[p][2]; k=me[ax]; q=4 if p==0 else 2
        R[p,"e"]=[mk(out2.at[(k+j)%q],r3.at[j-1],ax,j) for j in (1,2,3)]
        if p==0: R[p,"f"]=[mk(r4.at[xh],r4.at[xh],"x",2)]
    def addin(dst,other,cntn,f,g):
        def body(i,_):
            dst[f(i)]=(f32(dst[f(i)])+f32(other[g(i)])).astype(jnp.bfloat16)
            return 0
        lax.fori_loop(0,cntn,body,0)
    def first():
        for p in P3:
            for cp in ld[p][:2]: cp.start()
        for p in P3:
            for cp in R[p,"a"]: cp.start()
        for p in P3:
            for cp in R[p,"b"][:2]: cp.start()
    def relay(p):
        def f():
            own,rlp,rlm=bufs[p][:3]
            m=M[p]
            ld[p][0].wait(); R[p,"a"][0].wait_recv(); addin(own,rlp,2*m,lambda i:(i//m,i%m),lambda i:(i//m,i%m)); R[p,"b"][2].start()
            ld[p][1].wait(); R[p,"a"][1].wait_recv(); addin(own,rlm,2*m,lambda i:(2+i//m,i%m),lambda i:(i//m,i%m)); R[p,"b"][3].start()
        return f
    def reload(p):
        def f():
            for cp in R[p,"b"][2:]: cp.wait_send()
            ld[p][2].start()
        return f
    def sum1(p):
        def f():
            own,rm,rp=bufs[p][0],bufs[p][3],bufs[p][4]
            m=M[p]
            ld[p][2].wait()
            for cp in R[p,"b"]: cp.wait_recv()
            def body(i,_):
                j=(i//m,i%m)
                own[j]=(f32(own[j])+(f32(rm[j])+f32(rp[j]))).astype(jnp.bfloat16)
                return 0
            lax.fori_loop(0,4*m,body,0)
            for cp in R[p,"c"]: cp.start()
            for cp in R[p,"d"][:2]: cp.start()
        return f
    def relay2(p):
        def f():
            own,rl2p,rl2m=bufs[p][0],bufs[p][5],bufs[p][6]
            hm=M[p]//2; k=me[AX[p][1]]
            R[p,"c"][0].wait_recv()
            addin(own,rl2p,hm,lambda i:((k+1)%4,i),lambda i:i)
            R[p,"d"][2].start()
            R[p,"c"][1].wait_recv()
            addin(own,rl2m,hm,lambda i:((k+3)%4,hm+i),lambda i:i)
            R[p,"d"][3].start()
        return f
    def sum2(p):
        def f():
            own,rm2,rp2,out2=bufs[p][0],bufs[p][7],bufs[p][8],bufs[p][9]
            k=me[AX[p][1]]
            for cp in R[p,"d"]: cp.wait_recv()
            def body(i,_):
                out2[i]=(f32(own[k,i])+(f32(rm2[i])+f32(rp2[i]))).astype(jnp.bfloat16)
                return 0
            lax.fori_loop(0,M[p],body,0)
            for cp in R[p,"e"]: cp.start()
        return f
    def last(p):
        def f():
            out2,r3,r4=bufs[p][9:12]
            a,b=cut[p]
            for cp in R[p,"e"]: cp.wait_recv()
            k=me[AX[p][2]] if p==0 else xl
            s=(f32(out2[k])+f32(r3[1]))+(f32(r3[0])+f32(r3[2]))
            if p==0:
                r4[xh]=s.astype(jnp.bfloat16)
                R[p,"f"][0].start()
            else:
                out[:,pl.ds(a,b-a)]=s[0:out.shape[0],:]
        return f
    def end():
        a,b=cut[0]; h=(b-a)//2; r4=bufs[0][11]
        R[0,"f"][0].wait_recv()
        for j in range(2): out[:,pl.ds(a+j*h,h)]=f32(r4[j])[0:out.shape[0],:]
        for cp in allc: cp.wait_send()
    return [[first]]+[[f(p) for p in P3] for f in (relay,reload,sum1,relay2,sum2,last)]+[[end]]
STAGES=8
def staggered(chains,by):
    return [[f for i,ch in enumerate(chains) if 0<=tick-by*i<STAGES for f in ch[tick-by*i]] for tick in range(STAGES+by*(len(chains)-1))]
def scatter_bufs(nm,r,w):
    scr=[]
    for p,(a,b) in enumerate(rcuts(nm,w)):
        m=4 if p==0 else 2; v=(b-a)//2 if p==0 else b-a; hm=m//2
        B=lambda *s:pltpu.VMEM(s+(r,v),jnp.bfloat16)
        scr+=[B(4,m),B(2,m),B(2,m),B(4,m),B(4,m),B(hm),B(hm),B(m),B(m),B(m),B(3),B(2) if p==0 else pltpu.VMEM((8,128),jnp.bfloat16)]
    return scr
def scatter_sems():
    return [pltpu.SemaphoreType.DMA((46,)),pltpu.SemaphoreType.DMA((46,)),pltpu.SemaphoreType.DMA((9,))]
def by_part(refs):
    return [refs[12*p:12*p+12] for p in range(3)]
def narrowed(bufs,nm,w):
    out=[]
    for p,(a,b) in enumerate(rcuts(nm,w)):
        v=(b-a)//2 if p==0 else b-a
        out.append([ref if ref.shape[-1]==v or ref.shape==(8,128) else ref.at[(slice(None),)*(len(ref.shape)-1)+(pl.ds(0,v),)] for ref in bufs[p]])
    return out
def vector_steps(vbuf,sems):
    z,y,x,c=coords(); me=(x,y,z)
    ss,rs=sems
    R=[[pltpu.make_async_remote_copy(src_ref=vbuf[st].at[me[st]],dst_ref=vbuf[st].at[me[st]],send_sem=ss.at[3*st+k-1],recv_sem=rs.at[3*st+k-1],device_id=peer_of("xyz"[st],k),device_id_type=MESH) for k in (1,2,3)] for st in range(3)]
    def go(st,v):
        vbuf[st][pl.ds(me[st],1)]=v[None]
        for cp in R[st]: cp.start()
    def total(st):
        for cp in R[st]: cp.wait_recv()
        b=vbuf[st]
        return (b[0]+b[1])+(b[2]+b[3])
    def end():
        for l in R:
            for cp in l: cp.wait_send()
    return go,total,end


TT=256; KH=896; HD=64; LEN=4096; NEG=-1e30; ROWS=32
FQ,FK,BQ,BK=1024,1024,512,512
def dot(a,b): return lax.dot_general(a,b,(((1,),(0,)),((),())),preferred_element_type=jnp.float32)
def dot_nt(a,b): return lax.dot_general(a,b,(((1,),(1,)),((),())),preferred_element_type=jnp.float32)
def group_greet(d,r,c,across):
    bar=pltpu.get_barrier_semaphore()
    for rr in across: pl.semaphore_signal(bar,inc=1,device_id=(1-d,rr,c),device_id_type=MESH)
    def body(i,_):
        @pl.when(i!=r*2+c)
        def _():
            pl.semaphore_signal(bar,inc=1,device_id=(d,i//2,i%2),device_id_type=MESH)
        return 0
    lax.fori_loop(0,2*ROWS,body,0)
def group_wait(across):
    pl.semaphore_wait(pltpu.get_barrier_semaphore(),2*ROWS-1+across)
def push(src,dst,send_sem,recv_sem,same,target):
    @pl.when(same)
    def _():
        pltpu.make_async_copy(src,dst,recv_sem).start()
    @pl.when(jnp.logical_not(same))
    def _():
        pltpu.make_async_remote_copy(src_ref=src,dst_ref=dst,send_sem=send_sem,recv_sem=recv_sem,device_id=target,device_id_type=MESH).start()
def pushed(src,dst,send_sem,recv_sem,same,target):
    @pl.when(jnp.logical_not(same))
    def _():
        pltpu.make_async_remote_copy(src_ref=src,dst_ref=dst,send_sem=send_sem,recv_sem=recv_sem,device_id=target,device_id_type=MESH).wait_send()
def arrived(ref,sem):
    pltpu.make_async_copy(ref,ref,sem).wait()
def steps(text):
    return [text[k:k+2] for k in range(0,len(text),2)]
FWD_BEFORE=steps("q1o0q2e1q3o1q4e2q5")
FWD_LOAD=steps("c0e3o2")
FWD_PROJ=steps("c1o3")
FWD_SENT=steps("e4c2o4")
FWD_AT=((1,"c3"),)
FWD_THEN=steps("o5e5")
FWD_LATE=steps("c4")
FWD_END=steps("c5")
QW=2432
GC=0.7978845608028654
def dot_tn(a,b): return lax.dot_general(a,b,(((0,),(0,)),((),())),preferred_element_type=jnp.float32)
def attn_fwd_kernel(names,widths,*refs):
    it=iter(refs)
    take=lambda n:[next(it) for _ in range(n)]
    n=len(names)
    xt,cols,bias,eb,segs=take(5)
    src=take(n)
    qkv_out,oT,lse,start,op,h1t,norm1t,norm2t,recips,h2t,mid,pre,a_own,a_other=take(14)
    dst=take(n)
    o_recv,qkv,knt,obf,wv,wov,acc,pt,of,mt,stat_s,stat_r,s_in,s_out,r_in,r_out,l_sem,w_sem,x_sem=take(19)
    chains={nm:gather_steps(nm,[widths[t]],[src[t]],[dst[t]],*take(3)) for t,nm in enumerate(names)}
    def run(which):
        for k in which: chains[k[0]][int(k[1])]()
    d=lax.axis_index("dev"); r=lax.axis_index("row"); c=lax.axis_index("col")
    partner=(d,r,1-c)
    def swap(k,s,t):
        cp=pltpu.make_async_remote_copy(src_ref=s,dst_ref=t,send_sem=x_sem.at[2*k],recv_sem=x_sem.at[2*k+1],device_id=partner,device_id_type=MESH)
        cp.start()
        return cp
    def norm(k,v,gain,shift,normed,hidden):
        stat_s[k,0:1,:]=jnp.sum(v,axis=0,keepdims=True)
        stat_s[k,1:2,:]=jnp.sum(v*v,axis=0,keepdims=True)
        swap(2*k,stat_s.at[k],stat_r.at[k]).wait()
        m=(stat_s[k,0:1,:]+stat_r[k,0:1,:])*(1.0/D)
        recip=lax.rsqrt((stat_s[k,1:2,:]+stat_r[k,1:2,:])*(1.0/D)-m*m+1e-5)
        xhat=(v-m)*recip
        normed[...]=xhat
        recips[k:k+1,:]=recip
        own=pl.ds(pl.multiple_of(16*c,16),16)
        hidden[own]=(xhat*gain+shift).reshape(16,56,TT).astype(bf)
        return swap(2*k+1,hidden.at[own],hidden.at[own])
    group_greet(d,r,c,[r+1-2*(r%2)])
    acc[...]=jnp.broadcast_to(bias[...],acc.shape)
    pre[...]=jnp.broadcast_to(eb[...],pre.shape)
    seg=jnp.broadcast_to(jnp.where(r%2==0,segs[0:1,:],segs[1:2,:]),(8,LEN))
    pos=lax.broadcasted_iota(jnp.int32,(8,LEN),1)
    first=jnp.where((seg!=pltpu.roll(seg,1,1))&(pos>0),pos,0)
    for k in range(12):
        first=jnp.maximum(first,jnp.where(pos>=2**k,pltpu.roll(first,2**k,1),0))
    start[...]=first[0:1,:]
    group_wait(1)
    run(["q0","e0"])
    sent=norm(0,xt[...].astype(jnp.float32),cols[:,1:2],cols[:,3:4],norm1t,h1t)
    run(FWD_BEFORE)
    wq=wv.at[:,:,:,:,pl.ds(0,QW)]
    load=pltpu.make_async_copy(dst[0],wq,w_sem.at[0])
    load.start()
    run(FWD_LOAD)
    sent.wait()
    load.wait()
    def over_blocks(total,tile,hidden,weight):
        n=total.shape[1]
        def body(k,_):
            hk=jnp.concatenate([hidden[4*k+b] for b in range(4)],axis=0)
            for a0 in range(0,n,tile):
                sl=pl.ds(a0,min(tile,n-a0))
                wk=jnp.concatenate([weight[k//2,(k%2)*2+b//2,b%2,:,sl] for b in range(4)],axis=0)
                total[:,sl]+=dot_tn(hk,wk)
            return 0
        lax.fori_loop(0,8,body,0)
    over_blocks(acc,512,h1t,wv)
    run(FWD_PROJ)
    for a0 in range(0,2400,128):
        piece=acc[:,a0:min(a0+128,2400)].T.astype(bf)
        at=a0
        while at<min(a0+128,2400):
            t=at//800; end=min(a0+128,2400,(t+1)*800)
            pt[t,at-800*t:end-800*t,:]=piece[at-a0:end-a0]
            at=end
    lanes=pl.ds(pl.multiple_of(r*128,128),128)
    def full(fn):
        def body(k,_):
            i=(r+k)%24
            fn(pt.at[:,pl.ds(pl.multiple_of(64*(i//2)+32*c,32),64),pl.ds(pl.multiple_of((i%2)*128,128),128)],qkv.at[:,:,lanes],s_in.at[i],r_in,i==r,(d,i,c))
            return 0
        lax.fori_loop(0,24,body,0)
    def halves(fn):
        rows=pl.ds(pl.multiple_of(32*c,32),32)
        for s in range(2):
            fn(pt.at[:,pl.ds(pl.multiple_of(768*(1-c),32),32),pl.ds(s*128,128)],qkv.at[:,rows,lanes],s_in.at[24+s],r_in,(r==24+s)&(c==0),(d,24+s,0))
    full(push); halves(push)
    run(FWD_SENT)
    item=(r<24)|((c==0)&(r<26))
    head=r//2+13*c; seq=r%2
    def outs(qi,fn):
        def body(i,_):
            rr=qi*(FQ//128)+(r+i)%(FQ//128)
            fn(obf.at[:,pl.ds(pl.multiple_of(rr*128,128),128)],o_recv.at[seq,head],s_out.at[rr],r_out,rr==r,(d,rr,c))
            return 0
        lax.fori_loop(0,FQ//128,body,0)
    save=pltpu.make_async_copy(qkv,qkv_out,l_sem)
    @pl.when(item)
    def _():
        arrived(qkv,r_in)
        save.start()
        for a in range(LEN//512):
            sl=pl.ds(a*512,512)
            knt[sl,:]=qkv[1,:,sl].T
    def qloop(qi,_):
        @pl.when(item)
        def _():
            iota=lax.broadcasted_iota(jnp.int32,(FK,FQ),0)
            iotl=lax.broadcasted_iota(jnp.int32,(FK,FQ),1)
            qs=pl.ds(pl.multiple_of(qi*FQ,FQ),FQ)
            q=qkv[0,:,qs]*jnp.bfloat16(0.125)
            st=start[:,qs]
            def step(kj,carry,diag):
                m,l,acc=carry
                ks=pl.ds(pl.multiple_of(kj*FK,FK),FK)
                s=dot(knt[ks,:],q)
                ok=iota>=(st-kj*FK)
                if diag: ok=ok&(iota<=iotl)
                s=jnp.where(ok,s,NEG)
                mn=jnp.maximum(m,jnp.max(s,axis=0,keepdims=True))
                p=jnp.exp(s-mn)
                al=jnp.exp(m-mn)
                l=l*al+jnp.sum(p,axis=0,keepdims=True)
                acc=acc*al+dot(qkv[2,:,ks],p.astype(jnp.bfloat16))
                return mn,l,acc
            carry=(jnp.full((1,FQ),NEG,jnp.float32),jnp.zeros((1,FQ),jnp.float32),jnp.zeros((HD,FQ),jnp.float32))
            carry=lax.fori_loop(0,qi,lambda kj,cr:step(kj,cr,False),carry)
            m,l,acc=step(qi,carry,True)
            o=acc/l
            oT[:,qs]=o
            lse[:,qs]=m+jnp.log(l)
            obf[:,qs]=o.astype(jnp.bfloat16)
            outs(qi,push)
        for at,k in FWD_AT:
            pl.when(qi==at)(functools.partial(run,steps(k)))
        return 0
    lax.fori_loop(0,LEN//FQ,qloop,0)
    run(FWD_THEN)
    loads=[pltpu.make_async_copy(dst[3],wov,w_sem.at[0]),pltpu.make_async_copy(dst[1],wv,w_sem.at[1])]
    for cp in loads: cp.start()
    shares=[o_recv.at[:,pl.ds(0,13)],o_recv.at[:,pl.ds(13,12)]]
    def hand_over(mine):
        arrived(shares[mine],r_out)
        give=pltpu.make_async_remote_copy(src_ref=shares[mine],dst_ref=shares[mine],send_sem=x_sem.at[10],recv_sem=x_sem.at[11],device_id=partner,device_id_type=MESH)
        give.start()
        arrived(shares[1-mine],x_sem.at[11])
        give.wait_send()
    pl.when(c==0)(lambda:hand_over(0))
    pl.when(c==1)(lambda:hand_over(1))
    for s in range(2): of[:,pl.ds(128*s,128)]=o_recv[s].reshape(1600,128).astype(jnp.float32)
    for k in range(ROWS):
        op[k,0:50,:]=of[50*k:50*k+50,:].astype(bf)
        op[k,50:56,:]=jnp.zeros((6,TT),bf)
    loads[0].wait()
    mid[...]=jnp.zeros_like(mid)
    over_blocks(mid,512,op,wov)
    run(FWD_LATE)
    for k in range(7):
        sl=pl.ds(128*k,128)
        mt[sl,:]=mid[:,sl].T+cols[sl,5:6]+xt[sl,:].astype(jnp.float32)
        mid[:,sl]=(mt[sl,:]+cols[sl,6:7]).T
    norm(1,mt[...],cols[:,0:1],cols[:,4:5],norm2t,h2t).wait()
    loads[1].wait()
    over_blocks(pre,640,h2t,wv)
    for a0 in range(0,3200,640):
        p=pre[:,a0:a0+640]
        a_own[:,a0:a0+640]=(p*(0.5*(1.0+jnp.tanh(GC*(p+0.044715*(p*p*p)))))).astype(bf)
    sent=swap(4,a_own,a_other)
    run(FWD_END)
    sent.wait()
    @pl.when(item)
    def _():
        save.wait()
        for qi in range(LEN//FQ): outs(qi,pushed)
    full(pushed); halves(pushed)
BWD_START="e0"
BWD_MID="e1o0c0"
BWD_AT=((0,"e2o1"),(1,"c1e3"),(2,"o2"),(3,"e4c2o3"),(4,"c3"),(5,"e5o4"),(6,"c4e6"),(7,"o5"))
BWD_THEN="e7"
BWD_LAST="q0c5**o6q1c6q2o7--q3c7q4q5++q6q7"
BR=224
KQ=2432
def unpad_rows(dst,v):
    for g in range(16): dst[50*g:50*g+50,:]=v[56*g:56*g+50,:]
def token_sums(v):
    if v.dtype==bf: return lax.dot_general(jnp.ones((8,TT),bf),v,(((1,),(1,)),((),())),preferred_element_type=jnp.float32)[:1]
    v=v[:,:128]+v[:,128:]
    return jnp.concatenate([jnp.sum(v[128*k:128*k+128,:].T,axis=0,keepdims=True) for k in range(v.shape[0]//128)],axis=1)
def back_kernel(names,widths,*refs):
    it=iter(refs)
    take=lambda n:[next(it) for _ in range(n)]
    n=len(names)
    dh2t,norm2t,gt,cols,recips,op,wo,qkv,oT,start,lse,h1t,normt,vec_in,wq=take(15)
    parts=take(n)
    part_o,part_q,gtok,sum_o,sum_q,vec_out=take(6)
    sums=take(n)
    doT,knt,vnt,dqa,delta,dout,dq,stage,wblk,dh_send,dh_recv,do_recv,lhs,nbuf,dh,gmid,gat,dflat,dot_,stat_s,stat_r=take(21)
    vbuf=take(3); vtmp=next(it)
    s_in,s_out,r_in,r_out,q_sem,w_sem,x_sem,l_sem,free=take(9)
    v_sems=take(2)
    chains={}
    for t in range(n):
        b=by_part(take(36))
        if t==0: first_bufs=b
        chains[names[t]]=scatter_steps(names[t],widths[t],parts[t],sums[t],b,take(3))
    chains["o"]=scatter_steps("o",KH,part_o,sum_o,by_part(take(36)),take(3))
    chains["q"]=scatter_steps("q",KQ,part_q,sum_q,narrowed(first_bufs,"q",KQ),take(3))
    def run(which):
        for k in steps(which):
            for f in chains[k[0]][int(k[1])]: f()
    v_go,v_total,v_end=vector_steps(vbuf,v_sems)
    d=lax.axis_index("dev"); r=lax.axis_index("row"); c=lax.axis_index("col")
    partner=(d,r,1-c)
    item=(r<24)|((c==0)&(r<26))
    loads=[pltpu.make_async_copy(s,t,l_sem.at[k]) for k,(s,t) in enumerate(((dh2t,dh),(norm2t,nbuf),(op,lhs),(normt,nbuf),(h1t,lhs)))]
    for cp in loads[:3]: cp.start()
    group_greet(d,r,c,[r+1-2*(r%2),r])
    @pl.when(item)
    def _():
        for a in range(LEN//512):
            sl=pl.ds(a*512,512)
            knt[sl,:]=qkv[1,:,sl].T
            vnt[sl,:]=qkv[2,:,sl].T
        dqa[...]=jnp.zeros_like(dqa)
    stage[...]=jnp.zeros_like(stage)
    vtmp[...]=jnp.zeros_like(vtmp)
    def vec_rows(at,row):
        for k in range(row.shape[1]//128): vtmp[pl.ds(at+k,1),:]=row[:,128*k:128*k+128]
    def norm_back(k,incoming,normed,gain,recip):
        e=incoming*gain
        stat_s[k,0:1,:]=jnp.sum(e,axis=0,keepdims=True)
        stat_s[k,1:2,:]=jnp.sum(e*normed,axis=0,keepdims=True)
        cp=pltpu.make_async_remote_copy(src_ref=stat_s.at[k],dst_ref=stat_r.at[k],send_sem=x_sem.at[2*k],recv_sem=x_sem.at[2*k+1],device_id=partner,device_id_type=MESH)
        cp.start()
        cp.wait()
        s1=stat_s[k,0:1,:]+stat_r[k,0:1,:]
        s2=stat_s[k,1:2,:]+stat_r[k,1:2,:]
        return recip*(e-s1*(1.0/D)-normed*(s2*(1.0/D)))
    group_wait(2)
    run(BWD_START)
    loads[0].wait(); loads[1].wait()
    vec_rows(14,token_sums(dh[...]*nbuf[...]))
    vec_rows(21,token_sums(dh[...]))
    gmid[...]=(gt[...].astype(jnp.float32)+norm_back(0,dh[...],nbuf[...],cols[:,0:1],recips[1:2,:]))*cols[:,2:3]
    gat[...]=gmid[...].astype(bf)
    vec_rows(28,token_sums(gat[...]))
    vec_rows(35,token_sums(gt[...]))
    vec_rows(42,vec_in[...])
    loads[3].start()
    half=lambda w,base,k:w.at[pl.ds(pl.multiple_of(base*KH+BR*k,32),BR)]
    nb=KH//BR
    def pair_product(w,wide,rhs,recv,sem):
        blocks=[half(w,1-c,k) for k in range(nb)]+[half(w,c,k) for k in range(nb)]
        slot=lambda k:wblk.at[k%2,:,pl.ds(0,wide)] if wide<QW else wblk.at[k%2]
        ld=[pltpu.make_async_copy(blocks[k],slot(k),w_sem.at[k%2]) for k in range(2*nb)]
        ld[0].start(); ld[1].start()
        swap=pltpu.make_async_remote_copy(src_ref=dh_send,dst_ref=recv,send_sem=x_sem.at[sem],recv_sem=x_sem.at[sem+1],device_id=partner,device_id_type=MESH)
        for k in range(2*nb):
            ld[k].wait()
            v=dot(wblk[k%2,:,0:rhs.shape[0]],rhs)
            if k<nb: dh_send[pl.ds(BR*k,BR),:]=v.astype(bf)
            else: dh[pl.ds(BR*(k-nb),BR),:]=v
            if k<2*nb-2: ld[k+2].start()
            if k==nb-1: swap.start()
        return swap
    swap=pair_product(wo,KH,gat[...],do_recv,4)
    swap.wait()
    unpad_rows(dflat,dh[...]+do_recv[...].astype(jnp.float32))
    dot_[...]=dflat[...].astype(bf)
    lanes=pl.ds(pl.multiple_of(r*128,128),128)
    def full(fn):
        def body(k,_):
            i=(r+k)%24
            fn(dot_.at[pl.ds(pl.multiple_of(64*(i//2)+32*c,32),64),pl.ds(pl.multiple_of((i%2)*128,128),128)],doT.at[:,lanes],s_in.at[i],r_in,i==r,(d,i,c))
            return 0
        lax.fori_loop(0,24,body,0)
    def halves(fn):
        rows=pl.ds(pl.multiple_of(32*c,32),32)
        for s in range(2):
            fn(dot_.at[pl.ds(pl.multiple_of(768*(1-c),32),32),pl.ds(s*128,128)],doT.at[rows,lanes],s_in.at[24+s],r_in,(r==24+s)&(c==0),(d,24+s,0))
    full(push); halves(push)
    def emit(part,cols_,rhs):
        prev={}
        for b in range(8):
            slot=b%2
            if b>=2: prev[slot].wait()
            stage[slot,:,:,:,0:cols_]=dot_nt(lhs[pl.ds(224*b,224),:],rhs).reshape(2,2,56,cols_).astype(bf)
            src=stage.at[slot] if cols_==2400 else stage.at[slot,:,:,:,pl.ds(0,cols_)]
            prev[slot]=pltpu.make_async_copy(src,part.at[b//2,pl.ds(2*(b%2),2)],q_sem.at[slot])
            prev[slot].start()
        return prev
    loads[2].wait()
    for cp in emit(part_o,KH,gat[...]).values(): cp.wait()
    loads[4].start()
    run(BWD_MID)
    def outs(fn):
        seq=pl.ds(pl.multiple_of((r%2)*128,128),128)
        @pl.when(r<24)
        def _():
            def body(k,_):
                i=(r+k)%ROWS
                fn(dout.at[:,:,pl.ds(pl.multiple_of(i*128,128),128)],dq.at[:,pl.ds(pl.multiple_of(64*(r//2)+32*c,32),64),seq],s_out.at[i],r_out,i==r,(d,i,c))
                return 0
            lax.fori_loop(0,ROWS,body,0)
        @pl.when(r>=24)
        def _():
            def body(k,_):
                rr=(r+k//2)%ROWS; cc=k%2
                fn(dout.at[:,pl.ds(pl.multiple_of(32*cc,32),32),pl.ds(pl.multiple_of(rr*128,128),128)],dq.at[:,pl.ds(pl.multiple_of(768*(1-cc),32),32),seq],s_out.at[2*rr+cc],r_out,(rr==r)&(cc==c),(d,rr,cc))
                return 0
            lax.fori_loop(0,2*ROWS,body,0)
    @pl.when(item)
    def _():
        arrived(doT,r_in)
        for a in range(LEN//512):
            sl=pl.ds(a*512,512)
            delta[:,sl]=jnp.sum(oT[:,sl]*doT[:,sl].astype(jnp.float32),axis=0,keepdims=True)
    def kloop(kj,_):
        @pl.when(item)
        def _():
            iota=lax.broadcasted_iota(jnp.int32,(BK,BQ),0)
            iotl=lax.broadcasted_iota(jnp.int32,(BK,BQ),1)
            ks=pl.ds(pl.multiple_of(kj*BK,BK),BK)
            kn=knt[ks,:]; vn=vnt[ks,:]; kT=qkv[1,:,ks]
            def step(qi,carry,diag):
                dk,dv=carry
                qs=pl.ds(pl.multiple_of(qi*BQ,BQ),BQ)
                q=qkv[0,:,qs]*jnp.bfloat16(0.125)
                do=doT[:,qs]
                s=dot(kn,q)
                ok=iota>=(start[:,qs]-kj*BK)
                if diag: ok=ok&(iota<=iotl)
                p=jnp.exp(jnp.where(ok,s,NEG)-lse[:,qs])
                dp=dot(vn,do)
                ds=(p*(dp-delta[:,qs])).astype(jnp.bfloat16)
                dv=dv+dot_nt(do,p.astype(jnp.bfloat16))
                dk=dk+dot_nt(q,ds)
                dqa[:,qs]+=dot(kT,ds)
                return dk,dv
            z=jnp.zeros((HD,BK),jnp.float32)
            carry=step(kj,(z,z),True)
            dk,dv=lax.fori_loop(kj+1,LEN//BQ,lambda qi,cr:step(qi,cr,False),carry)
            dout[1,:,ks]=dk.astype(jnp.bfloat16)
            dout[2,:,ks]=dv.astype(jnp.bfloat16)
        for step,which in BWD_AT:
            pl.when(kj==step)(functools.partial(run,which))
        return 0
    lax.fori_loop(0,LEN//BK,kloop,0)
    @pl.when(item)
    def _():
        for a in range(LEN//512):
            sl=pl.ds(a*512,512)
            dout[0,:,sl]=(dqa[:,sl]*0.125).astype(jnp.bfloat16)
        outs(push)
    run(BWD_THEN)
    for ax,k in RPEERS: pl.semaphore_signal(free,inc=1,device_id=peer_of(ax,k),device_id_type=MESH)
    arrived(dq,r_out)
    grads=dq[...].reshape(2400,TT)
    loads[4].wait()
    for cp in emit(part_q,2400,grads).values(): cp.wait()
    pl.semaphore_wait(free,len(RPEERS))
    def late_product():
        chains["swap"]=pair_product(wq,QW,grads,dh_recv,6)
    def late_norm():
        chains["swap"].wait()
        dh[...]=dh[...]+dh_recv[...].astype(jnp.float32)
        loads[3].wait()
        vec_rows(0,token_sums(dh[...]*nbuf[...]))
        vec_rows(7,token_sums(dh[...]))
        vec_rows(67,jnp.concatenate((token_sums(grads),jnp.zeros((1,32),jnp.float32)),axis=1))
        v_go(0,vtmp[...])
        gtok[...]=(gmid[...]+norm_back(1,dh[...],nbuf[...],cols[:,1:2],recips[0:1,:])).astype(bf)
        v_go(1,v_total(0))
    def late_vec():
        v_go(2,v_total(1))
    for k in steps(BWD_LAST):
        if k=="**": late_product()
        elif k=="--": late_norm()
        elif k=="++": late_vec()
        else: run(k)
    vec_out[...]=v_total(2)
    v_end()
    pl.when(item)(lambda:outs(pushed))
    full(pushed); halves(pushed)
VM=pl.BlockSpec(memory_space=pltpu.VMEM); ANY=pl.BlockSpec(memory_space=pl.ANY)
bf=jnp.bfloat16
def attend(xt,cols,bias,eb,segs,names,arrs,cid=1):
    S=jax.ShapeDtypeStruct; n=len(names); V=pltpu.VMEM; DM=pltpu.SemaphoreType.DMA; f=jnp.float32
    FH=eb.shape[1]
    out=pl.pallas_call(functools.partial(attn_fwd_kernel,names,[a.shape[1] for a in arrs]),
      out_shape=(S((3,HD,LEN),bf),S((HD,LEN),f),S((1,LEN),f),S((1,LEN),jnp.int32),S((32,56,TT),bf),S((32,56,TT),bf),S((KH,TT),f),S((KH,TT),f),S((8,TT),f),S((32,56,TT),bf),
        S((TT,KH),f),S((TT,FH),f),S((TT,FH),bf),S((TT,FH),bf))+gather_shapes(arrs),
      in_specs=[VM]*5+[ANY]*n,out_specs=(ANY,)+(VM,)*12+(ANY,)+(ANY,)*n,
      scratch_shapes=[V((2,25,HD,128),bf),V((3,HD,LEN),bf),V((LEN,HD),bf),V((HD,LEN),bf),V((4,4,2,56,FH),bf),V((4,4,2,56,KH),bf),V((TT,2400),f),V((3,800,TT),bf),V((1600,TT),f),V((KH,TT),f),
        V((2,8,TT),f),V((2,8,TT),f),DM((26,)),DM((32,)),DM,DM,DM,DM((2,)),DM((12,))]+gather_sems(n),
      compiler_params=pltpu.CompilerParams(collective_id=cid,has_side_effects=True,vmem_limit_bytes=62<<20))(xt,cols,bias,eb,segs,*arrs)
    return out[:4],out[4:14],out[14:]
def attend_back(front,kept,h1t,normt,vec,wq,names,parts,cid=2):
    S=jax.ShapeDtypeStruct; n=len(names); f=jnp.float32; V=pltpu.VMEM; DM=pltpu.SemaphoreType.DMA
    qkv,oT,lse,start=kept
    rows=88
    out=pl.pallas_call(functools.partial(back_kernel,names,[a.shape[4] for a in parts]),
      out_shape=(S((4,4,2,56,KH),bf),S((4,4,2,56,KQ),bf),S((KH,TT),bf),S((50,KH),f),S((50,KQ),f),S((rows,128),f))+tuple(S((50 if a.shape[3]==56 else a.shape[3],a.shape[4]),f) for a in parts),
      in_specs=[ANY,ANY,VM,VM,VM,ANY,ANY,VM,VM,VM,VM,ANY,ANY,VM]+[ANY]*(1+n),out_specs=(ANY,ANY,VM,VM,VM,VM)+(VM,)*n,
      scratch_shapes=[V((HD,LEN),bf),V((LEN,HD),bf),V((LEN,HD),bf),V((HD,LEN),f),V((1,LEN),f),V((3,HD,LEN),bf),
        V((3,800,TT),bf),V((2,2,2,56,KQ),bf),V((2,BR,QW),bf),V((KH,TT),bf),V((KH,TT),bf),V((KH,TT),bf),V((KP,TT),bf),
        V((KH,TT),f),V((KH,TT),f),V((KH,TT),f),V((KH,TT),bf),V((800,TT),f),V((800,TT),bf),V((2,8,TT),f),V((2,8,TT),f)]+[V((4,rows,128),f)]*3+[V((rows,128),f)]+
        [DM((26,)),DM((64,)),DM,DM,DM((2,)),DM((2,)),DM((8,)),DM((5,)),pltpu.SemaphoreType.REGULAR,DM((9,)),DM((9,))]+
        sum([scatter_bufs(nm,*a.shape[3:])+scatter_sems() for nm,a in zip(names,parts)],[])+scatter_bufs("o",56,KH)+scatter_sems()*2,
      compiler_params=pltpu.CompilerParams(collective_id=cid,has_side_effects=True,vmem_limit_bytes=VMEM_BACK))(*front,qkv,oT,start,lse,h1t,normt,vec,wq,*parts)
    return out[2],out[3],out[4],out[5],out[6:]
VMEM_BACK=63<<20


FH=3200; TF=640
def mlp_kernel(h2t,we,wc,pre,a_own,a_other,mid,g,result,part_c,part_e,dh2,dsum,
        wev,wcv,da_send,da_recv,dpre,dh_send,dh_recv,stage_e,stage_c,w_sem,s_sem,r_sem,e_sem,c_sem):
    c=lax.axis_index("col"); other=1-c
    partner=(lax.axis_index("dev"),lax.axis_index("row"),other)
    loads=[pltpu.make_async_copy(wc,wcv,w_sem.at[0]),pltpu.make_async_copy(we,wev,w_sem.at[1])]
    for cp in loads: cp.start()
    bar=pltpu.get_barrier_semaphore()
    pl.semaphore_signal(bar,inc=1,device_id=partner,device_id_type=MESH)
    pl.semaphore_wait(bar,1)
    def swap(i,s,d):
        return pltpu.make_async_remote_copy(src_ref=s,dst_ref=d,send_sem=s_sem.at[i],recv_sem=r_sem.at[i],device_id=partner,device_id_type=MESH)
    x_da,x_dh=swap(0,da_send,da_recv),swap(1,dh_send,dh_recv)
    lanes=lambda k,n:pl.ds(pl.multiple_of(k*n,128),n)
    rows=lambda base,k,n:pl.ds(pl.multiple_of(base+k*n,64),n)
    f32=lambda v:v.astype(jnp.float32)
    NT=FH//TF
    def loop(n,f):
        def body(k,_):
            f(k)
            return 0
        lax.fori_loop(0,n,body,0)
    loads[0].wait()
    def f(k): da_send[:,lanes(k,TF)]=dot_nt(g[...],wcv[rows(other*FH,k,TF),:]).astype(bf)
    loop(NT,f)
    x_da.start()
    def emit(i,stage,sem,dst,value):
        slot=i%2
        cp=pltpu.make_async_copy(stage.at[slot],dst,sem.at[slot])
        if i>=2: prev[slot].wait()
        stage[slot]=value
        cp.start(); prev[slot]=cp
    prev={}
    for i in range(2*NT):
        a,b,k=(a_own,c,i) if i<NT else (a_other,other,i-NT)
        emit(i,stage_c,c_sem,part_c.at[rows(b*FH,k,TF)],dot_tn(a[:,k*TF:k*TF+TF],g[...]).astype(bf))
    prev_c=prev
    x_da.wait_recv()
    def f(k):
        sl=lanes(k,TF)
        d=dot_nt(g[...],wcv[rows(c*FH,k,TF),:])+f32(da_recv[:,sl])
        p=pre[:,sl]
        t=jnp.tanh(GC*(p+0.044715*(p*p*p)))
        slope=0.5*(1.0+t)+p*(0.5*(1.0-t*t)*(GC*(1.0+(3*0.044715)*(p*p))))
        dp=(d*slope).astype(bf)
        dpre[:,sl]=dp
        dsum[:,sl]=jnp.sum(f32(dp),axis=0,keepdims=True)
    loop(NT,f)
    loads[1].wait()
    def f(k): dh_send[rows(0,k,448),:]=dot_nt(wev[rows(other*KH,k,448),:],dpre[...]).astype(bf)
    loop(2,f)
    x_dh.start()
    def f(k): dh2[rows(0,k,448),:]=dot_nt(wev[rows(c*KH,k,448),:],dpre[...])
    loop(2,f)
    prev={}
    for j in range(KP//256):
        emit(j,stage_e,e_sem,part_e.at[pl.ds(256*j,256)],dot(h2t[256*j:256*j+256,:],dpre[...]).astype(bf))
    br=dot(a_own[...],wcv[rows(c*FH,0,FH),:])+dot(a_other[...],wcv[rows(other*FH,0,FH),:])
    result[...]=(mid[...]+br).astype(bf)
    x_dh.wait_recv()
    dh2[...]=dh2[...]+f32(dh_recv[...])
    for cp in list(prev.values())+list(prev_c.values()): cp.wait()
    for cp in (x_da,x_dh): cp.wait_send()
def mlp(h2t,we,wc,pre,a_own,a_other,mid,g,cid=4):
    S=jax.ShapeDtypeStruct; f=jnp.float32; V=pltpu.VMEM
    return pl.pallas_call(mlp_kernel,
      out_shape=(S((TT,KH),bf),S((6400,KH),bf),S((KP,FH),bf),S((KH,TT),f),S((1,FH),f)),
      in_specs=[VM,ANY,ANY]+[VM]*5,out_specs=(VM,ANY,ANY,VM,VM),
      scratch_shapes=[V((KP,FH),bf),V((6400,KH),bf)]+[V((TT,FH),bf)]*3+[V((KH,TT),bf)]*2+[V((2,256,FH),bf),V((2,TF,KH),bf)]+[pltpu.SemaphoreType.DMA((n,)) for n in (2,2,2,2,2)],
      compiler_params=pltpu.CompilerParams(collective_id=cid,has_side_effects=True,vmem_limit_bytes=58<<20))(h2t,we,wc,pre,a_own,a_other,mid,g)


def pad_rows(block):
    return jnp.pad(block, ((0, 6), (0, 0)))


def pad_columns(values):
    n = values.shape[0]
    return jnp.pad(values.reshape(n, 16, 50), ((0, 0), (0, 0), (0, 6))).reshape(n, KH)


def unpad_features(values):
    n = values.shape[0]
    return values.reshape(n, 16, 56)[:, :, :50].reshape(n, 800)


def per_device(
    tokens,
    segments,
    first_gain,
    first_bias,
    attention_in,
    attention_bias,
    attention_out,
    output_bias,
    second_gain,
    second_bias,
    expand_weight,
    expand_bias,
    contract_weight,
    contract_bias,
    cotangent,
):
    seqs, block_len, width = tokens.shape
    row_total = seqs * block_len
    grad_low = pad_columns(cotangent.reshape(row_total, width))
    tokens_back = pad_columns(tokens.reshape(row_total, width)).T
    zeros = jnp.zeros_like(first_gain)
    small = jnp.concatenate(
        (second_gain, first_gain, zeros + 1.0, first_bias, second_bias, output_bias, contract_bias, zeros)
    )
    columns = pad_columns(small.reshape(8, width)).T
    bias_three = jnp.concatenate((attention_bias[0], zeros, attention_bias[1]))
    kept, saved, gathered = attend(
        tokens_back,
        columns,
        bias_three[None],
        expand_bias[None],
        segments,
        "qeco",
        (
            jnp.pad(attention_in.reshape(50, 3 * width), ((0, 6), (0, 32))),
            pad_rows(expand_weight),
            pad_columns(contract_weight),
            pad_rows(pad_columns(attention_out)),
        ),
        1,
    )
    rows_attn, rows_one, normed_one, normed_two, recips, rows_two, middle, pre_gelu, gelu_own, gelu_other = saved
    weight_qkv = gathered[0].reshape(KP, QW)
    weight_expand = gathered[1].reshape(KP, 4 * width)
    weight_contract = gathered[2].reshape(4 * D, KH)
    weight_out = gathered[3].reshape(KP, KH)
    result, part_contract, part_expand, grad_two, expand_sums = mlp(
        rows_two.reshape(KP, row_total),
        weight_expand,
        weight_contract,
        pre_gelu,
        gelu_own,
        gelu_other,
        middle,
        grad_low,
        4,
    )
    result = unpad_features(result).reshape(tokens.shape)
    gradient_tokens, sum_out, sum_qkv, vector, (sum_expand, sum_contract) = attend_back(
        (
            grad_two,
            normed_two,
            grad_low.T,
            columns,
            recips,
            rows_attn.reshape(KP, row_total),
            weight_out,
        ),
        kept,
        rows_one.reshape(KP, row_total),
        normed_one,
        expand_sums,
        weight_qkv,
        "ec",
        (
            part_expand.reshape(4, 4, 2, 56, 4 * width),
            part_contract.reshape(4, 4, 2, 200, KH),
        ),
        2,
    )
    gradient_tokens = unpad_features(gradient_tokens.T).reshape(tokens.shape)
    padded = unpad_features(vector[:42].reshape(6, KH)).reshape(-1)
    sums = [padded[width * k : width * (k + 1)] for k in range(6)]
    qkv_sums = vector[67:86].reshape(-1)
    return (
        result,
        gradient_tokens,
        sums[0],
        sums[1],
        sum_qkv[:, : 3 * width].reshape(50, 3, width),
        jnp.concatenate((qkv_sums[:width], qkv_sums[2 * width : 3 * width])).reshape(2, width),
        unpad_features(sum_out),
        sums[4],
        sums[2],
        sums[3],
        sum_expand,
        vector[42:67].reshape(-1),
        unpad_features(sum_contract),
        sums[5],
    )


def solution(mesh):
    return jax.shard_map(
        per_device,
        mesh=mesh,
        in_specs=(
            P("dev", "row", "col"),
            P("dev", None),
            P("col"),
            P("col"),
            P("row", None, "col"),
            P(None, "col"),
            P("row", "col"),
            P("col"),
            P("col"),
            P("col"),
            P("row", "col"),
            P("col"),
            P("row", "col"),
            P("col"),
            P("dev", "row", "col"),
        ),
        out_specs=(
            P("dev", "row", "col"),
            P("dev", "row", "col"),
            P("col"),
            P("col"),
            P("row", None, "col"),
            P(None, "col"),
            P("row", "col"),
            P("col"),
            P("col"),
            P("col"),
            P("row", "col"),
            P("col"),
            P("row", "col"),
            P("col"),
        ),
        check_vma=False,
    )
```

```python
import functools

import jax
import jax.numpy as jnp
from jax import lax
from jax.experimental import pallas as pl
from jax.experimental.pallas import tpu as pltpu
from jax.sharding import PartitionSpec as P

MESH = pl.DeviceIdType.MESH
D = 1600
KP = 1792


def coords():
    d=lax.axis_index("dev"); r=lax.axis_index("row"); c=lax.axis_index("col")
    return r//8, (r//2)%4, d*2+r%2, c
def place(z,y,x,c):
    return (x//2, (z*4+y)*2+x%2, c)
def peer_of(ax,k):
    z,y,x,c=coords()
    if ax=="z": z=(z+k)%4
    if ax=="y": y=(y+k)%4
    if ax=="x": x=(x+k)%4
    return place(z,y,x,c)
def greet(peers):
    bar=pltpu.get_barrier_semaphore()
    for ax,k in peers: pl.semaphore_signal(bar,inc=1,device_id=peer_of(ax,k),device_id_type=MESH)
    pl.semaphore_wait(bar,len(peers))
SPLIT={"q":(4,4,6,5),"o":(2,1,2,2),"e":(7,4,7,7),"c":(1,2,2,2)}
ORD=("yzx","zyx","yxz","zxy")
GPEERS=[("z",1),("z",3),("z",2),("y",1),("y",3),("y",2),("x",1),("x",3)]
def cuts(name,W):
    out=[];p=0
    for n in SPLIT[name]:
        out.append((p,min(p+n*128,W))); p+=n*128
    assert out[-1][1]==W
    return out
def gather_steps(names,widths,src,dst,ss,rs,ls):
    n=len(names)
    z,y,x,c=coords(); xl=x%2
    cnt=[0]; allc=[]
    FULL=slice(None)
    LO=pl.ds(0,2); HI=pl.ds(2,2)
    def mk(s,d,ax,k):
        i=cnt[0]; cnt[0]+=1
        cp=pltpu.make_async_remote_copy(src_ref=s,dst_ref=d,send_sem=ss.at[i],recv_sem=rs.at[i],device_id=peer_of(ax,k),device_id_type=MESH)
        allc.append(cp); return cp
    cut=[cuts(nm,w) for nm,w in zip(names,widths)]
    def at(t,p,zi,yi,xi):
        a,b=cut[t][p]
        return dst[t].at[zi,yi,xi,:,pl.ds(a,b-a)]
    def wait(l):
        for cp in l: cp.wait_recv()
    def go(l):
        for cp in l: cp.start()
    loc=[pltpu.make_async_copy(src[t],dst[t].at[z,y,xl],ls.at[t]) for t in range(n)]
    st1=[[],[],[],[]]
    for t in range(n):
        for p in range(4):
            a,b=cut[t][p]
            for k in (1,3,2):
                st1[p].append(mk(src[t].at[:,pl.ds(a,b-a)],at(t,p,z,y,xl),ORD[p][0],k))
    def both(p,f):
        return [cp for t in range(n) for cp in f(t,p)]
    def xsend(zi,yi):
        return lambda t,p:[mk(at(t,p,*zi,xl),at(t,p,*zi,xl),"x",1),mk(at(t,p,*yi,xl),at(t,p,*yi,xl),"x",3)]
    def ring_a(ax,zi,yi,xi):
        return lambda t,p:[mk(at(t,p,zi,yi,xi),at(t,p,zi,yi,xi),ax,k) for k in (1,3)]
    def ring_b(ax,xi):
        def f(t,p):
            if ax=="z":
                u=at(t,p,(z+3)%4,LO,xi); v=at(t,p,(z+1)%4,HI,xi)
            else:
                u=at(t,p,LO,(y+3)%4,xi); v=at(t,p,HI,(y+1)%4,xi)
            return [mk(u,u,ax,1),mk(v,v,ax,3)]
        return f
    A2=both(0,ring_a("z",z,FULL,xl)); B2=both(1,ring_a("y",FULL,y,xl))
    C2=both(2,xsend((z,LO),(z,HI))); D2=both(3,xsend((LO,y),(HI,y)))
    A2b=both(0,ring_b("z",xl)); B2b=both(1,ring_b("y",xl))
    C3=both(2,ring_a("z",z,FULL,FULL)); D3=both(3,ring_a("y",FULL,y,FULL))
    A3=both(0,xsend((LO,FULL),(HI,FULL))); B3=both(1,xsend((LO,FULL),(HI,FULL)))
    C3b=both(2,ring_b("z",FULL)); D3b=both(3,ring_b("y",FULL))
    def f0():
        go(loc)
        for p in range(4): go(st1[p])
    def f1():
        wait_loc=[cp.wait() for cp in loc]
        wait(st1[0]); go(A2)
        wait(st1[1]); go(B2)
        wait(st1[2]); go(C2)
        wait(st1[3]); go(D2)
    def f2():
        wait(A2); go(A2b); wait(B2); go(B2b)
        wait(C2); go(C3); wait(D2); go(D3)
    def f3():
        wait(A2b); go(A3); wait(B2b); go(B3)
    def f4():
        wait(C3); go(C3b); wait(D3); go(D3b)
    def f5():
        wait(A3);wait(B3);wait(C3b);wait(D3b)
        for cp in allc: cp.wait_send()
    return [f0,f1,f2,f3,f4,f5]
def gather_sems(n):
    return [pltpu.SemaphoreType.DMA((36,)),pltpu.SemaphoreType.DMA((36,)),pltpu.SemaphoreType.DMA((1,))]*n
def gather_chains(names,widths,src,dst,sems):
    chains=[gather_steps(names[t],[widths[t]],[src[t]],[dst[t]],*sems[3*t:3*t+3]) for t in range(len(names))]
    def both(k):
        def f():
            for ch in chains: ch[k]()
        return f
    return [both(k) for k in range(6)]
def gather_kernel(names,widths,*refs):
    n=len(names)
    steps=gather_chains(names,widths,refs[:n],refs[n:2*n],refs[2*n:])
    greet(GPEERS)
    for f in steps: f()
def gather_shapes(arrs):
    return tuple(jax.ShapeDtypeStruct((4,4,2)+a.shape,a.dtype) for a in arrs)
def gather(names,arrs,cid=0):
    n=len(names)
    return pl.pallas_call(functools.partial(gather_kernel,names,[a.shape[1] for a in arrs]),
      out_shape=gather_shapes(arrs),
      in_specs=[pl.BlockSpec(memory_space=pl.ANY)]*n,out_specs=tuple([pl.BlockSpec(memory_space=pl.ANY)]*n),
      scratch_shapes=gather_sems(n),
      compiler_params=pltpu.CompilerParams(collective_id=cid,has_side_effects=True))(*arrs)


RSPLIT={"q":(6,7,6),"o":(2,3,2),"e":(10,7,8),"c":(2,3,2)}
AX=("xzy","yzx","zyx")
RPEERS=[(a,k) for a in "xyz" for k in (1,2,3)]
def rcuts(name,W):
    out=[];p=0
    for n in RSPLIT[name]:
        out.append((p,min(p+n*128,W))); p+=n*128
    assert out[-1][1]==W
    return out
def scatter_steps(nm,width,src,out,bufs,sems):
    ss,rs,ls=sems
    z,y,x,c=coords(); xl=x%2; xh=x//2
    me={"x":x,"y":y,"z":z}
    cnt=[0]; lcnt=[0]; allc=[]
    def mk(s,d,ax,k,keep=True):
        i=cnt[0]; cnt[0]+=1
        cp=pltpu.make_async_remote_copy(src_ref=s,dst_ref=d,send_sem=ss.at[i],recv_sem=rs.at[i],device_id=peer_of(ax,k),device_id_type=MESH)
        if keep: allc.append(cp)
        return cp
    def mkload(s,d):
        i=lcnt[0]; lcnt[0]+=1
        return pltpu.make_async_copy(s,d,ls.at[i])
    cut=rcuts(nm,width)
    f32=lambda a:a.astype(jnp.float32)
    def D(p,k,i=None):
        a,b=cut[p]; s=slice(None) if i is None else pl.ds(2*i,2)
        if p==0:
            h=(b-a)//2
            return src.at[s,:,k%2,:,pl.ds(pl.multiple_of(a+(k//2)*h,128),h)]
        if p==1: return src.at[s,k,:,:,pl.ds(a,b-a)]
        return src.at[k,s,:,:,pl.ds(a,b-a)]
    M=(4,2,2); P3=(0,1,2)
    ld={}; R={}
    for p in P3:
        own,rlp,rlm,rm,rp,rl2p,rl2m,rm2,rp2,out2,r3,r4=bufs[p]
        k=me[AX[p][0]]; ax=AX[p][0]
        bp=own.at[pl.ds(0,2)]; bm=own.at[pl.ds(2,2)]
        ld[p]=[mkload(D(p,(k+1)%4,0),bp),mkload(D(p,(k+3)%4,1),bm),mkload(D(p,k),own)]
        R[p,"a"]=[mk(D(p,(k+2)%4,0),rlp,ax,1),mk(D(p,(k+2)%4,1),rlm,ax,3)]
        R[p,"b"]=[mk(D(p,(k+1)%4,1),rm.at[pl.ds(2,2)],ax,1),mk(D(p,(k+3)%4,0),rp.at[pl.ds(0,2)],ax,3),
                  mk(bp,rm.at[pl.ds(0,2)],ax,1,False),mk(bm,rp.at[pl.ds(2,2)],ax,3,False)]
        m=M[p]; hm=m//2
        ax=AX[p][1]; k=me[ax]
        L=pl.ds(0,hm); H=pl.ds(hm,hm)
        R[p,"c"]=[mk(own.at[(k+2)%4,L],rl2p,ax,1),mk(own.at[(k+2)%4,H],rl2m,ax,3)]
        R[p,"d"]=[mk(own.at[(k+1)%4,H],rm2.at[H],ax,1),mk(own.at[(k+3)%4,L],rp2.at[L],ax,3),
                  mk(own.at[(k+1)%4,L],rm2.at[L],ax,1),mk(own.at[(k+3)%4,H],rp2.at[H],ax,3)]
        ax=AX[p][2]; k=me[ax]; q=4 if p==0 else 2
        R[p,"e"]=[mk(out2.at[(k+j)%q],r3.at[j-1],ax,j) for j in (1,2,3)]
        if p==0: R[p,"f"]=[mk(r4.at[xh],r4.at[xh],"x",2)]
    def addin(dst,other,cntn,f,g):
        def body(i,_):
            dst[f(i)]=(f32(dst[f(i)])+f32(other[g(i)])).astype(jnp.bfloat16)
            return 0
        lax.fori_loop(0,cntn,body,0)
    def first():
        for p in P3:
            for cp in ld[p][:2]: cp.start()
        for p in P3:
            for cp in R[p,"a"]: cp.start()
        for p in P3:
            for cp in R[p,"b"][:2]: cp.start()
    def relay(p):
        def f():
            own,rlp,rlm=bufs[p][:3]
            m=M[p]
            ld[p][0].wait(); R[p,"a"][0].wait_recv(); addin(own,rlp,2*m,lambda i:(i//m,i%m),lambda i:(i//m,i%m)); R[p,"b"][2].start()
            ld[p][1].wait(); R[p,"a"][1].wait_recv(); addin(own,rlm,2*m,lambda i:(2+i//m,i%m),lambda i:(i//m,i%m)); R[p,"b"][3].start()
        return f
    def reload(p):
        def f():
            for cp in R[p,"b"][2:]: cp.wait_send()
            ld[p][2].start()
        return f
    def sum1(p):
        def f():
            own,rm,rp=bufs[p][0],bufs[p][3],bufs[p][4]
            m=M[p]
            ld[p][2].wait()
            for cp in R[p,"b"]: cp.wait_recv()
            def body(i,_):
                j=(i//m,i%m)
                own[j]=(f32(own[j])+(f32(rm[j])+f32(rp[j]))).astype(jnp.bfloat16)
                return 0
            lax.fori_loop(0,4*m,body,0)
            for cp in R[p,"c"]: cp.start()
            for cp in R[p,"d"][:2]: cp.start()
        return f
    def relay2(p):
        def f():
            own,rl2p,rl2m=bufs[p][0],bufs[p][5],bufs[p][6]
            hm=M[p]//2; k=me[AX[p][1]]
            R[p,"c"][0].wait_recv()
            addin(own,rl2p,hm,lambda i:((k+1)%4,i),lambda i:i)
            R[p,"d"][2].start()
            R[p,"c"][1].wait_recv()
            addin(own,rl2m,hm,lambda i:((k+3)%4,hm+i),lambda i:i)
            R[p,"d"][3].start()
        return f
    def sum2(p):
        def f():
            own,rm2,rp2,out2=bufs[p][0],bufs[p][7],bufs[p][8],bufs[p][9]
            k=me[AX[p][1]]
            for cp in R[p,"d"]: cp.wait_recv()
            def body(i,_):
                out2[i]=(f32(own[k,i])+(f32(rm2[i])+f32(rp2[i]))).astype(jnp.bfloat16)
                return 0
            lax.fori_loop(0,M[p],body,0)
            for cp in R[p,"e"]: cp.start()
        return f
    def last(p):
        def f():
            out2,r3,r4=bufs[p][9:12]
            a,b=cut[p]
            for cp in R[p,"e"]: cp.wait_recv()
            k=me[AX[p][2]] if p==0 else xl
            s=(f32(out2[k])+f32(r3[1]))+(f32(r3[0])+f32(r3[2]))
            if p==0:
                r4[xh]=s.astype(jnp.bfloat16)
                R[p,"f"][0].start()
            else:
                out[:,pl.ds(a,b-a)]=s[0:out.shape[0],:]
        return f
    def end():
        a,b=cut[0]; h=(b-a)//2; r4=bufs[0][11]
        R[0,"f"][0].wait_recv()
        for j in range(2): out[:,pl.ds(a+j*h,h)]=f32(r4[j])[0:out.shape[0],:]
        for cp in allc: cp.wait_send()
    return [[first]]+[[f(p) for p in P3] for f in (relay,reload,sum1,relay2,sum2,last)]+[[end]]
STAGES=8
def staggered(chains,by):
    return [[f for i,ch in enumerate(chains) if 0<=tick-by*i<STAGES for f in ch[tick-by*i]] for tick in range(STAGES+by*(len(chains)-1))]
def scatter_bufs(nm,r,w):
    scr=[]
    for p,(a,b) in enumerate(rcuts(nm,w)):
        m=4 if p==0 else 2; v=(b-a)//2 if p==0 else b-a; hm=m//2
        B=lambda *s:pltpu.VMEM(s+(r,v),jnp.bfloat16)
        scr+=[B(4,m),B(2,m),B(2,m),B(4,m),B(4,m),B(hm),B(hm),B(m),B(m),B(m),B(3),B(2) if p==0 else pltpu.VMEM((8,128),jnp.bfloat16)]
    return scr
def scatter_sems():
    return [pltpu.SemaphoreType.DMA((46,)),pltpu.SemaphoreType.DMA((46,)),pltpu.SemaphoreType.DMA((9,))]
def by_part(refs):
    return [refs[12*p:12*p+12] for p in range(3)]
def narrowed(bufs,nm,w):
    out=[]
    for p,(a,b) in enumerate(rcuts(nm,w)):
        v=(b-a)//2 if p==0 else b-a
        out.append([ref if ref.shape[-1]==v or ref.shape==(8,128) else ref.at[(slice(None),)*(len(ref.shape)-1)+(pl.ds(0,v),)] for ref in bufs[p]])
    return out
def vector_steps(vbuf,sems):
    z,y,x,c=coords(); me=(x,y,z)
    ss,rs=sems
    R=[[pltpu.make_async_remote_copy(src_ref=vbuf[st].at[me[st]],dst_ref=vbuf[st].at[me[st]],send_sem=ss.at[3*st+k-1],recv_sem=rs.at[3*st+k-1],device_id=peer_of("xyz"[st],k),device_id_type=MESH) for k in (1,2,3)] for st in range(3)]
    def go(st,v):
        vbuf[st][pl.ds(me[st],1)]=v[None]
        for cp in R[st]: cp.start()
    def total(st):
        for cp in R[st]: cp.wait_recv()
        b=vbuf[st]
        return (b[0]+b[1])+(b[2]+b[3])
    def end():
        for l in R:
            for cp in l: cp.wait_send()
    return go,total,end


TT=256; KH=896; HD=64; LEN=4096; NEG=-1e30; ROWS=32
FQ,FK,BQ,BK=1024,1024,512,512
def dot(a,b): return lax.dot_general(a,b,(((1,),(0,)),((),())),preferred_element_type=jnp.float32)
def dot_nt(a,b): return lax.dot_general(a,b,(((1,),(1,)),((),())),preferred_element_type=jnp.float32)
def group_greet(d,r,c,across):
    bar=pltpu.get_barrier_semaphore()
    def greet_one(*target):
        pl.semaphore_signal(bar,inc=1,device_id=target,device_id_type=MESH)
    for rr in across: greet_one(1-d,rr,c)
    greet_one(d,r,1-c)
    def column(i,_):
        greet_one(d,(r+i)%ROWS,c)
        return 0
    lax.fori_loop(1,ROWS,column,0)
    @pl.when(c==1)
    def _():
        greet_one(d,24,0); greet_one(d,25,0)
    @pl.when((c==0)&(r//2==12))
    def _():
        def other_column(i,_):
            greet_one(d,i,1)
            return 0
        lax.fori_loop(0,ROWS,other_column,0)
def group_wait(r,c,across):
    shared=(1-jnp.minimum(jnp.abs(r//2-12),1))*(1-c)
    pl.semaphore_wait(pltpu.get_barrier_semaphore(),ROWS+across+2*c+ROWS*shared)
def push(src,dst,send_sem,recv_sem,same,target):
    @pl.when(same)
    def _():
        pltpu.make_async_copy(src,dst,recv_sem).start()
    @pl.when(jnp.logical_not(same))
    def _():
        pltpu.make_async_remote_copy(src_ref=src,dst_ref=dst,send_sem=send_sem,recv_sem=recv_sem,device_id=target,device_id_type=MESH).start()
def pushed(src,dst,send_sem,recv_sem,same,target):
    @pl.when(jnp.logical_not(same))
    def _():
        pltpu.make_async_remote_copy(src_ref=src,dst_ref=dst,send_sem=send_sem,recv_sem=recv_sem,device_id=target,device_id_type=MESH).wait_send()
def arrived(ref,sem):
    pltpu.make_async_copy(ref,ref,sem).wait()
def steps(text):
    return [text[k:k+2] for k in range(0,len(text),2)]
FWD_BEFORE=steps("q1o0q2e1q3o1q4e2q5")
FWD_LOAD=steps("c0e3o2")
FWD_PROJ=steps("c1o3")
FWD_SENT=steps("e4c2o4")
FWD_AT=((1,"c3"),)
FWD_THEN=steps("o5e5")
FWD_LATE=steps("c4")
FWD_END=steps("c5")
QW=2432
GC=0.7978845608028654
def dot_tn(a,b): return lax.dot_general(a,b,(((0,),(0,)),((),())),preferred_element_type=jnp.float32)
def attn_fwd_kernel(names,widths,*refs):
    it=iter(refs)
    take=lambda n:[next(it) for _ in range(n)]
    n=len(names)
    xt,cols,bias,eb,segs=take(5)
    src=take(n)
    qkv_out,oT,lse,start,op,h1t,norm1t,norm2t,recips,h2t,mid,pre,a_own,a_other=take(14)
    dst=take(n)
    o_recv,qkv,knt,obf,wv,wov,acc,pt,of,mt,stat_s,stat_r,s_in,s_out,r_in,r_out,l_sem,w_sem,x_sem=take(19)
    chains={nm:gather_steps(nm,[widths[t]],[src[t]],[dst[t]],*take(3)) for t,nm in enumerate(names)}
    def run(which):
        for k in which: chains[k[0]][int(k[1])]()
    d=lax.axis_index("dev"); r=lax.axis_index("row"); c=lax.axis_index("col")
    partner=(d,r,1-c)
    def swap(k,s,t):
        cp=pltpu.make_async_remote_copy(src_ref=s,dst_ref=t,send_sem=x_sem.at[2*k],recv_sem=x_sem.at[2*k+1],device_id=partner,device_id_type=MESH)
        cp.start()
        return cp
    def norm(k,v,gain,shift,normed,hidden):
        stat_s[k,0:1,:]=jnp.sum(v,axis=0,keepdims=True)
        stat_s[k,1:2,:]=jnp.sum(v*v,axis=0,keepdims=True)
        swap(2*k,stat_s.at[k],stat_r.at[k]).wait()
        m=(stat_s[k,0:1,:]+stat_r[k,0:1,:])*(1.0/D)
        recip=lax.rsqrt((stat_s[k,1:2,:]+stat_r[k,1:2,:])*(1.0/D)-m*m+1e-5)
        xhat=(v-m)*recip
        normed[...]=xhat
        recips[k:k+1,:]=recip
        own=pl.ds(pl.multiple_of(16*c,16),16)
        hidden[own]=(xhat*gain+shift).reshape(16,56,TT).astype(bf)
        return swap(2*k+1,hidden.at[own],hidden.at[own])
    group_greet(d,r,c,[r+1-2*(r%2)])
    acc[...]=jnp.broadcast_to(bias[...],acc.shape)
    pre[...]=jnp.broadcast_to(eb[...],pre.shape)
    seg=jnp.broadcast_to(jnp.where(r%2==0,segs[0:1,:],segs[1:2,:]),(8,LEN))
    pos=lax.broadcasted_iota(jnp.int32,(8,LEN),1)
    first=jnp.where((seg!=pltpu.roll(seg,1,1))&(pos>0),pos,0)
    for k in range(12):
        first=jnp.maximum(first,jnp.where(pos>=2**k,pltpu.roll(first,2**k,1),0))
    start[...]=first[0:1,:]
    group_wait(r,c,1)
    run(["q0","e0"])
    sent=norm(0,xt[...].astype(jnp.float32),cols[:,1:2],cols[:,3:4],norm1t,h1t)
    run(FWD_BEFORE)
    wq=wv.at[:,:,:,:,pl.ds(0,QW)]
    load=pltpu.make_async_copy(dst[0],wq,w_sem.at[0])
    load.start()
    run(FWD_LOAD)
    sent.wait()
    load.wait()
    def over_blocks(total,tile,hidden,weight):
        n=total.shape[1]
        def body(k,_):
            hk=jnp.concatenate([hidden[4*k+b] for b in range(4)],axis=0)
            for a0 in range(0,n,tile):
                sl=pl.ds(a0,min(tile,n-a0))
                wk=jnp.concatenate([weight[k//2,(k%2)*2+b//2,b%2,:,sl] for b in range(4)],axis=0)
                total[:,sl]+=dot_tn(hk,wk)
            return 0
        lax.fori_loop(0,8,body,0)
    over_blocks(acc,512,h1t,wv)
    run(FWD_PROJ)
    for a0 in range(0,2400,128):
        piece=acc[:,a0:min(a0+128,2400)].T.astype(bf)
        at=a0
        while at<min(a0+128,2400):
            t=at//800; end=min(a0+128,2400,(t+1)*800)
            pt[t,at-800*t:end-800*t,:]=piece[at-a0:end-a0]
            at=end
    lanes=pl.ds(pl.multiple_of(r*128,128),128)
    def full(fn):
        def body(k,_):
            i=(r+k)%24
            fn(pt.at[:,pl.ds(pl.multiple_of(64*(i//2)+32*c,32),64),pl.ds(pl.multiple_of((i%2)*128,128),128)],qkv.at[:,:,lanes],s_in.at[i],r_in,i==r,(d,i,c))
            return 0
        lax.fori_loop(0,24,body,0)
    def halves(fn):
        rows=pl.ds(pl.multiple_of(32*c,32),32)
        for s in range(2):
            fn(pt.at[:,pl.ds(pl.multiple_of(768*(1-c),32),32),pl.ds(s*128,128)],qkv.at[:,rows,lanes],s_in.at[24+s],r_in,(r==24+s)&(c==0),(d,24+s,0))
    full(push); halves(push)
    run(FWD_SENT)
    item=(r<24)|((c==0)&(r<26))
    head=r//2+13*c; seq=r%2
    def outs(qi,fn):
        def body(i,_):
            rr=qi*(FQ//128)+(r+i)%(FQ//128)
            fn(obf.at[:,pl.ds(pl.multiple_of(rr*128,128),128)],o_recv.at[seq,head],s_out.at[rr],r_out,rr==r,(d,rr,c))
            return 0
        lax.fori_loop(0,FQ//128,body,0)
    save=pltpu.make_async_copy(qkv,qkv_out,l_sem)
    @pl.when(item)
    def _():
        arrived(qkv,r_in)
        save.start()
        for a in range(LEN//512):
            sl=pl.ds(a*512,512)
            knt[sl,:]=qkv[1,:,sl].T
    def qloop(qi,_):
        @pl.when(item)
        def _():
            iota=lax.broadcasted_iota(jnp.int32,(FK,FQ),0)
            iotl=lax.broadcasted_iota(jnp.int32,(FK,FQ),1)
            qs=pl.ds(pl.multiple_of(qi*FQ,FQ),FQ)
            q=qkv[0,:,qs]*jnp.bfloat16(0.125)
            st=start[:,qs]
            def step(kj,carry,diag):
                m,l,acc=carry
                ks=pl.ds(pl.multiple_of(kj*FK,FK),FK)
                s=dot(knt[ks,:],q)
                ok=iota>=(st-kj*FK)
                if diag: ok=ok&(iota<=iotl)
                s=jnp.where(ok,s,NEG)
                mn=jnp.maximum(m,jnp.max(s,axis=0,keepdims=True))
                p=jnp.exp(s-mn)
                al=jnp.exp(m-mn)
                l=l*al+jnp.sum(p,axis=0,keepdims=True)
                acc=acc*al+dot(qkv[2,:,ks],p.astype(jnp.bfloat16))
                return mn,l,acc
            carry=(jnp.full((1,FQ),NEG,jnp.float32),jnp.zeros((1,FQ),jnp.float32),jnp.zeros((HD,FQ),jnp.float32))
            carry=lax.fori_loop(0,qi,lambda kj,cr:step(kj,cr,False),carry)
            m,l,acc=step(qi,carry,True)
            o=acc/l
            oT[:,qs]=o
            lse[:,qs]=m+jnp.log(l)
            obf[:,qs]=o.astype(jnp.bfloat16)
            outs(qi,push)
        for at,k in FWD_AT:
            pl.when(qi==at)(functools.partial(run,steps(k)))
        return 0
    lax.fori_loop(0,LEN//FQ,qloop,0)
    run(FWD_THEN)
    loads=[pltpu.make_async_copy(dst[3],wov,w_sem.at[0]),pltpu.make_async_copy(dst[1],wv,w_sem.at[1])]
    for cp in loads: cp.start()
    shares=[o_recv.at[:,pl.ds(0,13)],o_recv.at[:,pl.ds(13,12)]]
    def hand_over(mine):
        arrived(shares[mine],r_out)
        give=pltpu.make_async_remote_copy(src_ref=shares[mine],dst_ref=shares[mine],send_sem=x_sem.at[10],recv_sem=x_sem.at[11],device_id=partner,device_id_type=MESH)
        give.start()
        arrived(shares[1-mine],x_sem.at[11])
        give.wait_send()
    pl.when(c==0)(lambda:hand_over(0))
    pl.when(c==1)(lambda:hand_over(1))
    for s in range(2): of[:,pl.ds(128*s,128)]=o_recv[s].reshape(1600,128).astype(jnp.float32)
    for k in range(ROWS):
        op[k,0:50,:]=of[50*k:50*k+50,:].astype(bf)
        op[k,50:56,:]=jnp.zeros((6,TT),bf)
    loads[0].wait()
    mid[...]=jnp.zeros_like(mid)
    over_blocks(mid,512,op,wov)
    run(FWD_LATE)
    for k in range(7):
        sl=pl.ds(128*k,128)
        mt[sl,:]=mid[:,sl].T+cols[sl,5:6]+xt[sl,:].astype(jnp.float32)
        mid[:,sl]=(mt[sl,:]+cols[sl,6:7]).T
    norm(1,mt[...],cols[:,0:1],cols[:,4:5],norm2t,h2t).wait()
    loads[1].wait()
    over_blocks(pre,640,h2t,wv)
    for a0 in range(0,3200,640):
        p=pre[:,a0:a0+640]
        a_own[:,a0:a0+640]=(p*(0.5*(1.0+jnp.tanh(GC*(p+0.044715*(p*p*p)))))).astype(bf)
    sent=swap(4,a_own,a_other)
    run(FWD_END)
    sent.wait()
    @pl.when(item)
    def _():
        save.wait()
        for qi in range(LEN//FQ): outs(qi,pushed)
    full(pushed); halves(pushed)
BWD_START="e0"
BWD_MID="e1o0c0"
BWD_AT=((0,"e2o1"),(1,"c1e3"),(2,"o2"),(3,"e4c2o3"),(4,"c3"),(5,"e5o4"),(6,"c4e6"),(7,"o5"))
BWD_THEN="e7"
BWD_LAST="q0c5**o6q1c6q2o7--q3c7q4q5++q6q7"
BR=224
KQ=2432
def unpad_rows(dst,v):
    for g in range(16): dst[50*g:50*g+50,:]=v[56*g:56*g+50,:]
def token_sums(v):
    if v.dtype==bf: return lax.dot_general(jnp.ones((8,TT),bf),v,(((1,),(1,)),((),())),preferred_element_type=jnp.float32)[:1]
    v=v[:,:128]+v[:,128:]
    return jnp.concatenate([jnp.sum(v[128*k:128*k+128,:].T,axis=0,keepdims=True) for k in range(v.shape[0]//128)],axis=1)
def back_kernel(names,widths,*refs):
    it=iter(refs)
    take=lambda n:[next(it) for _ in range(n)]
    n=len(names)
    dh2t,norm2t,gt,cols,recips,op,wo,qkv,oT,start,lse,h1t,normt,vec_in,wq=take(15)
    parts=take(n)
    part_o,part_q,gtok,sum_o,sum_q,vec_out=take(6)
    sums=take(n)
    doT,knt,vnt,dqa,delta,dout,dq,stage,wblk,dh_send,dh_recv,do_recv,lhs,nbuf,dh,gmid,gat,dflat,dot_,stat_s,stat_r=take(21)
    vbuf=take(3); vtmp=next(it)
    s_in,s_out,r_in,r_out,q_sem,w_sem,x_sem,l_sem,free=take(9)
    v_sems=take(2)
    chains={}
    for t in range(n):
        b=by_part(take(36))
        if t==0: first_bufs=b
        chains[names[t]]=scatter_steps(names[t],widths[t],parts[t],sums[t],b,take(3))
    chains["o"]=scatter_steps("o",KH,part_o,sum_o,by_part(take(36)),take(3))
    chains["q"]=scatter_steps("q",KQ,part_q,sum_q,narrowed(first_bufs,"q",KQ),take(3))
    def run(which):
        for k in steps(which):
            for f in chains[k[0]][int(k[1])]: f()
    v_go,v_total,v_end=vector_steps(vbuf,v_sems)
    d=lax.axis_index("dev"); r=lax.axis_index("row"); c=lax.axis_index("col")
    partner=(d,r,1-c)
    item=(r<24)|((c==0)&(r<26))
    loads=[pltpu.make_async_copy(s,t,l_sem.at[k]) for k,(s,t) in enumerate(((dh2t,dh),(norm2t,nbuf),(op,lhs),(normt,nbuf),(h1t,lhs)))]
    for cp in loads[:3]: cp.start()
    group_greet(d,r,c,[r+1-2*(r%2),r])
    @pl.when(item)
    def _():
        for a in range(LEN//512):
            sl=pl.ds(a*512,512)
            knt[sl,:]=qkv[1,:,sl].T
            vnt[sl,:]=qkv[2,:,sl].T
        dqa[...]=jnp.zeros_like(dqa)
    stage[...]=jnp.zeros_like(stage)
    vtmp[...]=jnp.zeros_like(vtmp)
    def vec_rows(at,row):
        for k in range(row.shape[1]//128): vtmp[pl.ds(at+k,1),:]=row[:,128*k:128*k+128]
    def norm_back(k,incoming,normed,gain,recip):
        e=incoming*gain
        stat_s[k,0:1,:]=jnp.sum(e,axis=0,keepdims=True)
        stat_s[k,1:2,:]=jnp.sum(e*normed,axis=0,keepdims=True)
        cp=pltpu.make_async_remote_copy(src_ref=stat_s.at[k],dst_ref=stat_r.at[k],send_sem=x_sem.at[2*k],recv_sem=x_sem.at[2*k+1],device_id=partner,device_id_type=MESH)
        cp.start()
        cp.wait()
        s1=stat_s[k,0:1,:]+stat_r[k,0:1,:]
        s2=stat_s[k,1:2,:]+stat_r[k,1:2,:]
        return recip*(e-s1*(1.0/D)-normed*(s2*(1.0/D)))
    group_wait(r,c,2)
    run(BWD_START)
    loads[0].wait(); loads[1].wait()
    vec_rows(14,token_sums(dh[...]*nbuf[...]))
    vec_rows(21,token_sums(dh[...]))
    gmid[...]=(gt[...].astype(jnp.float32)+norm_back(0,dh[...],nbuf[...],cols[:,0:1],recips[1:2,:]))*cols[:,2:3]
    gat[...]=gmid[...].astype(bf)
    vec_rows(28,token_sums(gat[...]))
    vec_rows(35,token_sums(gt[...]))
    vec_rows(42,vec_in[...])
    loads[3].start()
    half=lambda w,base,k:w.at[pl.ds(pl.multiple_of(base*KH+BR*k,32),BR)]
    nb=KH//BR
    def pair_product(w,wide,rhs,recv,sem):
        blocks=[half(w,1-c,k) for k in range(nb)]+[half(w,c,k) for k in range(nb)]
        slot=lambda k:wblk.at[k%2,:,pl.ds(0,wide)] if wide<QW else wblk.at[k%2]
        ld=[pltpu.make_async_copy(blocks[k],slot(k),w_sem.at[k%2]) for k in range(2*nb)]
        ld[0].start(); ld[1].start()
        swap=pltpu.make_async_remote_copy(src_ref=dh_send,dst_ref=recv,send_sem=x_sem.at[sem],recv_sem=x_sem.at[sem+1],device_id=partner,device_id_type=MESH)
        for k in range(2*nb):
            ld[k].wait()
            v=dot(wblk[k%2,:,0:rhs.shape[0]],rhs)
            if k<nb: dh_send[pl.ds(BR*k,BR),:]=v.astype(bf)
            else: dh[pl.ds(BR*(k-nb),BR),:]=v
            if k<2*nb-2: ld[k+2].start()
            if k==nb-1: swap.start()
        return swap
    swap=pair_product(wo,KH,gat[...],do_recv,4)
    swap.wait()
    unpad_rows(dflat,dh[...]+do_recv[...].astype(jnp.float32))
    dot_[...]=dflat[...].astype(bf)
    lanes=pl.ds(pl.multiple_of(r*128,128),128)
    def full(fn):
        def body(k,_):
            i=(r+k)%24
            fn(dot_.at[pl.ds(pl.multiple_of(64*(i//2)+32*c,32),64),pl.ds(pl.multiple_of((i%2)*128,128),128)],doT.at[:,lanes],s_in.at[i],r_in,i==r,(d,i,c))
            return 0
        lax.fori_loop(0,24,body,0)
    def halves(fn):
        rows=pl.ds(pl.multiple_of(32*c,32),32)
        for s in range(2):
            fn(dot_.at[pl.ds(pl.multiple_of(768*(1-c),32),32),pl.ds(s*128,128)],doT.at[rows,lanes],s_in.at[24+s],r_in,(r==24+s)&(c==0),(d,24+s,0))
    full(push); halves(push)
    def emit(part,cols_,rhs):
        prev={}
        for b in range(8):
            slot=b%2
            if b>=2: prev[slot].wait()
            stage[slot,:,:,:,0:cols_]=dot_nt(lhs[pl.ds(224*b,224),:],rhs).reshape(2,2,56,cols_).astype(bf)
            src=stage.at[slot] if cols_==2400 else stage.at[slot,:,:,:,pl.ds(0,cols_)]
            prev[slot]=pltpu.make_async_copy(src,part.at[b//2,pl.ds(2*(b%2),2)],q_sem.at[slot])
            prev[slot].start()
        return prev
    loads[2].wait()
    for cp in emit(part_o,KH,gat[...]).values(): cp.wait()
    loads[4].start()
    run(BWD_MID)
    def outs(fn):
        seq=pl.ds(pl.multiple_of((r%2)*128,128),128)
        @pl.when(r<24)
        def _():
            def body(k,_):
                i=(r+k)%ROWS
                fn(dout.at[:,:,pl.ds(pl.multiple_of(i*128,128),128)],dq.at[:,pl.ds(pl.multiple_of(64*(r//2)+32*c,32),64),seq],s_out.at[i],r_out,i==r,(d,i,c))
                return 0
            lax.fori_loop(0,ROWS,body,0)
        @pl.when(r>=24)
        def _():
            def body(k,_):
                rr=(r+k//2)%ROWS; cc=k%2
                fn(dout.at[:,pl.ds(pl.multiple_of(32*cc,32),32),pl.ds(pl.multiple_of(rr*128,128),128)],dq.at[:,pl.ds(pl.multiple_of(768*(1-cc),32),32),seq],s_out.at[2*rr+cc],r_out,(rr==r)&(cc==c),(d,rr,cc))
                return 0
            lax.fori_loop(0,2*ROWS,body,0)
    @pl.when(item)
    def _():
        arrived(doT,r_in)
        for a in range(LEN//512):
            sl=pl.ds(a*512,512)
            delta[:,sl]=jnp.sum(oT[:,sl]*doT[:,sl].astype(jnp.float32),axis=0,keepdims=True)
    def kloop(kj,_):
        @pl.when(item)
        def _():
            iota=lax.broadcasted_iota(jnp.int32,(BK,BQ),0)
            iotl=lax.broadcasted_iota(jnp.int32,(BK,BQ),1)
            ks=pl.ds(pl.multiple_of(kj*BK,BK),BK)
            kn=knt[ks,:]; vn=vnt[ks,:]; kT=qkv[1,:,ks]
            def step(qi,carry,diag):
                dk,dv=carry
                qs=pl.ds(pl.multiple_of(qi*BQ,BQ),BQ)
                q=qkv[0,:,qs]*jnp.bfloat16(0.125)
                do=doT[:,qs]
                s=dot(kn,q)
                ok=iota>=(start[:,qs]-kj*BK)
                if diag: ok=ok&(iota<=iotl)
                p=jnp.exp(jnp.where(ok,s,NEG)-lse[:,qs])
                dp=dot(vn,do)
                ds=(p*(dp-delta[:,qs])).astype(jnp.bfloat16)
                dv=dv+dot_nt(do,p.astype(jnp.bfloat16))
                dk=dk+dot_nt(q,ds)
                dqa[:,qs]+=dot(kT,ds)
                return dk,dv
            z=jnp.zeros((HD,BK),jnp.float32)
            carry=step(kj,(z,z),True)
            dk,dv=lax.fori_loop(kj+1,LEN//BQ,lambda qi,cr:step(qi,cr,False),carry)
            dout[1,:,ks]=dk.astype(jnp.bfloat16)
            dout[2,:,ks]=dv.astype(jnp.bfloat16)
        for step,which in BWD_AT:
            pl.when(kj==step)(functools.partial(run,which))
        return 0
    lax.fori_loop(0,LEN//BK,kloop,0)
    @pl.when(item)
    def _():
        for a in range(LEN//512):
            sl=pl.ds(a*512,512)
            dout[0,:,sl]=(dqa[:,sl]*0.125).astype(jnp.bfloat16)
        outs(push)
    run(BWD_THEN)
    for ax,k in RPEERS: pl.semaphore_signal(free,inc=1,device_id=peer_of(ax,k),device_id_type=MESH)
    arrived(dq,r_out)
    grads=dq[...].reshape(2400,TT)
    loads[4].wait()
    for cp in emit(part_q,2400,grads).values(): cp.wait()
    pl.semaphore_wait(free,len(RPEERS))
    def late_product():
        chains["swap"]=pair_product(wq,QW,grads,dh_recv,6)
    def late_norm():
        chains["swap"].wait()
        dh[...]=dh[...]+dh_recv[...].astype(jnp.float32)
        loads[3].wait()
        vec_rows(0,token_sums(dh[...]*nbuf[...]))
        vec_rows(7,token_sums(dh[...]))
        vec_rows(67,jnp.concatenate((token_sums(grads),jnp.zeros((1,32),jnp.float32)),axis=1))
        v_go(0,vtmp[...])
        gtok[...]=(gmid[...]+norm_back(1,dh[...],nbuf[...],cols[:,1:2],recips[0:1,:])).astype(bf)
        v_go(1,v_total(0))
    def late_vec():
        v_go(2,v_total(1))
    for k in steps(BWD_LAST):
        if k=="**": late_product()
        elif k=="--": late_norm()
        elif k=="++": late_vec()
        else: run(k)
    vec_out[...]=v_total(2)
    v_end()
    pl.when(item)(lambda:outs(pushed))
    full(pushed); halves(pushed)
VM=pl.BlockSpec(memory_space=pltpu.VMEM); ANY=pl.BlockSpec(memory_space=pl.ANY)
bf=jnp.bfloat16
def attend(xt,cols,bias,eb,segs,names,arrs,cid=1):
    S=jax.ShapeDtypeStruct; n=len(names); V=pltpu.VMEM; DM=pltpu.SemaphoreType.DMA; f=jnp.float32
    FH=eb.shape[1]
    out=pl.pallas_call(functools.partial(attn_fwd_kernel,names,[a.shape[1] for a in arrs]),
      out_shape=(S((3,HD,LEN),bf),S((HD,LEN),f),S((1,LEN),f),S((1,LEN),jnp.int32),S((32,56,TT),bf),S((32,56,TT),bf),S((KH,TT),f),S((KH,TT),f),S((8,TT),f),S((32,56,TT),bf),
        S((TT,KH),f),S((TT,FH),f),S((TT,FH),bf),S((TT,FH),bf))+gather_shapes(arrs),
      in_specs=[VM]*5+[ANY]*n,out_specs=(ANY,)+(VM,)*12+(ANY,)+(ANY,)*n,
      scratch_shapes=[V((2,25,HD,128),bf),V((3,HD,LEN),bf),V((LEN,HD),bf),V((HD,LEN),bf),V((4,4,2,56,FH),bf),V((4,4,2,56,KH),bf),V((TT,2400),f),V((3,800,TT),bf),V((1600,TT),f),V((KH,TT),f),
        V((2,8,TT),f),V((2,8,TT),f),DM((26,)),DM((32,)),DM,DM,DM,DM((2,)),DM((12,))]+gather_sems(n),
      compiler_params=pltpu.CompilerParams(collective_id=cid,has_side_effects=True,vmem_limit_bytes=62<<20))(xt,cols,bias,eb,segs,*arrs)
    return out[:4],out[4:14],out[14:]
def attend_back(front,kept,h1t,normt,vec,wq,names,parts,cid=2):
    S=jax.ShapeDtypeStruct; n=len(names); f=jnp.float32; V=pltpu.VMEM; DM=pltpu.SemaphoreType.DMA
    qkv,oT,lse,start=kept
    rows=88
    out=pl.pallas_call(functools.partial(back_kernel,names,[a.shape[4] for a in parts]),
      out_shape=(S((4,4,2,56,KH),bf),S((4,4,2,56,KQ),bf),S((KH,TT),bf),S((50,KH),f),S((50,KQ),f),S((rows,128),f))+tuple(S((50 if a.shape[3]==56 else a.shape[3],a.shape[4]),f) for a in parts),
      in_specs=[ANY,ANY,VM,VM,VM,ANY,ANY,VM,VM,VM,VM,ANY,ANY,VM]+[ANY]*(1+n),out_specs=(ANY,ANY,VM,VM,VM,VM)+(VM,)*n,
      scratch_shapes=[V((HD,LEN),bf),V((LEN,HD),bf),V((LEN,HD),bf),V((HD,LEN),f),V((1,LEN),f),V((3,HD,LEN),bf),
        V((3,800,TT),bf),V((2,2,2,56,KQ),bf),V((2,BR,QW),bf),V((KH,TT),bf),V((KH,TT),bf),V((KH,TT),bf),V((KP,TT),bf),
        V((KH,TT),f),V((KH,TT),f),V((KH,TT),f),V((KH,TT),bf),V((800,TT),f),V((800,TT),bf),V((2,8,TT),f),V((2,8,TT),f)]+[V((4,rows,128),f)]*3+[V((rows,128),f)]+
        [DM((26,)),DM((64,)),DM,DM,DM((2,)),DM((2,)),DM((8,)),DM((5,)),pltpu.SemaphoreType.REGULAR,DM((9,)),DM((9,))]+
        sum([scatter_bufs(nm,*a.shape[3:])+scatter_sems() for nm,a in zip(names,parts)],[])+scatter_bufs("o",56,KH)+scatter_sems()*2,
      compiler_params=pltpu.CompilerParams(collective_id=cid,has_side_effects=True,vmem_limit_bytes=VMEM_BACK))(*front,qkv,oT,start,lse,h1t,normt,vec,wq,*parts)
    return out[2],out[3],out[4],out[5],out[6:]
VMEM_BACK=63<<20


FH=3200; TF=640
def mlp_kernel(h2t,we,wc,pre,a_own,a_other,mid,g,result,part_c,part_e,dh2,dsum,
        wev,wcv,da_send,da_recv,dpre,dh_send,dh_recv,stage_e,stage_c,w_sem,s_sem,r_sem,e_sem,c_sem):
    c=lax.axis_index("col"); other=1-c
    partner=(lax.axis_index("dev"),lax.axis_index("row"),other)
    loads=[pltpu.make_async_copy(wc,wcv,w_sem.at[0]),pltpu.make_async_copy(we,wev,w_sem.at[1])]
    for cp in loads: cp.start()
    bar=pltpu.get_barrier_semaphore()
    pl.semaphore_signal(bar,inc=1,device_id=partner,device_id_type=MESH)
    pl.semaphore_wait(bar,1)
    def swap(i,s,d):
        return pltpu.make_async_remote_copy(src_ref=s,dst_ref=d,send_sem=s_sem.at[i],recv_sem=r_sem.at[i],device_id=partner,device_id_type=MESH)
    x_da,x_dh=swap(0,da_send,da_recv),swap(1,dh_send,dh_recv)
    lanes=lambda k,n:pl.ds(pl.multiple_of(k*n,128),n)
    rows=lambda base,k,n:pl.ds(pl.multiple_of(base+k*n,64),n)
    f32=lambda v:v.astype(jnp.float32)
    NT=FH//TF
    def loop(n,f):
        def body(k,_):
            f(k)
            return 0
        lax.fori_loop(0,n,body,0)
    loads[0].wait()
    def f(k): da_send[:,lanes(k,TF)]=dot_nt(g[...],wcv[rows(other*FH,k,TF),:]).astype(bf)
    loop(NT,f)
    x_da.start()
    def emit(i,stage,sem,dst,value):
        slot=i%2
        cp=pltpu.make_async_copy(stage.at[slot],dst,sem.at[slot])
        if i>=2: prev[slot].wait()
        stage[slot]=value
        cp.start(); prev[slot]=cp
    prev={}
    for i in range(2*NT):
        a,b,k=(a_own,c,i) if i<NT else (a_other,other,i-NT)
        emit(i,stage_c,c_sem,part_c.at[rows(b*FH,k,TF)],dot_tn(a[:,k*TF:k*TF+TF],g[...]).astype(bf))
    prev_c=prev
    x_da.wait_recv()
    def f(k):
        sl=lanes(k,TF)
        d=dot_nt(g[...],wcv[rows(c*FH,k,TF),:])+f32(da_recv[:,sl])
        p=pre[:,sl]
        t=jnp.tanh(GC*(p+0.044715*(p*p*p)))
        slope=0.5*(1.0+t)+p*(0.5*(1.0-t*t)*(GC*(1.0+(3*0.044715)*(p*p))))
        dp=(d*slope).astype(bf)
        dpre[:,sl]=dp
        dsum[:,sl]=jnp.sum(f32(dp),axis=0,keepdims=True)
    loop(NT,f)
    loads[1].wait()
    def f(k): dh_send[rows(0,k,448),:]=dot_nt(wev[rows(other*KH,k,448),:],dpre[...]).astype(bf)
    loop(2,f)
    x_dh.start()
    def f(k): dh2[rows(0,k,448),:]=dot_nt(wev[rows(c*KH,k,448),:],dpre[...])
    loop(2,f)
    prev={}
    for j in range(KP//256):
        emit(j,stage_e,e_sem,part_e.at[pl.ds(256*j,256)],dot(h2t[256*j:256*j+256,:],dpre[...]).astype(bf))
    br=dot(a_own[...],wcv[rows(c*FH,0,FH),:])+dot(a_other[...],wcv[rows(other*FH,0,FH),:])
    result[...]=(mid[...]+br).astype(bf)
    x_dh.wait_recv()
    dh2[...]=dh2[...]+f32(dh_recv[...])
    for cp in list(prev.values())+list(prev_c.values()): cp.wait()
    for cp in (x_da,x_dh): cp.wait_send()
def mlp(h2t,we,wc,pre,a_own,a_other,mid,g,cid=4):
    S=jax.ShapeDtypeStruct; f=jnp.float32; V=pltpu.VMEM
    return pl.pallas_call(mlp_kernel,
      out_shape=(S((TT,KH),bf),S((6400,KH),bf),S((KP,FH),bf),S((KH,TT),f),S((1,FH),f)),
      in_specs=[VM,ANY,ANY]+[VM]*5,out_specs=(VM,ANY,ANY,VM,VM),
      scratch_shapes=[V((KP,FH),bf),V((6400,KH),bf)]+[V((TT,FH),bf)]*3+[V((KH,TT),bf)]*2+[V((2,256,FH),bf),V((2,TF,KH),bf)]+[pltpu.SemaphoreType.DMA((n,)) for n in (2,2,2,2,2)],
      compiler_params=pltpu.CompilerParams(collective_id=cid,has_side_effects=True,vmem_limit_bytes=58<<20))(h2t,we,wc,pre,a_own,a_other,mid,g)


def pad_rows(block):
    return jnp.pad(block, ((0, 6), (0, 0)))


def pad_columns(values):
    n = values.shape[0]
    return jnp.pad(values.reshape(n, 16, 50), ((0, 0), (0, 0), (0, 6))).reshape(n, KH)


def unpad_features(values):
    n = values.shape[0]
    return values.reshape(n, 16, 56)[:, :, :50].reshape(n, 800)


def per_device(
    tokens,
    segments,
    first_gain,
    first_bias,
    attention_in,
    attention_bias,
    attention_out,
    output_bias,
    second_gain,
    second_bias,
    expand_weight,
    expand_bias,
    contract_weight,
    contract_bias,
    cotangent,
):
    seqs, block_len, width = tokens.shape
    row_total = seqs * block_len
    grad_low = pad_columns(cotangent.reshape(row_total, width))
    tokens_back = pad_columns(tokens.reshape(row_total, width)).T
    zeros = jnp.zeros_like(first_gain)
    small = jnp.concatenate(
        (second_gain, first_gain, zeros + 1.0, first_bias, second_bias, output_bias, contract_bias, zeros)
    )
    columns = pad_columns(small.reshape(8, width)).T
    bias_three = jnp.concatenate((attention_bias[0], zeros, attention_bias[1]))
    kept, saved, gathered = attend(
        tokens_back,
        columns,
        bias_three[None],
        expand_bias[None],
        segments,
        "qeco",
        (
            jnp.pad(attention_in.reshape(50, 3 * width), ((0, 6), (0, 32))),
            pad_rows(expand_weight),
            pad_columns(contract_weight),
            pad_rows(pad_columns(attention_out)),
        ),
        1,
    )
    rows_attn, rows_one, normed_one, normed_two, recips, rows_two, middle, pre_gelu, gelu_own, gelu_other = saved
    weight_qkv = gathered[0].reshape(KP, QW)
    weight_expand = gathered[1].reshape(KP, 4 * width)
    weight_contract = gathered[2].reshape(4 * D, KH)
    weight_out = gathered[3].reshape(KP, KH)
    result, part_contract, part_expand, grad_two, expand_sums = mlp(
        rows_two.reshape(KP, row_total),
        weight_expand,
        weight_contract,
        pre_gelu,
        gelu_own,
        gelu_other,
        middle,
        grad_low,
        4,
    )
    result = unpad_features(result).reshape(tokens.shape)
    gradient_tokens, sum_out, sum_qkv, vector, (sum_expand, sum_contract) = attend_back(
        (
            grad_two,
            normed_two,
            grad_low.T,
            columns,
            recips,
            rows_attn.reshape(KP, row_total),
            weight_out,
        ),
        kept,
        rows_one.reshape(KP, row_total),
        normed_one,
        expand_sums,
        weight_qkv,
        "ec",
        (
            part_expand.reshape(4, 4, 2, 56, 4 * width),
            part_contract.reshape(4, 4, 2, 200, KH),
        ),
        2,
    )
    gradient_tokens = unpad_features(gradient_tokens.T).reshape(tokens.shape)
    padded = unpad_features(vector[:42].reshape(6, KH)).reshape(-1)
    sums = [padded[width * k : width * (k + 1)] for k in range(6)]
    qkv_sums = vector[67:86].reshape(-1)
    return (
        result,
        gradient_tokens,
        sums[0],
        sums[1],
        sum_qkv[:, : 3 * width].reshape(50, 3, width),
        jnp.concatenate((qkv_sums[:width], qkv_sums[2 * width : 3 * width])).reshape(2, width),
        unpad_features(sum_out),
        sums[4],
        sums[2],
        sums[3],
        sum_expand,
        vector[42:67].reshape(-1),
        unpad_features(sum_contract),
        sums[5],
    )


def solution(mesh):
    return jax.shard_map(
        per_device,
        mesh=mesh,
        in_specs=(
            P("dev", "row", "col"),
            P("dev", None),
            P("col"),
            P("col"),
            P("row", None, "col"),
            P(None, "col"),
            P("row", "col"),
            P("col"),
            P("col"),
            P("col"),
            P("row", "col"),
            P("col"),
            P("row", "col"),
            P("col"),
            P("dev", "row", "col"),
        ),
        out_specs=(
            P("dev", "row", "col"),
            P("dev", "row", "col"),
            P("col"),
            P("col"),
            P("row", None, "col"),
            P(None, "col"),
            P("row", "col"),
            P("col"),
            P("col"),
            P("col"),
            P("row", "col"),
            P("col"),
            P("row", "col"),
            P("col"),
        ),
        check_vma=False,
    )
```

```python
import functools

import jax
import jax.numpy as jnp
from jax import lax
from jax.experimental import pallas as pl
from jax.experimental.pallas import tpu as pltpu
from jax.sharding import PartitionSpec as P

MESH = pl.DeviceIdType.MESH
D = 1600
KP = 1792


def coords():
    d=lax.axis_index("dev"); r=lax.axis_index("row"); c=lax.axis_index("col")
    return r//8, (r//2)%4, d*2+r%2, c
def place(z,y,x,c):
    return (x//2, (z*4+y)*2+x%2, c)
def peer_of(ax,k):
    z,y,x,c=coords()
    if ax=="z": z=(z+k)%4
    if ax=="y": y=(y+k)%4
    if ax=="x": x=(x+k)%4
    return place(z,y,x,c)
def greet(peers):
    bar=pltpu.get_barrier_semaphore()
    for ax,k in peers: pl.semaphore_signal(bar,inc=1,device_id=peer_of(ax,k),device_id_type=MESH)
    pl.semaphore_wait(bar,len(peers))
SPLIT={"q":(4,4,6,5),"o":(2,1,2,2),"e":(7,4,7,7),"c":(1,2,2,2)}
ORD=("yzx","zyx","yxz","zxy")
GPEERS=[("z",1),("z",3),("z",2),("y",1),("y",3),("y",2),("x",1),("x",3)]
def cuts(name,W):
    out=[];p=0
    for n in SPLIT[name]:
        out.append((p,min(p+n*128,W))); p+=n*128
    assert out[-1][1]==W
    return out
def gather_steps(names,widths,src,dst,ss,rs,ls):
    n=len(names)
    z,y,x,c=coords(); xl=x%2
    cnt=[0]; allc=[]
    FULL=slice(None)
    LO=pl.ds(0,2); HI=pl.ds(2,2)
    def mk(s,d,ax,k):
        i=cnt[0]; cnt[0]+=1
        cp=pltpu.make_async_remote_copy(src_ref=s,dst_ref=d,send_sem=ss.at[i],recv_sem=rs.at[i],device_id=peer_of(ax,k),device_id_type=MESH)
        allc.append(cp); return cp
    cut=[cuts(nm,w) for nm,w in zip(names,widths)]
    def at(t,p,zi,yi,xi):
        a,b=cut[t][p]
        return dst[t].at[zi,yi,xi,:,pl.ds(a,b-a)]
    def wait(l):
        for cp in l: cp.wait_recv()
    def go(l):
        for cp in l: cp.start()
    loc=[pltpu.make_async_copy(src[t],dst[t].at[z,y,xl],ls.at[t]) for t in range(n)]
    st1=[[],[],[],[]]
    for t in range(n):
        for p in range(4):
            a,b=cut[t][p]
            for k in (1,3,2):
                st1[p].append(mk(src[t].at[:,pl.ds(a,b-a)],at(t,p,z,y,xl),ORD[p][0],k))
    def both(p,f):
        return [cp for t in range(n) for cp in f(t,p)]
    def xsend(zi,yi):
        return lambda t,p:[mk(at(t,p,*zi,xl),at(t,p,*zi,xl),"x",1),mk(at(t,p,*yi,xl),at(t,p,*yi,xl),"x",3)]
    def ring_a(ax,zi,yi,xi):
        return lambda t,p:[mk(at(t,p,zi,yi,xi),at(t,p,zi,yi,xi),ax,k) for k in (1,3)]
    def ring_b(ax,xi):
        def f(t,p):
            if ax=="z":
                u=at(t,p,(z+3)%4,LO,xi); v=at(t,p,(z+1)%4,HI,xi)
            else:
                u=at(t,p,LO,(y+3)%4,xi); v=at(t,p,HI,(y+1)%4,xi)
            return [mk(u,u,ax,1),mk(v,v,ax,3)]
        return f
    A2=both(0,ring_a("z",z,FULL,xl)); B2=both(1,ring_a("y",FULL,y,xl))
    C2=both(2,xsend((z,LO),(z,HI))); D2=both(3,xsend((LO,y),(HI,y)))
    A2b=both(0,ring_b("z",xl)); B2b=both(1,ring_b("y",xl))
    C3=both(2,ring_a("z",z,FULL,FULL)); D3=both(3,ring_a("y",FULL,y,FULL))
    A3=both(0,xsend((LO,FULL),(HI,FULL))); B3=both(1,xsend((LO,FULL),(HI,FULL)))
    C3b=both(2,ring_b("z",FULL)); D3b=both(3,ring_b("y",FULL))
    def f0():
        go(loc)
        for p in range(4): go(st1[p])
    def f1():
        wait_loc=[cp.wait() for cp in loc]
        wait(st1[0]); go(A2)
        wait(st1[1]); go(B2)
        wait(st1[2]); go(C2)
        wait(st1[3]); go(D2)
    def f2():
        wait(A2); go(A2b); wait(B2); go(B2b)
        wait(C2); go(C3); wait(D2); go(D3)
    def f3():
        wait(A2b); go(A3); wait(B2b); go(B3)
    def f4():
        wait(C3); go(C3b); wait(D3); go(D3b)
    def f5():
        wait(A3);wait(B3);wait(C3b);wait(D3b)
        for cp in allc: cp.wait_send()
    return [f0,f1,f2,f3,f4,f5]
def gather_sems(n):
    return [pltpu.SemaphoreType.DMA((36,)),pltpu.SemaphoreType.DMA((36,)),pltpu.SemaphoreType.DMA((1,))]*n
def gather_chains(names,widths,src,dst,sems):
    chains=[gather_steps(names[t],[widths[t]],[src[t]],[dst[t]],*sems[3*t:3*t+3]) for t in range(len(names))]
    def both(k):
        def f():
            for ch in chains: ch[k]()
        return f
    return [both(k) for k in range(6)]
def gather_kernel(names,widths,*refs):
    n=len(names)
    steps=gather_chains(names,widths,refs[:n],refs[n:2*n],refs[2*n:])
    greet(GPEERS)
    for f in steps: f()
def gather_shapes(arrs):
    return tuple(jax.ShapeDtypeStruct((4,4,2)+a.shape,a.dtype) for a in arrs)
def gather(names,arrs,cid=0):
    n=len(names)
    return pl.pallas_call(functools.partial(gather_kernel,names,[a.shape[1] for a in arrs]),
      out_shape=gather_shapes(arrs),
      in_specs=[pl.BlockSpec(memory_space=pl.ANY)]*n,out_specs=tuple([pl.BlockSpec(memory_space=pl.ANY)]*n),
      scratch_shapes=gather_sems(n),
      compiler_params=pltpu.CompilerParams(collective_id=cid,has_side_effects=True))(*arrs)


RSPLIT={"q":(6,7,6),"o":(2,3,2),"e":(10,7,8),"c":(2,3,2)}
AX=("xzy","yzx","zyx")
RPEERS=[(a,k) for a in "xyz" for k in (1,2,3)]
def rcuts(name,W):
    out=[];p=0
    for n in RSPLIT[name]:
        out.append((p,min(p+n*128,W))); p+=n*128
    assert out[-1][1]==W
    return out
def scatter_steps(nm,width,src,out,bufs,sems):
    ss,rs,ls=sems
    z,y,x,c=coords(); xl=x%2; xh=x//2
    me={"x":x,"y":y,"z":z}
    cnt=[0]; lcnt=[0]; allc=[]
    def mk(s,d,ax,k,keep=True):
        i=cnt[0]; cnt[0]+=1
        cp=pltpu.make_async_remote_copy(src_ref=s,dst_ref=d,send_sem=ss.at[i],recv_sem=rs.at[i],device_id=peer_of(ax,k),device_id_type=MESH)
        if keep: allc.append(cp)
        return cp
    def mkload(s,d):
        i=lcnt[0]; lcnt[0]+=1
        return pltpu.make_async_copy(s,d,ls.at[i])
    cut=rcuts(nm,width)
    f32=lambda a:a.astype(jnp.float32)
    def D(p,k,i=None):
        a,b=cut[p]; s=slice(None) if i is None else pl.ds(2*i,2)
        if p==0:
            h=(b-a)//2
            return src.at[s,:,k%2,:,pl.ds(pl.multiple_of(a+(k//2)*h,128),h)]
        if p==1: return src.at[s,k,:,:,pl.ds(a,b-a)]
        return src.at[k,s,:,:,pl.ds(a,b-a)]
    M=(4,2,2); P3=(0,1,2)
    ld={}; R={}
    for p in P3:
        own,rlp,rlm,rm,rp,rl2p,rl2m,rm2,rp2,out2,r3,r4=bufs[p]
        k=me[AX[p][0]]; ax=AX[p][0]
        bp=own.at[pl.ds(0,2)]; bm=own.at[pl.ds(2,2)]
        ld[p]=[mkload(D(p,(k+1)%4,0),bp),mkload(D(p,(k+3)%4,1),bm),mkload(D(p,k),own)]
        R[p,"a"]=[mk(D(p,(k+2)%4,0),rlp,ax,1),mk(D(p,(k+2)%4,1),rlm,ax,3)]
        R[p,"b"]=[mk(D(p,(k+1)%4,1),rm.at[pl.ds(2,2)],ax,1),mk(D(p,(k+3)%4,0),rp.at[pl.ds(0,2)],ax,3),
                  mk(bp,rm.at[pl.ds(0,2)],ax,1,False),mk(bm,rp.at[pl.ds(2,2)],ax,3,False)]
        m=M[p]; hm=m//2
        ax=AX[p][1]; k=me[ax]
        L=pl.ds(0,hm); H=pl.ds(hm,hm)
        R[p,"c"]=[mk(own.at[(k+2)%4,L],rl2p,ax,1),mk(own.at[(k+2)%4,H],rl2m,ax,3)]
        R[p,"d"]=[mk(own.at[(k+1)%4,H],rm2.at[H],ax,1),mk(own.at[(k+3)%4,L],rp2.at[L],ax,3),
                  mk(own.at[(k+1)%4,L],rm2.at[L],ax,1),mk(own.at[(k+3)%4,H],rp2.at[H],ax,3)]
        ax=AX[p][2]; k=me[ax]; q=4 if p==0 else 2
        R[p,"e"]=[mk(out2.at[(k+j)%q],r3.at[j-1],ax,j) for j in (1,2,3)]
        if p==0: R[p,"f"]=[mk(r4.at[xh],r4.at[xh],"x",2)]
    def addin(dst,other,cntn,f,g):
        def body(i,_):
            dst[f(i)]=(f32(dst[f(i)])+f32(other[g(i)])).astype(jnp.bfloat16)
            return 0
        lax.fori_loop(0,cntn,body,0)
    def first():
        for p in P3:
            for cp in ld[p][:2]: cp.start()
        for p in P3:
            for cp in R[p,"a"]: cp.start()
        for p in P3:
            for cp in R[p,"b"][:2]: cp.start()
    def relay(p):
        def f():
            own,rlp,rlm=bufs[p][:3]
            m=M[p]
            ld[p][0].wait(); R[p,"a"][0].wait_recv(); addin(own,rlp,2*m,lambda i:(i//m,i%m),lambda i:(i//m,i%m)); R[p,"b"][2].start()
            ld[p][1].wait(); R[p,"a"][1].wait_recv(); addin(own,rlm,2*m,lambda i:(2+i//m,i%m),lambda i:(i//m,i%m)); R[p,"b"][3].start()
        return f
    def reload(p):
        def f():
            for cp in R[p,"b"][2:]: cp.wait_send()
            ld[p][2].start()
        return f
    def sum1(p):
        def f():
            own,rm,rp=bufs[p][0],bufs[p][3],bufs[p][4]
            m=M[p]
            ld[p][2].wait()
            for cp in R[p,"b"]: cp.wait_recv()
            def body(i,_):
                j=(i//m,i%m)
                own[j]=(f32(own[j])+(f32(rm[j])+f32(rp[j]))).astype(jnp.bfloat16)
                return 0
            lax.fori_loop(0,4*m,body,0)
            for cp in R[p,"c"]: cp.start()
            for cp in R[p,"d"][:2]: cp.start()
        return f
    def relay2(p):
        def f():
            own,rl2p,rl2m=bufs[p][0],bufs[p][5],bufs[p][6]
            hm=M[p]//2; k=me[AX[p][1]]
            R[p,"c"][0].wait_recv()
            addin(own,rl2p,hm,lambda i:((k+1)%4,i),lambda i:i)
            R[p,"d"][2].start()
            R[p,"c"][1].wait_recv()
            addin(own,rl2m,hm,lambda i:((k+3)%4,hm+i),lambda i:i)
            R[p,"d"][3].start()
        return f
    def sum2(p):
        def f():
            own,rm2,rp2,out2=bufs[p][0],bufs[p][7],bufs[p][8],bufs[p][9]
            k=me[AX[p][1]]
            for cp in R[p,"d"]: cp.wait_recv()
            def body(i,_):
                out2[i]=(f32(own[k,i])+(f32(rm2[i])+f32(rp2[i]))).astype(jnp.bfloat16)
                return 0
            lax.fori_loop(0,M[p],body,0)
            for cp in R[p,"e"]: cp.start()
        return f
    def last(p):
        def f():
            out2,r3,r4=bufs[p][9:12]
            a,b=cut[p]
            for cp in R[p,"e"]: cp.wait_recv()
            k=me[AX[p][2]] if p==0 else xl
            s=(f32(out2[k])+f32(r3[1]))+(f32(r3[0])+f32(r3[2]))
            if p==0:
                r4[xh]=s.astype(jnp.bfloat16)
                R[p,"f"][0].start()
            else:
                out[:,pl.ds(a,b-a)]=s[0:out.shape[0],:]
        return f
    def end():
        a,b=cut[0]; h=(b-a)//2; r4=bufs[0][11]
        R[0,"f"][0].wait_recv()
        for j in range(2): out[:,pl.ds(a+j*h,h)]=f32(r4[j])[0:out.shape[0],:]
        for cp in allc: cp.wait_send()
    return [[first]]+[[f(p) for p in P3] for f in (relay,reload,sum1,relay2,sum2,last)]+[[end]]
STAGES=8
def staggered(chains,by):
    return [[f for i,ch in enumerate(chains) if 0<=tick-by*i<STAGES for f in ch[tick-by*i]] for tick in range(STAGES+by*(len(chains)-1))]
def scatter_bufs(nm,r,w):
    scr=[]
    for p,(a,b) in enumerate(rcuts(nm,w)):
        m=4 if p==0 else 2; v=(b-a)//2 if p==0 else b-a; hm=m//2
        B=lambda *s:pltpu.VMEM(s+(r,v),jnp.bfloat16)
        scr+=[B(4,m),B(2,m),B(2,m),B(4,m),B(4,m),B(hm),B(hm),B(m),B(m),B(m),B(3),B(2) if p==0 else pltpu.VMEM((8,128),jnp.bfloat16)]
    return scr
def scatter_sems():
    return [pltpu.SemaphoreType.DMA((46,)),pltpu.SemaphoreType.DMA((46,)),pltpu.SemaphoreType.DMA((9,))]
def by_part(refs):
    return [refs[12*p:12*p+12] for p in range(3)]
def narrowed(bufs,nm,w):
    out=[]
    for p,(a,b) in enumerate(rcuts(nm,w)):
        v=(b-a)//2 if p==0 else b-a
        out.append([ref if ref.shape[-1]==v or ref.shape==(8,128) else ref.at[(slice(None),)*(len(ref.shape)-1)+(pl.ds(0,v),)] for ref in bufs[p]])
    return out
def vector_steps(vbuf,sems):
    z,y,x,c=coords(); me=(x,y,z)
    ss,rs=sems
    R=[[pltpu.make_async_remote_copy(src_ref=vbuf[st].at[me[st]],dst_ref=vbuf[st].at[me[st]],send_sem=ss.at[3*st+k-1],recv_sem=rs.at[3*st+k-1],device_id=peer_of("xyz"[st],k),device_id_type=MESH) for k in (1,2,3)] for st in range(3)]
    def go(st,v):
        vbuf[st][pl.ds(me[st],1)]=v[None]
        for cp in R[st]: cp.start()
    def total(st):
        for cp in R[st]: cp.wait_recv()
        b=vbuf[st]
        return (b[0]+b[1])+(b[2]+b[3])
    def end():
        for l in R:
            for cp in l: cp.wait_send()
    return go,total,end


TT=256; KH=896; HD=64; LEN=4096; NEG=-1e30; ROWS=32
FQ,FK,BQ,BK=1024,1024,512,512
def dot(a,b): return lax.dot_general(a,b,(((1,),(0,)),((),())),preferred_element_type=jnp.float32)
def dot_nt(a,b): return lax.dot_general(a,b,(((1,),(1,)),((),())),preferred_element_type=jnp.float32)
def group_greet(d,r,c,across):
    bar=pltpu.get_barrier_semaphore()
    for rr in across: pl.semaphore_signal(bar,inc=1,device_id=(1-d,rr,c),device_id_type=MESH)
    def body(i,_):
        @pl.when(i!=r*2+c)
        def _():
            pl.semaphore_signal(bar,inc=1,device_id=(d,i//2,i%2),device_id_type=MESH)
        return 0
    lax.fori_loop(0,2*ROWS,body,0)
def group_wait(across):
    pl.semaphore_wait(pltpu.get_barrier_semaphore(),2*ROWS-1+across)
def push(src,dst,send_sem,recv_sem,same,target):
    @pl.when(same)
    def _():
        pltpu.make_async_copy(src,dst,recv_sem).start()
    @pl.when(jnp.logical_not(same))
    def _():
        pltpu.make_async_remote_copy(src_ref=src,dst_ref=dst,send_sem=send_sem,recv_sem=recv_sem,device_id=target,device_id_type=MESH).start()
def pushed(src,dst,send_sem,recv_sem,same,target):
    @pl.when(jnp.logical_not(same))
    def _():
        pltpu.make_async_remote_copy(src_ref=src,dst_ref=dst,send_sem=send_sem,recv_sem=recv_sem,device_id=target,device_id_type=MESH).wait_send()
def arrived(ref,sem):
    pltpu.make_async_copy(ref,ref,sem).wait()
def steps(text):
    return [text[k:k+2] for k in range(0,len(text),2)]
FWD_BEFORE=steps("q1o0q2e1q3o1q4e2q5")
FWD_LOAD=steps("c0e3o2")
FWD_PROJ=steps("c1o3")
FWD_SENT=steps("e4c2o4")
FWD_AT=((1,"c3"),)
FWD_THEN=steps("o5e5")
FWD_LATE=steps("c4")
FWD_END=steps("c5")
QW=2432
GC=0.7978845608028654
def dot_tn(a,b): return lax.dot_general(a,b,(((0,),(0,)),((),())),preferred_element_type=jnp.float32)
def attn_fwd_kernel(names,widths,*refs):
    it=iter(refs)
    take=lambda n:[next(it) for _ in range(n)]
    n=len(names)
    xt,cols,bias,eb,segs=take(5)
    src=take(n)
    qkv_out,oT,lse,start,op,h1t,norm1t,norm2t,recips,h2t,mid,pre,a_own,a_other=take(14)
    dst=take(n)
    o_recv,qkv,knt,obf,wv,wov,acc,pt,of,mt,stat_s,stat_r,s_in,s_out,r_in,r_out,l_sem,w_sem,x_sem=take(19)
    chains={nm:gather_steps(nm,[widths[t]],[src[t]],[dst[t]],*take(3)) for t,nm in enumerate(names)}
    def run(which):
        for k in which: chains[k[0]][int(k[1])]()
    d=lax.axis_index("dev"); r=lax.axis_index("row"); c=lax.axis_index("col")
    partner=(d,r,1-c)
    def swap(k,s,t):
        cp=pltpu.make_async_remote_copy(src_ref=s,dst_ref=t,send_sem=x_sem.at[2*k],recv_sem=x_sem.at[2*k+1],device_id=partner,device_id_type=MESH)
        cp.start()
        return cp
    def norm(k,v,gain,shift,normed,hidden):
        stat_s[k,0:1,:]=jnp.sum(v,axis=0,keepdims=True)
        stat_s[k,1:2,:]=jnp.sum(v*v,axis=0,keepdims=True)
        swap(2*k,stat_s.at[k],stat_r.at[k]).wait()
        m=(stat_s[k,0:1,:]+stat_r[k,0:1,:])*(1.0/D)
        recip=lax.rsqrt((stat_s[k,1:2,:]+stat_r[k,1:2,:])*(1.0/D)-m*m+1e-5)
        xhat=(v-m)*recip
        normed[...]=xhat
        recips[k:k+1,:]=recip
        own=pl.ds(pl.multiple_of(16*c,16),16)
        hidden[own]=(xhat*gain+shift).reshape(16,56,TT).astype(bf)
        return swap(2*k+1,hidden.at[own],hidden.at[own])
    group_greet(d,r,c,[r+1-2*(r%2)])
    acc[...]=jnp.broadcast_to(bias[...],acc.shape)
    pre[...]=jnp.broadcast_to(eb[...],pre.shape)
    seg=jnp.broadcast_to(jnp.where(r%2==0,segs[0:1,:],segs[1:2,:]),(8,LEN))
    pos=lax.broadcasted_iota(jnp.int32,(8,LEN),1)
    first=jnp.where((seg!=pltpu.roll(seg,1,1))&(pos>0),pos,0)
    for k in range(12):
        first=jnp.maximum(first,jnp.where(pos>=2**k,pltpu.roll(first,2**k,1),0))
    start[...]=first[0:1,:]
    group_wait(1)
    run(["q0","e0"])
    sent=norm(0,xt[...].astype(jnp.float32),cols[:,1:2],cols[:,3:4],norm1t,h1t)
    run(FWD_BEFORE)
    wq=wv.at[:,:,:,:,pl.ds(0,QW)]
    load=pltpu.make_async_copy(dst[0],wq,w_sem.at[0])
    load.start()
    run(FWD_LOAD)
    sent.wait()
    load.wait()
    def over_blocks(total,tile,hidden,weight):
        n=total.shape[1]
        def body(k,_):
            hk=jnp.concatenate([hidden[4*k+b] for b in range(4)],axis=0)
            for a0 in range(0,n,tile):
                sl=pl.ds(a0,min(tile,n-a0))
                wk=jnp.concatenate([weight[k//2,(k%2)*2+b//2,b%2,:,sl] for b in range(4)],axis=0)
                total[:,sl]+=dot_tn(hk,wk)
            return 0
        lax.fori_loop(0,8,body,0)
    over_blocks(acc,512,h1t,wv)
    run(FWD_PROJ)
    for a0 in range(0,2400,128):
        piece=acc[:,a0:min(a0+128,2400)].T.astype(bf)
        at=a0
        while at<min(a0+128,2400):
            t=at//800; end=min(a0+128,2400,(t+1)*800)
            pt[t,at-800*t:end-800*t,:]=piece[at-a0:end-a0]
            at=end
    lanes=pl.ds(pl.multiple_of(r*128,128),128)
    def full(fn):
        def body(k,_):
            i=(r+k)%24
            fn(pt.at[:,pl.ds(pl.multiple_of(64*(i//2)+32*c,32),64),pl.ds(pl.multiple_of((i%2)*128,128),128)],qkv.at[:,:,lanes],s_in.at[i],r_in,i==r,(d,i,c))
            return 0
        lax.fori_loop(0,24,body,0)
    def halves(fn):
        rows=pl.ds(pl.multiple_of(32*c,32),32)
        for s in range(2):
            fn(pt.at[:,pl.ds(pl.multiple_of(768*(1-c),32),32),pl.ds(s*128,128)],qkv.at[:,rows,lanes],s_in.at[24+s],r_in,(r==24+s)&(c==0),(d,24+s,0))
    full(push); halves(push)
    run(FWD_SENT)
    item=(r<24)|((c==0)&(r<26))
    head=r//2+13*c; seq=r%2
    def outs(qi,fn):
        def body(i,_):
            rr=qi*(FQ//128)+(r+i)%(FQ//128)
            fn(obf.at[:,pl.ds(pl.multiple_of(rr*128,128),128)],o_recv.at[seq,head],s_out.at[rr],r_out,rr==r,(d,rr,c))
            return 0
        lax.fori_loop(0,FQ//128,body,0)
    save=pltpu.make_async_copy(qkv,qkv_out,l_sem)
    @pl.when(item)
    def _():
        arrived(qkv,r_in)
        save.start()
        for a in range(LEN//512):
            sl=pl.ds(a*512,512)
            knt[sl,:]=qkv[1,:,sl].T
    def qloop(qi,_):
        @pl.when(item)
        def _():
            iota=lax.broadcasted_iota(jnp.int32,(FK,FQ),0)
            iotl=lax.broadcasted_iota(jnp.int32,(FK,FQ),1)
            qs=pl.ds(pl.multiple_of(qi*FQ,FQ),FQ)
            q=qkv[0,:,qs]*jnp.bfloat16(0.125)
            st=start[:,qs]
            def step(kj,carry,diag):
                m,l,acc=carry
                ks=pl.ds(pl.multiple_of(kj*FK,FK),FK)
                s=dot(knt[ks,:],q)
                ok=iota>=(st-kj*FK)
                if diag: ok=ok&(iota<=iotl)
                s=jnp.where(ok,s,NEG)
                mn=jnp.maximum(m,jnp.max(s,axis=0,keepdims=True))
                p=jnp.exp(s-mn)
                al=jnp.exp(m-mn)
                l=l*al+jnp.sum(p,axis=0,keepdims=True)
                acc=acc*al+dot(qkv[2,:,ks],p.astype(jnp.bfloat16))
                return mn,l,acc
            carry=(jnp.full((1,FQ),NEG,jnp.float32),jnp.zeros((1,FQ),jnp.float32),jnp.zeros((HD,FQ),jnp.float32))
            carry=lax.fori_loop(0,qi,lambda kj,cr:step(kj,cr,False),carry)
            m,l,acc=step(qi,carry,True)
            o=acc/l
            oT[:,qs]=o
            lse[:,qs]=m+jnp.log(l)
            obf[:,qs]=o.astype(jnp.bfloat16)
            outs(qi,push)
        for at,k in FWD_AT:
            pl.when(qi==at)(functools.partial(run,steps(k)))
        return 0
    lax.fori_loop(0,LEN//FQ,qloop,0)
    run(FWD_THEN)
    loads=[pltpu.make_async_copy(dst[3],wov,w_sem.at[0]),pltpu.make_async_copy(dst[1],wv,w_sem.at[1])]
    for cp in loads: cp.start()
    shares=[o_recv.at[:,pl.ds(0,13)],o_recv.at[:,pl.ds(13,12)]]
    def hand_over(mine):
        arrived(shares[mine],r_out)
        give=pltpu.make_async_remote_copy(src_ref=shares[mine],dst_ref=shares[mine],send_sem=x_sem.at[10],recv_sem=x_sem.at[11],device_id=partner,device_id_type=MESH)
        give.start()
        arrived(shares[1-mine],x_sem.at[11])
        give.wait_send()
    pl.when(c==0)(lambda:hand_over(0))
    pl.when(c==1)(lambda:hand_over(1))
    for s in range(2): of[:,pl.ds(128*s,128)]=o_recv[s].reshape(1600,128).astype(jnp.float32)
    for k in range(ROWS):
        op[k,0:50,:]=of[50*k:50*k+50,:].astype(bf)
        op[k,50:56,:]=jnp.zeros((6,TT),bf)
    loads[0].wait()
    mid[...]=jnp.zeros_like(mid)
    over_blocks(mid,512,op,wov)
    run(FWD_LATE)
    for k in range(7):
        sl=pl.ds(128*k,128)
        mt[sl,:]=mid[:,sl].T+cols[sl,5:6]+xt[sl,:].astype(jnp.float32)
        mid[:,sl]=(mt[sl,:]+cols[sl,6:7]).T
    norm(1,mt[...],cols[:,0:1],cols[:,4:5],norm2t,h2t).wait()
    loads[1].wait()
    over_blocks(pre,640,h2t,wv)
    for a0 in range(0,3200,640):
        p=pre[:,a0:a0+640]
        a_own[:,a0:a0+640]=(p*(0.5*(1.0+jnp.tanh(GC*(p+0.044715*(p*p*p)))))).astype(bf)
    sent=swap(4,a_own,a_other)
    run(FWD_END)
    sent.wait()
    @pl.when(item)
    def _():
        save.wait()
        for qi in range(LEN//FQ): outs(qi,pushed)
    full(pushed); halves(pushed)
BWD_START="e0"
BWD_MID="e1o0c0"
BWD_AT=((0,"e2o1"),(1,"c1e3"),(2,"o2"),(3,"e4c2o3"),(4,"c3"),(5,"e5o4"),(6,"c4e6"),(7,"o5"))
BWD_THEN="e7"
BWD_LAST="q0c5**o6q1c6q2o7--q3c7q4q5++q6q7"
BR=224
KQ=2432
def unpad_rows(dst,v):
    for g in range(16): dst[50*g:50*g+50,:]=v[56*g:56*g+50,:]
def token_sums(v):
    if v.dtype==bf: return lax.dot_general(jnp.ones((8,TT),bf),v,(((1,),(1,)),((),())),preferred_element_type=jnp.float32)[:1]
    v=v[:,:128]+v[:,128:]
    return jnp.concatenate([jnp.sum(v[128*k:128*k+128,:].T,axis=0,keepdims=True) for k in range(v.shape[0]//128)],axis=1)
def back_kernel(names,widths,*refs):
    it=iter(refs)
    take=lambda n:[next(it) for _ in range(n)]
    n=len(names)
    dh2t,norm2t,gt,cols,recips,op,wo,qkv,oT,start,lse,h1t,normt,vec_in,wq=take(15)
    parts=take(n)
    part_o,part_q,gtok,sum_o,sum_q,vec_out=take(6)
    sums=take(n)
    doT,knt,vnt,dqa,delta,dout,dq,stage,wblk,dh_send,dh_recv,do_recv,lhs,nbuf,dh,gmid,gat,dflat,dot_,stat_s,stat_r=take(21)
    vbuf=take(3); vtmp=next(it)
    s_in,s_out,r_in,r_out,q_sem,w_sem,x_sem,l_sem,free=take(9)
    v_sems=take(2)
    chains={}
    for t in range(n):
        b=by_part(take(36))
        if t==0: first_bufs=b
        chains[names[t]]=scatter_steps(names[t],widths[t],parts[t],sums[t],b,take(3))
    chains["o"]=scatter_steps("o",KH,part_o,sum_o,by_part(take(36)),take(3))
    chains["q"]=scatter_steps("q",KQ,part_q,sum_q,narrowed(first_bufs,"q",KQ),take(3))
    def run(which):
        for k in steps(which):
            for f in chains[k[0]][int(k[1])]: f()
    v_go,v_total,v_end=vector_steps(vbuf,v_sems)
    d=lax.axis_index("dev"); r=lax.axis_index("row"); c=lax.axis_index("col")
    partner=(d,r,1-c)
    item=(r<24)|((c==0)&(r<26))
    loads=[pltpu.make_async_copy(s,t,l_sem.at[k]) for k,(s,t) in enumerate(((dh2t,dh),(norm2t,nbuf),(op,lhs),(normt,nbuf),(h1t,lhs)))]
    for cp in loads[:3]: cp.start()
    group_greet(d,r,c,[r+1-2*(r%2),r])
    @pl.when(item)
    def _():
        for a in range(LEN//512):
            sl=pl.ds(a*512,512)
            knt[sl,:]=qkv[1,:,sl].T
            vnt[sl,:]=qkv[2,:,sl].T
        dqa[...]=jnp.zeros_like(dqa)
    stage[...]=jnp.zeros_like(stage)
    vtmp[...]=jnp.zeros_like(vtmp)
    def vec_rows(at,row):
        for k in range(row.shape[1]//128): vtmp[pl.ds(at+k,1),:]=row[:,128*k:128*k+128]
    def norm_back(k,incoming,normed,gain,recip):
        e=incoming*gain
        stat_s[k,0:1,:]=jnp.sum(e,axis=0,keepdims=True)
        stat_s[k,1:2,:]=jnp.sum(e*normed,axis=0,keepdims=True)
        cp=pltpu.make_async_remote_copy(src_ref=stat_s.at[k],dst_ref=stat_r.at[k],send_sem=x_sem.at[2*k],recv_sem=x_sem.at[2*k+1],device_id=partner,device_id_type=MESH)
        cp.start()
        cp.wait()
        s1=stat_s[k,0:1,:]+stat_r[k,0:1,:]
        s2=stat_s[k,1:2,:]+stat_r[k,1:2,:]
        return recip*(e-s1*(1.0/D)-normed*(s2*(1.0/D)))
    group_wait(2)
    run(BWD_START)
    loads[0].wait(); loads[1].wait()
    vec_rows(14,token_sums(dh[...]*nbuf[...]))
    vec_rows(21,token_sums(dh[...]))
    gmid[...]=(gt[...].astype(jnp.float32)+norm_back(0,dh[...],nbuf[...],cols[:,0:1],recips[1:2,:]))*cols[:,2:3]
    gat[...]=gmid[...].astype(bf)
    vec_rows(28,token_sums(gat[...]))
    vec_rows(35,token_sums(gt[...]))
    vec_rows(42,vec_in[...])
    loads[3].start()
    half=lambda w,base,k:w.at[pl.ds(pl.multiple_of(base*KH+BR*k,32),BR)]
    nb=KH//BR
    def pair_product(w,wide,rhs,recv,sem):
        blocks=[half(w,1-c,k) for k in range(nb)]+[half(w,c,k) for k in range(nb)]
        slot=lambda k:wblk.at[k%2,:,pl.ds(0,wide)] if wide<QW else wblk.at[k%2]
        ld=[pltpu.make_async_copy(blocks[k],slot(k),w_sem.at[k%2]) for k in range(2*nb)]
        ld[0].start(); ld[1].start()
        swap=pltpu.make_async_remote_copy(src_ref=dh_send,dst_ref=recv,send_sem=x_sem.at[sem],recv_sem=x_sem.at[sem+1],device_id=partner,device_id_type=MESH)
        for k in range(2*nb):
            ld[k].wait()
            v=dot(wblk[k%2,:,0:rhs.shape[0]],rhs)
            if k<nb: dh_send[pl.ds(BR*k,BR),:]=v.astype(bf)
            else: dh[pl.ds(BR*(k-nb),BR),:]=v
            if k<2*nb-2: ld[k+2].start()
            if k==nb-1: swap.start()
        return swap
    swap=pair_product(wo,KH,gat[...],do_recv,4)
    swap.wait()
    unpad_rows(dflat,dh[...]+do_recv[...].astype(jnp.float32))
    dot_[...]=dflat[...].astype(bf)
    lanes=pl.ds(pl.multiple_of(r*128,128),128)
    def full(fn):
        def body(k,_):
            i=(r+k)%24
            fn(dot_.at[pl.ds(pl.multiple_of(64*(i//2)+32*c,32),64),pl.ds(pl.multiple_of((i%2)*128,128),128)],doT.at[:,lanes],s_in.at[i],r_in,i==r,(d,i,c))
            return 0
        lax.fori_loop(0,24,body,0)
    def halves(fn):
        rows=pl.ds(pl.multiple_of(32*c,32),32)
        for s in range(2):
            fn(dot_.at[pl.ds(pl.multiple_of(768*(1-c),32),32),pl.ds(s*128,128)],doT.at[rows,lanes],s_in.at[24+s],r_in,(r==24+s)&(c==0),(d,24+s,0))
    full(push); halves(push)
    def emit(part,cols_,rhs):
        prev={}
        for b in range(8):
            slot=b%2
            if b>=2: prev[slot].wait()
            stage[slot,:,:,:,0:cols_]=dot_nt(lhs[pl.ds(224*b,224),:],rhs).reshape(2,2,56,cols_).astype(bf)
            src=stage.at[slot] if cols_==2400 else stage.at[slot,:,:,:,pl.ds(0,cols_)]
            prev[slot]=pltpu.make_async_copy(src,part.at[b//2,pl.ds(2*(b%2),2)],q_sem.at[slot])
            prev[slot].start()
        return prev
    loads[2].wait()
    for cp in emit(part_o,KH,gat[...]).values(): cp.wait()
    loads[4].start()
    run(BWD_MID)
    def outs(fn):
        seq=pl.ds(pl.multiple_of((r%2)*128,128),128)
        @pl.when(r<24)
        def _():
            def body(k,_):
                i=(r+k)%ROWS
                fn(dout.at[:,:,pl.ds(pl.multiple_of(i*128,128),128)],dq.at[:,pl.ds(pl.multiple_of(64*(r//2)+32*c,32),64),seq],s_out.at[i],r_out,i==r,(d,i,c))
                return 0
            lax.fori_loop(0,ROWS,body,0)
        @pl.when(r>=24)
        def _():
            def body(k,_):
                rr=(r+k//2)%ROWS; cc=k%2
                fn(dout.at[:,pl.ds(pl.multiple_of(32*cc,32),32),pl.ds(pl.multiple_of(rr*128,128),128)],dq.at[:,pl.ds(pl.multiple_of(768*(1-cc),32),32),seq],s_out.at[2*rr+cc],r_out,(rr==r)&(cc==c),(d,rr,cc))
                return 0
            lax.fori_loop(0,2*ROWS,body,0)
    @pl.when(item)
    def _():
        arrived(doT,r_in)
        for a in range(LEN//512):
            sl=pl.ds(a*512,512)
            delta[:,sl]=jnp.sum(oT[:,sl]*doT[:,sl].astype(jnp.float32),axis=0,keepdims=True)
    def kloop(kj,_):
        @pl.when(item)
        def _():
            iota=lax.broadcasted_iota(jnp.int32,(BK,BQ),0)
            iotl=lax.broadcasted_iota(jnp.int32,(BK,BQ),1)
            ks=pl.ds(pl.multiple_of(kj*BK,BK),BK)
            kn=knt[ks,:]; vn=vnt[ks,:]; kT=qkv[1,:,ks]
            def step(qi,carry,diag):
                dk,dv=carry
                qs=pl.ds(pl.multiple_of(qi*BQ,BQ),BQ)
                q=qkv[0,:,qs]*jnp.bfloat16(0.125)
                do=doT[:,qs]
                s=dot(kn,q)
                ok=iota>=(start[:,qs]-kj*BK)
                if diag: ok=ok&(iota<=iotl)
                p=jnp.exp(jnp.where(ok,s,NEG)-lse[:,qs])
                dp=dot(vn,do)
                ds=(p*(dp-delta[:,qs])).astype(jnp.bfloat16)
                dv=dv+dot_nt(do,p.astype(jnp.bfloat16))
                dk=dk+dot_nt(q,ds)
                dqa[:,qs]+=dot(kT,ds)
                return dk,dv
            z=jnp.zeros((HD,BK),jnp.float32)
            carry=step(kj,(z,z),True)
            dk,dv=lax.fori_loop(kj+1,LEN//BQ,lambda qi,cr:step(qi,cr,False),carry)
            dout[1,:,ks]=dk.astype(jnp.bfloat16)
            dout[2,:,ks]=dv.astype(jnp.bfloat16)
        for step,which in BWD_AT:
            pl.when(kj==step)(functools.partial(run,which))
        return 0
    lax.fori_loop(0,LEN//BK,kloop,0)
    @pl.when(item)
    def _():
        for a in range(LEN//512):
            sl=pl.ds(a*512,512)
            dout[0,:,sl]=(dqa[:,sl]*0.125).astype(jnp.bfloat16)
        outs(push)
    run(BWD_THEN)
    for ax,k in RPEERS: pl.semaphore_signal(free,inc=1,device_id=peer_of(ax,k),device_id_type=MESH)
    arrived(dq,r_out)
    grads=dq[...].reshape(2400,TT)
    loads[4].wait()
    for cp in emit(part_q,2400,grads).values(): cp.wait()
    pl.semaphore_wait(free,len(RPEERS))
    def late_product():
        chains["swap"]=pair_product(wq,QW,grads,dh_recv,6)
    def late_norm():
        chains["swap"].wait()
        dh[...]=dh[...]+dh_recv[...].astype(jnp.float32)
        loads[3].wait()
        vec_rows(0,token_sums(dh[...]*nbuf[...]))
        vec_rows(7,token_sums(dh[...]))
        vec_rows(67,jnp.concatenate((token_sums(grads),jnp.zeros((1,32),jnp.float32)),axis=1))
        v_go(0,vtmp[...])
        gtok[...]=(gmid[...]+norm_back(1,dh[...],nbuf[...],cols[:,1:2],recips[0:1,:])).astype(bf)
        v_go(1,v_total(0))
    def late_vec():
        v_go(2,v_total(1))
    for k in steps(BWD_LAST):
        if k=="**": late_product()
        elif k=="--": late_norm()
        elif k=="++": late_vec()
        else: run(k)
    vec_out[...]=v_total(2)
    v_end()
    pl.when(item)(lambda:outs(pushed))
    full(pushed); halves(pushed)
VM=pl.BlockSpec(memory_space=pltpu.VMEM); ANY=pl.BlockSpec(memory_space=pl.ANY)
bf=jnp.bfloat16
def attend(xt,cols,bias,eb,segs,names,arrs,cid=1):
    S=jax.ShapeDtypeStruct; n=len(names); V=pltpu.VMEM; DM=pltpu.SemaphoreType.DMA; f=jnp.float32
    FH=eb.shape[1]
    out=pl.pallas_call(functools.partial(attn_fwd_kernel,names,[a.shape[1] for a in arrs]),
      out_shape=(S((3,HD,LEN),bf),S((HD,LEN),f),S((1,LEN),f),S((1,LEN),jnp.int32),S((32,56,TT),bf),S((32,56,TT),bf),S((KH,TT),f),S((KH,TT),f),S((8,TT),f),S((32,56,TT),bf),
        S((TT,KH),f),S((TT,FH),f),S((TT,FH),bf),S((TT,FH),bf))+gather_shapes(arrs),
      in_specs=[VM]*5+[ANY]*n,out_specs=(ANY,)+(VM,)*12+(ANY,)+(ANY,)*n,
      scratch_shapes=[V((2,25,HD,128),bf),V((3,HD,LEN),bf),V((LEN,HD),bf),V((HD,LEN),bf),V((4,4,2,56,FH),bf),V((4,4,2,56,KH),bf),V((TT,2400),f),V((3,800,TT),bf),V((1600,TT),f),V((KH,TT),f),
        V((2,8,TT),f),V((2,8,TT),f),DM((26,)),DM((32,)),DM,DM,DM,DM((2,)),DM((12,))]+gather_sems(n),
      compiler_params=pltpu.CompilerParams(collective_id=cid,has_side_effects=True,vmem_limit_bytes=62<<20))(xt,cols,bias,eb,segs,*arrs)
    return out[:4],out[4:14],out[14:]
def attend_back(front,kept,h1t,normt,vec,wq,names,parts,cid=2):
    S=jax.ShapeDtypeStruct; n=len(names); f=jnp.float32; V=pltpu.VMEM; DM=pltpu.SemaphoreType.DMA
    qkv,oT,lse,start=kept
    rows=88
    out=pl.pallas_call(functools.partial(back_kernel,names,[a.shape[4] for a in parts]),
      out_shape=(S((4,4,2,56,KH),bf),S((4,4,2,56,KQ),bf),S((KH,TT),bf),S((50,KH),f),S((50,KQ),f),S((rows,128),f))+tuple(S((50 if a.shape[3]==56 else a.shape[3],a.shape[4]),f) for a in parts),
      in_specs=[ANY,ANY,VM,VM,VM,ANY,ANY,VM,VM,VM,VM,ANY,ANY,VM]+[ANY]*(1+n),out_specs=(ANY,ANY,VM,VM,VM,VM)+(VM,)*n,
      scratch_shapes=[V((HD,LEN),bf),V((LEN,HD),bf),V((LEN,HD),bf),V((HD,LEN),f),V((1,LEN),f),V((3,HD,LEN),bf),
        V((3,800,TT),bf),V((2,2,2,56,KQ),bf),V((2,BR,QW),bf),V((KH,TT),bf),V((KH,TT),bf),V((KH,TT),bf),V((KP,TT),bf),
        V((KH,TT),f),V((KH,TT),f),V((KH,TT),f),V((KH,TT),bf),V((800,TT),f),V((800,TT),bf),V((2,8,TT),f),V((2,8,TT),f)]+[V((4,rows,128),f)]*3+[V((rows,128),f)]+
        [DM((26,)),DM((64,)),DM,DM,DM((2,)),DM((2,)),DM((8,)),DM((5,)),pltpu.SemaphoreType.REGULAR,DM((9,)),DM((9,))]+
        sum([scatter_bufs(nm,*a.shape[3:])+scatter_sems() for nm,a in zip(names,parts)],[])+scatter_bufs("o",56,KH)+scatter_sems()*2,
      compiler_params=pltpu.CompilerParams(collective_id=cid,has_side_effects=True,vmem_limit_bytes=VMEM_BACK))(*front,qkv,oT,start,lse,h1t,normt,vec,wq,*parts)
    return out[2],out[3],out[4],out[5],out[6:]
VMEM_BACK=63<<20


FH=3200; TF=640
def mlp_kernel(h2t,we,wc,pre,a_own,a_other,mid,g,result,part_c,part_e,dh2,dsum,
        wev,wcv,da_send,da_recv,dpre,dh_send,dh_recv,stage_e,stage_c,w_sem,s_sem,r_sem,e_sem,c_sem):
    c=lax.axis_index("col"); other=1-c
    partner=(lax.axis_index("dev"),lax.axis_index("row"),other)
    loads=[pltpu.make_async_copy(wc,wcv,w_sem.at[0]),pltpu.make_async_copy(we,wev,w_sem.at[1])]
    for cp in loads: cp.start()
    bar=pltpu.get_barrier_semaphore()
    pl.semaphore_signal(bar,inc=1,device_id=partner,device_id_type=MESH)
    pl.semaphore_wait(bar,1)
    def swap(i,s,d):
        return pltpu.make_async_remote_copy(src_ref=s,dst_ref=d,send_sem=s_sem.at[i],recv_sem=r_sem.at[i],device_id=partner,device_id_type=MESH)
    x_da,x_dh=swap(0,da_send,da_recv),swap(1,dh_send,dh_recv)
    lanes=lambda k,n:pl.ds(pl.multiple_of(k*n,128),n)
    rows=lambda base,k,n:pl.ds(pl.multiple_of(base+k*n,64),n)
    f32=lambda v:v.astype(jnp.float32)
    NT=FH//TF
    def loop(n,f):
        def body(k,_):
            f(k)
            return 0
        lax.fori_loop(0,n,body,0)
    def emit(i,stage,sem,dst,value):
        slot=i%2
        cp=pltpu.make_async_copy(stage.at[slot],dst,sem.at[slot])
        if i>=2: prev[slot].wait()
        stage[slot]=value
        cp.start(); prev[slot]=cp
    prev={}
    for i in range(2*NT):
        if i==NT:
            loads[0].wait()
            def f(k): da_send[:,lanes(k,TF)]=dot_nt(g[...],wcv[rows(other*FH,k,TF),:]).astype(bf)
            loop(NT,f)
            x_da.start()
        a,b,k=(a_own,c,i) if i<NT else (a_other,other,i-NT)
        emit(i,stage_c,c_sem,part_c.at[rows(b*FH,k,TF)],dot_tn(a[:,k*TF:k*TF+TF],g[...]).astype(bf))
    prev_c=prev
    x_da.wait_recv()
    def f(k):
        sl=lanes(k,TF)
        d=dot_nt(g[...],wcv[rows(c*FH,k,TF),:])+f32(da_recv[:,sl])
        p=pre[:,sl]
        t=jnp.tanh(GC*(p+0.044715*(p*p*p)))
        slope=0.5*(1.0+t)+p*(0.5*(1.0-t*t)*(GC*(1.0+(3*0.044715)*(p*p))))
        dp=(d*slope).astype(bf)
        dpre[:,sl]=dp
        dsum[:,sl]=jnp.sum(f32(dp),axis=0,keepdims=True)
    loop(NT,f)
    loads[1].wait()
    def f(k): dh_send[rows(0,k,448),:]=dot_nt(wev[rows(other*KH,k,448),:],dpre[...]).astype(bf)
    loop(2,f)
    x_dh.start()
    def f(k): dh2[rows(0,k,448),:]=dot_nt(wev[rows(c*KH,k,448),:],dpre[...])
    loop(2,f)
    prev={}
    for j in range(KP//256):
        emit(j,stage_e,e_sem,part_e.at[pl.ds(256*j,256)],dot(h2t[256*j:256*j+256,:],dpre[...]).astype(bf))
    br=dot(a_own[...],wcv[rows(c*FH,0,FH),:])+dot(a_other[...],wcv[rows(other*FH,0,FH),:])
    result[...]=(mid[...]+br).astype(bf)
    x_dh.wait_recv()
    dh2[...]=dh2[...]+f32(dh_recv[...])
    for cp in list(prev.values())+list(prev_c.values()): cp.wait()
    for cp in (x_da,x_dh): cp.wait_send()
def mlp(h2t,we,wc,pre,a_own,a_other,mid,g,cid=4):
    S=jax.ShapeDtypeStruct; f=jnp.float32; V=pltpu.VMEM
    return pl.pallas_call(mlp_kernel,
      out_shape=(S((TT,KH),bf),S((6400,KH),bf),S((KP,FH),bf),S((KH,TT),f),S((1,FH),f)),
      in_specs=[VM,ANY,ANY]+[VM]*5,out_specs=(VM,ANY,ANY,VM,VM),
      scratch_shapes=[V((KP,FH),bf),V((6400,KH),bf)]+[V((TT,FH),bf)]*3+[V((KH,TT),bf)]*2+[V((2,256,FH),bf),V((2,TF,KH),bf)]+[pltpu.SemaphoreType.DMA((n,)) for n in (2,2,2,2,2)],
      compiler_params=pltpu.CompilerParams(collective_id=cid,has_side_effects=True,vmem_limit_bytes=58<<20))(h2t,we,wc,pre,a_own,a_other,mid,g)


def pad_rows(block):
    return jnp.pad(block, ((0, 6), (0, 0)))


def pad_columns(values):
    n = values.shape[0]
    return jnp.pad(values.reshape(n, 16, 50), ((0, 0), (0, 0), (0, 6))).reshape(n, KH)


def unpad_features(values):
    n = values.shape[0]
    return values.reshape(n, 16, 56)[:, :, :50].reshape(n, 800)


def per_device(
    tokens,
    segments,
    first_gain,
    first_bias,
    attention_in,
    attention_bias,
    attention_out,
    output_bias,
    second_gain,
    second_bias,
    expand_weight,
    expand_bias,
    contract_weight,
    contract_bias,
    cotangent,
):
    seqs, block_len, width = tokens.shape
    row_total = seqs * block_len
    grad_low = pad_columns(cotangent.reshape(row_total, width))
    tokens_back = pad_columns(tokens.reshape(row_total, width)).T
    zeros = jnp.zeros_like(first_gain)
    small = jnp.concatenate(
        (second_gain, first_gain, zeros + 1.0, first_bias, second_bias, output_bias, contract_bias, zeros)
    )
    columns = pad_columns(small.reshape(8, width)).T
    bias_three = jnp.concatenate((attention_bias[0], zeros, attention_bias[1]))
    kept, saved, gathered = attend(
        tokens_back,
        columns,
        bias_three[None],
        expand_bias[None],
        segments,
        "qeco",
        (
            jnp.pad(attention_in.reshape(50, 3 * width), ((0, 6), (0, 32))),
            pad_rows(expand_weight),
            pad_columns(contract_weight),
            pad_rows(pad_columns(attention_out)),
        ),
        1,
    )
    rows_attn, rows_one, normed_one, normed_two, recips, rows_two, middle, pre_gelu, gelu_own, gelu_other = saved
    weight_qkv = gathered[0].reshape(KP, QW)
    weight_expand = gathered[1].reshape(KP, 4 * width)
    weight_contract = gathered[2].reshape(4 * D, KH)
    weight_out = gathered[3].reshape(KP, KH)
    result, part_contract, part_expand, grad_two, expand_sums = mlp(
        rows_two.reshape(KP, row_total),
        weight_expand,
        weight_contract,
        pre_gelu,
        gelu_own,
        gelu_other,
        middle,
        grad_low,
        4,
    )
    result = unpad_features(result).reshape(tokens.shape)
    gradient_tokens, sum_out, sum_qkv, vector, (sum_expand, sum_contract) = attend_back(
        (
            grad_two,
            normed_two,
            grad_low.T,
            columns,
            recips,
            rows_attn.reshape(KP, row_total),
            weight_out,
        ),
        kept,
        rows_one.reshape(KP, row_total),
        normed_one,
        expand_sums,
        weight_qkv,
        "ec",
        (
            part_expand.reshape(4, 4, 2, 56, 4 * width),
            part_contract.reshape(4, 4, 2, 200, KH),
        ),
        2,
    )
    gradient_tokens = unpad_features(gradient_tokens.T).reshape(tokens.shape)
    padded = unpad_features(vector[:42].reshape(6, KH)).reshape(-1)
    sums = [padded[width * k : width * (k + 1)] for k in range(6)]
    qkv_sums = vector[67:86].reshape(-1)
    return (
        result,
        gradient_tokens,
        sums[0],
        sums[1],
        sum_qkv[:, : 3 * width].reshape(50, 3, width),
        jnp.concatenate((qkv_sums[:width], qkv_sums[2 * width : 3 * width])).reshape(2, width),
        unpad_features(sum_out),
        sums[4],
        sums[2],
        sums[3],
        sum_expand,
        vector[42:67].reshape(-1),
        unpad_features(sum_contract),
        sums[5],
    )


def solution(mesh):
    return jax.shard_map(
        per_device,
        mesh=mesh,
        in_specs=(
            P("dev", "row", "col"),
            P("dev", None),
            P("col"),
            P("col"),
            P("row", None, "col"),
            P(None, "col"),
            P("row", "col"),
            P("col"),
            P("col"),
            P("col"),
            P("row", "col"),
            P("col"),
            P("row", "col"),
            P("col"),
            P("dev", "row", "col"),
        ),
        out_specs=(
            P("dev", "row", "col"),
            P("dev", "row", "col"),
            P("col"),
            P("col"),
            P("row", None, "col"),
            P(None, "col"),
            P("row", "col"),
            P("col"),
            P("col"),
            P("col"),
            P("row", "col"),
            P("col"),
            P("row", "col"),
            P("col"),
        ),
        check_vma=False,
    )
```
